32 devices in a mesh: gx: 8 (over z, x), gy: 4 (over y, core).
Axes of the slice: x: 2, y: 2, z: 4, core: 2. Of those that a mesh axis runs over, the one named last changes fastest.
Arguments:
- inputs: bfloat16 [16384, 1280], P(('gx', 'gy')), may hold values from -6 to 6
- hidden_pre: bfloat16 [16384, 5120], P(('gx', 'gy')), may hold values from -6 to 6
- cotangent: bfloat16 [16384, 1280], P(('gx', 'gy')), may hold values from -6 to 6
- w_in: float32 [1280, 5120], P('gx'), may hold values from -60 to 60
- m_in: float32 [1280, 5120], P('gx'), may hold values from -30 to 30
- v_in: float32 [1280, 5120], P('gx'), may hold values from 0.2 to 2
- w_out: float32 [5120, 1280], P('gx'), may hold values from -60 to 60
- m_out: float32 [5120, 1280], P('gx'), may hold values from -30 to 30
- v_out: float32 [5120, 1280], P('gx'), may hold values from 0.2 to 2
Outputs:
- new_w_in: float32 [1280, 5120], P('gx')
- new_m_in: float32 [1280, 5120], P('gx')
- new_v_in: float32 [1280, 5120], P('gx')
- new_w_out: float32 [5120, 1280], P('gx')
- new_m_out: float32 [5120, 1280], P('gx')
- new_v_out: float32 [5120, 1280], P('gx')
The draws below stay inside these ranges and needn't reach their ends.
All inputs are finite; a program needn't handle non-finite values.
Results may differ from the reference program's by a relative error of at most 0.02.
Values may be sent and summed in bfloat16 or wider, within the bound.
No kernel may reach another device: no remote copies, remote signals or barrier semaphores. Data moves between devices by JAX's collectives and lax.ppermute only.
A program may use at most 192 MiB of HBM per device.

```python
import math
import jax
import jax.numpy as jnp
from jax import lax

D = 1280
FF = 5120
TOK_DEV = 512
TOKENS = 16384
N_GX = 8
N_GY = 4


def scaled_matrix(key, rows, cols):
    key_base, key_col = jax.random.split(key, 2)
    rising = 1.0 + 29.0 * jnp.arange(rows, dtype=jnp.float32) / (rows - 1)
    columns = jnp.exp(jax.random.uniform(key_col, (1, cols), jnp.float32, 0.0, math.log(10.0)))
    base = jax.random.normal(key_base, (rows, cols), jnp.float32)
    base = jnp.clip(base, -5.0, 5.0)
    return base * rising[:, None] * columns * 0.04


def falling_matrix(key, rows, cols):
    falling = 30.0 - 29.0 * jnp.arange(rows, dtype=jnp.float32) / (rows - 1)
    base = jnp.clip(jax.random.normal(key, (rows, cols), jnp.float32), -3.0, 3.0)
    return base * falling[:, None] * 0.3


def draw_w_in(key, part):
    key = jax.random.fold_in(key, 11)
    return scaled_matrix(key, D, FF)


def draw_w_out(key, part):
    key = jax.random.fold_in(key, 23)
    return scaled_matrix(key, FF, D)


def draw_m_in(key, part):
    key = jax.random.fold_in(key, 37)
    return falling_matrix(key, D, FF)


def draw_m_out(key, part):
    key = jax.random.fold_in(key, 41)
    return falling_matrix(key, FF, D)


def block_scale(stream_key, dims, cuts, smallest, largest):
    gain, own = 1.0, jax.random.fold_in(stream_key, 6)
    for axis_at, blocks in cuts:
        heights = jnp.exp(jax.random.uniform(jax.random.fold_in(own, axis_at), (blocks,), jnp.float32, smallest / len(cuts), largest / len(cuts)))
        gain = gain * jnp.repeat(heights, dims[axis_at] // blocks).reshape([-1 if axis == axis_at else 1 for axis in range(len(dims))])
    return gain


def normal_values(key, shape, width, limit, cuts=(), held_as=jnp.bfloat16):
    array = jax.random.normal(key, shape, jnp.float32) * width
    if len(cuts) > 0:
        array = block_scale(key, shape, cuts, -0.22, 0.18) * array
    return jnp.clip(array, min=-limit, max=limit).astype(held_as)


def setup_inputs(seed: int = 0) -> dict:
    seeds = jax.random.split(jax.random.key(seed), 10)
    return {
        "inputs": normal_values(seeds[0], (TOKENS, D), 1.0, 6.0, ((0, 32),)),
        "hidden_pre": normal_values(seeds[1], (TOKENS, FF), 1.0, 6.0, ((0, 32),)),
        "cotangent": normal_values(seeds[2], (TOKENS, D), 1.0, 6.0, ((0, 32),)),
        "w_in": draw_w_in(jax.random.fold_in(seeds[9], 71), 0),
        "m_in": draw_m_in(jax.random.fold_in(seeds[9], 71), 0),
        "v_in": jnp.clip(jnp.exp(math.log(2.0) - 2.3025851 * jax.random.uniform(seeds[5], (D, FF), jnp.float32) ** block_scale(seeds[5], (D, FF), ((0, 8),), -0.2, 0.2)), 0.2, 2.0),
        "w_out": draw_w_out(jax.random.fold_in(seeds[9], 71), 0),
        "m_out": draw_m_out(jax.random.fold_in(seeds[9], 71), 0),
        "v_out": jnp.clip(jnp.exp(math.log(2.0) - 2.3025851 * jax.random.uniform(seeds[8], (FF, D), jnp.float32) ** block_scale(seeds[8], (FF, D), ((0, 8),), -0.2, 0.2)), 0.2, 2.0),
    }


def gelu_parts(hidden):
    value = hidden.astype(jnp.float32)
    cdf = 0.5 * (1.0 + jax.scipy.special.erf(value / math.sqrt(2.0)))
    pdf = jnp.exp(-0.5 * value * value) / math.sqrt(2.0 * math.pi)
    return (value * cdf, cdf + value * pdf)

def lamb_step(weight, first, second, grad):
    new_first = 0.9 * first + 0.1 * grad
    new_second = 0.95 * second + 0.05 * grad * grad
    update = new_first / (jnp.sqrt(new_second) + 1e-06) + 0.05 * weight
    ratio = jnp.sqrt(jnp.sum(weight * weight)) / jnp.sqrt(jnp.sum(update * update))
    return (weight - 0.4 * ratio * update, new_first, new_second)

def reference(inputs, hidden_pre, cotangent, w_in, m_in, v_in, w_out, m_out, v_out):
    count = N_GX * N_GY
    scale_in = 1.0 / math.sqrt(D)
    scale_out = 1.0 / math.sqrt(FF)
    w_half = w_out.astype(jnp.bfloat16)
    blocks = (inputs.reshape(count, TOK_DEV, D), hidden_pre.reshape(count, TOK_DEV, FF), cotangent.reshape(count, TOK_DEV, D))

    def one_device(carry, parts):
        tokens, hidden, upstream = parts
        act, slope = gelu_parts(hidden)
        act = act.astype(jnp.bfloat16)
        grad_act = lax.dot_general(upstream, w_half, (((1,), (1,)), ((), ())), preferred_element_type=jnp.float32) * scale_out
        grad_pre = (grad_act * slope).astype(jnp.bfloat16)
        term_in = lax.dot_general(tokens, grad_pre, (((0,), (0,)), ((), ())), preferred_element_type=jnp.float32) * scale_in
        term_out = lax.dot_general(act, upstream, (((0,), (0,)), ((), ())), preferred_element_type=jnp.float32) * scale_out
        term_in = lax.optimization_barrier(term_in.astype(jnp.bfloat16)).astype(jnp.float32)
        term_out = lax.optimization_barrier(term_out.astype(jnp.bfloat16)).astype(jnp.float32)
        return ((carry[0] + term_in, carry[1] + term_out), None)
    start = (jnp.zeros((D, FF), jnp.float32), jnp.zeros((FF, D), jnp.float32))
    (grad_in, grad_out), _ = lax.scan(one_device, start, blocks)
    new_w_in, new_m_in, new_v_in = lamb_step(w_in, m_in, v_in, grad_in)
    new_w_out, new_m_out, new_v_out = lamb_step(w_out, m_out, v_out, grad_out)
    return (new_w_in, new_m_in, new_v_in, new_w_out, new_m_out, new_v_out)
```

```python
import functools
import math

import jax
import jax.numpy as jnp
from jax import lax
from jax.experimental import pallas as pl
from jax.experimental.pallas import tpu as pltpu
from jax.sharding import PartitionSpec as P

BF16 = jnp.bfloat16
F32 = jnp.float32
CORES = 2
CHIPS_Z = 4
LANES = 128
VMEM = 56 * 1024 * 1024


def moments(weight, first, second, grad):
    new_first = 0.9 * first + 0.1 * grad
    new_second = 0.95 * second + 0.05 * grad * grad
    update = new_first / (jnp.sqrt(new_second) + 1e-06) + 0.05 * weight
    return (new_first, new_second, update)


def squares(value):
    return jnp.sum(value * value)


def gelu(value):
    return 0.5 * value * (1.0 + lax.erf(value * (1.0 / math.sqrt(2.0))))


def gelu_slope(value):
    cdf = 0.5 * (1.0 + lax.erf(value * (1.0 / math.sqrt(2.0))))
    return cdf + value * (jnp.exp(-0.5 * value * value) * (1.0 / math.sqrt(2.0 * math.pi)))


def widths(shard):
    if shard % LANES:
        return (shard,)
    tiles = shard // LANES
    cut = []
    while tiles > 2:
        cut.append(2 * LANES)
        tiles -= 2
    return tuple(cut + [tiles * LANES])


def dot(left, right, dims):
    return lax.dot_general(left, right, (dims, ((), ())), preferred_element_type=F32)


def params(flops, nbytes, transcendentals=0):
    return dict(
        compiler_params=pltpu.CompilerParams(vmem_limit_bytes=VMEM),
        cost_estimate=pl.CostEstimate(
            flops=int(flops), bytes_accessed=int(nbytes), transcendentals=int(transcendentals)
        ),
    )


def take_columns(hidden, at, nz, nx, cuts):
    tokens, hidden_width = hidden.shape
    shard = hidden_width // (nz * nx)
    if shard % LANES:
        parts = [
            lax.dynamic_slice_in_dim(hidden, (z * nx + at) * shard, shard, 1).T for z in range(nz)
        ]
        whole = jnp.stack(parts)
        starts = [sum(cuts[:k]) for k in range(len(cuts))]
        return [whole[:, s : s + w] for s, w in zip(starts, cuts)]

    def body(at_ref, h_ref, *out_refs):
        start = 0
        for width, out_ref in zip(cuts, out_refs):
            part = h_ref[:, start : start + width]
            out_ref[0] = part.T
            start += width

    return pl.pallas_call(
        body,
        grid_spec=pltpu.PrefetchScalarGridSpec(
            num_scalar_prefetch=1,
            grid=(nz,),
            in_specs=[pl.BlockSpec((tokens, shard), lambda z, a: (0, z * nx + a[0]))],
            out_specs=[pl.BlockSpec((1, w, tokens), lambda z, a: (z, 0, 0)) for w in cuts],
        ),
        out_shape=[jax.ShapeDtypeStruct((nz, w, tokens), BF16) for w in cuts],
        **params(0, 4 * tokens * shard * nz),
    )(jnp.reshape(at, (1,)).astype(jnp.int32), hidden)


def grad_out_chunk(hiddens, cots, core, scale):
    nz, width, tokens = hiddens[0].shape
    model = cots[0].shape[1]
    half = model // CORES
    count = len(hiddens)

    def body(c_ref, *refs):
        h_refs, cot_refs = refs[:count], refs[count : 2 * count]
        send_ref, keep_ref = refs[2 * count :]
        acts = [gelu(h[0].astype(F32)).astype(BF16) for h in h_refs]
        for out_ref, which in ((send_ref, 1 - c_ref[0]), (keep_ref, c_ref[0])):
            cols = pl.ds(pl.multiple_of(which * half, LANES), half)
            total = sum(dot(a, cot[:, cols], ((1,), (0,))) for a, cot in zip(acts, cot_refs))
            out_ref[0] = (total * scale).astype(BF16)

    return pl.pallas_call(
        body,
        grid_spec=pltpu.PrefetchScalarGridSpec(
            num_scalar_prefetch=1,
            grid=(nz,),
            in_specs=[pl.BlockSpec((1, width, tokens), lambda z, c: (z, 0, 0))] * count
            + [pl.BlockSpec((tokens, model), lambda z, c: (0, 0))] * count,
            out_specs=[pl.BlockSpec((1, width, half), lambda z, c: (z, 0, 0))] * 2,
        ),
        out_shape=[jax.ShapeDtypeStruct((nz, width, half), BF16)] * 2,
        **params(
            2 * nz * width * tokens * model * count,
            2 * (nz * width * tokens * count + tokens * model * count + nz * width * model),
            nz * width * tokens * count,
        ),
    )(core, *hiddens, *cots)


def grad_pre_chunk(hiddens, cots, weights, row, zed, scale):
    nz, width, tokens = hiddens[0].shape
    shard, model = weights.shape[1:]
    count = len(hiddens)

    def body(z_ref, *refs):
        h_refs, cot_refs = refs[:count], refs[count : 2 * count]
        w_ref = refs[2 * count]
        out_refs = refs[2 * count + 1 :]
        w = w_ref[0, row : row + width, :]
        for h, cot, out_ref in zip(h_refs, cot_refs, out_refs):
            grad_act = dot(w, cot[...], ((1,), (1,))) * scale
            out_ref[0] = (grad_act * gelu_slope(h[0].astype(F32))).astype(BF16)

    return pl.pallas_call(
        body,
        grid_spec=pltpu.PrefetchScalarGridSpec(
            num_scalar_prefetch=1,
            grid=(nz,),
            in_specs=[pl.BlockSpec((1, width, tokens), lambda z, m: (z, 0, 0))] * count
            + [pl.BlockSpec((tokens, model), lambda z, m: (0, 0))] * count
            + [pl.BlockSpec((1, shard, model), lambda z, m: (z ^ m[0], 0, 0))],
            out_specs=[pl.BlockSpec((1, width, tokens), lambda z, m: (z, 0, 0))] * count,
        ),
        out_shape=[jax.ShapeDtypeStruct((nz, width, tokens), BF16)] * count,
        **params(
            2 * nz * width * tokens * model * count,
            2 * (2 * nz * width * tokens * count + tokens * model * count + nz * shard * model),
            2 * nz * width * tokens * count,
        ),
    )(zed, *hiddens, *cots, weights)


def grad_in_half(grads, inputs, which, scale):
    nz, width, tokens = grads[0].shape
    model = inputs[0].shape[0]
    count = len(grads)
    half = nz // CORES

    def body(c_ref, *refs):
        g_refs, in_refs, out_ref = refs[:count], refs[count : 2 * count], refs[2 * count]
        total = sum(dot(i[...], g[0], ((1,), (1,))) for i, g in zip(in_refs, g_refs))
        out_ref[0] = (total * scale).astype(BF16)

    return pl.pallas_call(
        body,
        grid_spec=pltpu.PrefetchScalarGridSpec(
            num_scalar_prefetch=1,
            grid=(half,),
            in_specs=[pl.BlockSpec((1, width, tokens), lambda z, c: (c[0] * half + z, 0, 0))] * count
            + [pl.BlockSpec((model, tokens), lambda z, c: (0, 0))] * count,
            out_specs=pl.BlockSpec((1, model, width), lambda z, c: (z, 0, 0)),
        ),
        out_shape=jax.ShapeDtypeStruct((half, model, width), BF16),
        **params(
            2 * half * width * tokens * model * count,
            2 * (half * width * tokens * count + tokens * model * count + half * width * model),
        ),
    )(which, *grads, *inputs)


def plan(nz, nx, ny):
    def along_x(value, step):
        pairs = [
            (z * nx + x, z * nx + (x + step) % nx) for z in range(nz) for x in range(nx)
        ]
        return lax.ppermute(value, "gx", pairs)

    def along_z(value, flip):
        pairs = [(z * nx + x, (z ^ flip) * nx + x) for z in range(nz) for x in range(nx)]
        return lax.ppermute(value, "gx", pairs)

    def along_y(value, step):
        pairs = [
            (y * CORES + c, (y + step) % ny * CORES + c) for y in range(ny) for c in range(CORES)
        ]
        return lax.ppermute(value, "gy", pairs)

    def across(value):
        pairs = [(k, k ^ 1) for k in range(ny * CORES)]
        return lax.ppermute(value, "gy", pairs)

    def ordered(pieces, place, size):
        if size == 2:
            first = jnp.where(place == 0, pieces[0], pieces[1])
            second = jnp.where(place == 0, pieces[1], pieces[0])
            return jnp.stack([first, second])
        stacked = jnp.stack(pieces)
        return jnp.take(stacked, (place - jnp.arange(size)) % size, axis=0)

    def pick(value, at, axis):
        return lax.dynamic_index_in_dim(value, at, axis, keepdims=False)

    def local(inputs, hidden_pre, cotangent, w_in, m_in, v_in, w_out, m_out, v_out):
        model = inputs.shape[1]
        hidden_width = hidden_pre.shape[1]
        shard = hidden_width // (nz * nx)
        rows = model // (nz * nx)
        cuts = widths(shard)
        starts = [sum(cuts[:k]) for k in range(len(cuts))]
        scale_in = 1.0 / math.sqrt(model)
        scale_out = 1.0 / math.sqrt(hidden_width)
        place = lax.axis_index("gx")
        side = lax.axis_index("gy")
        z, x = place // nx, place % nx
        y, c = side // CORES, side % CORES
        scalar = lambda value: jnp.reshape(value, (1,)).astype(jnp.int32)

        cots = [cotangent] + [along_x(cotangent, s) for s in range(1, nx)]
        sends = [take_columns(hidden_pre, (x + s) % nx, nz, nx, cuts) for s in range(1, nx)]
        own = take_columns(hidden_pre, x, nz, nx, cuts)
        hiddens = [
            [own[k]] + [along_x(sends[s - 1][k], s) for s in range(1, nx)]
            for k in range(len(cuts))
        ]
        flipped = inputs.T
        columns = [flipped] + [along_x(flipped, s) for s in range(1, nx)]

        part = lax.dynamic_slice_in_dim(w_out, c * (shard // CORES), shard // CORES, 0).astype(BF16)
        rel = [part]
        bit = nz // 2
        found = {0: part}
        while bit:
            for key in list(found):
                found[key ^ bit] = along_z(found[key], bit)
            bit //= 2
        both = []
        for key in range(nz):
            mine, other = found[key], across(found[key])
            both.append(jnp.concatenate([jnp.where(c == 0, mine, other), jnp.where(c == 0, other, mine)]))
        weights = jnp.stack(both)

        def reduce_y(mine, axis):
            total = pick(mine, y, axis)
            for s in range(1, ny):
                total = total + along_y(pick(mine, (y + s) % ny, axis).astype(BF16), s).astype(F32)
            return total

        def reduce_z(mine, axis):
            bit, left = 1, nz
            while left > 1:
                here = (z // bit) % 2
                shape = mine.shape[:axis] + (left // 2, 2) + mine.shape[axis + 1 :]
                pairs = mine.reshape(shape)
                send = pick(pairs, 1 - here, axis + 1).astype(BF16)
                mine = pick(pairs, here, axis + 1) + along_z(send, bit).astype(F32)
                left //= 2
                bit *= 2
            return pick(mine, 0, axis)

        def share_y(value):
            return ordered([value] + [along_y(value, s) for s in range(1, ny)], y, ny)

        def share_c(value):
            return ordered([value, across(value)], c, 2)

        outs = []
        for k, width in enumerate(cuts):
            send, keep = grad_out_chunk(hiddens[k], cots, scalar(c), scale_out)
            mine = keep.astype(F32) + across(send).astype(F32)
            mine = mine.reshape(nz, ny, width // ny, model // CORES)
            mine = reduce_z(reduce_y(mine, 1), 0).astype(BF16)
            mine = share_y(mine).reshape(width, model // CORES)
            mine = share_c(mine)
            outs.append(jnp.concatenate([mine[0], mine[1]], axis=1))
        grad_out = jnp.concatenate(outs, axis=0).astype(F32)

        pres = [
            grad_pre_chunk(hiddens[k], cots, weights, starts[k], scalar(z), scale_out)
            for k in range(len(cuts))
        ]
        ins = []
        for k, width in enumerate(cuts):
            send = grad_in_half(pres[k], columns, scalar(1 - c), scale_in)
            keep = grad_in_half(pres[k], columns, scalar(c), scale_in)
            mine = keep.astype(F32) + across(send).astype(F32)
            mine = mine.reshape(nz // CORES, nz, nx, ny, rows // ny, width)
            mine = reduce_z(reduce_y(mine, 3), 1).astype(BF16)
            got = [pick(mine, x, 1)] + [along_x(pick(mine, (x + s) % nx, 1), s) for s in range(1, nx)]
            mine = ordered(got, x, nx)
            mine = share_c(share_y(mine))
            ins.append(mine)
        joined = jnp.concatenate(ins, axis=-1)
        grad_in = joined.transpose(1, 4, 0, 3, 2, 5).reshape(rows, hidden_width).astype(F32)

        first_in, second_in, update_in = moments(w_in, m_in, v_in, grad_in)
        first_out, second_out, update_out = moments(w_out, m_out, v_out, grad_out)
        norm_w_in, norm_w_out, norm_u_in, norm_u_out = lax.psum(
            (squares(w_in), squares(w_out), squares(update_in), squares(update_out)), "gx"
        )
        ratio_in = jnp.sqrt(norm_w_in) / jnp.sqrt(norm_u_in)
        ratio_out = jnp.sqrt(norm_w_out) / jnp.sqrt(norm_u_out)
        return (
            w_in - 0.4 * ratio_in * update_in,
            first_in,
            second_in,
            w_out - 0.4 * ratio_out * update_out,
            first_out,
            second_out,
        )

    return local


def solution(mesh):
    gx, gy = mesh.shape["gx"], mesh.shape["gy"]
    nz = CHIPS_Z
    state = P("gx", None)
    tokens = P(("gx", "gy"), None)
    return jax.shard_map(
        plan(nz, gx // nz, gy // CORES),
        mesh=mesh,
        in_specs=(tokens,) * 3 + (state,) * 6,
        out_specs=(state,) * 6,
        check_vma=False,
    )
```

```python
import functools
import math

import jax
import jax.numpy as jnp
from jax import lax
from jax.experimental import pallas as pl
from jax.experimental.pallas import tpu as pltpu
from jax.sharding import PartitionSpec as P

BF16 = jnp.bfloat16
F32 = jnp.float32
CORES = 2
CHIPS_Z = 4
LANES = 128
VMEM = 32 * 1024 * 1024


def moments(weight, first, second, grad):
    new_first = 0.9 * first + 0.1 * grad
    new_second = 0.95 * second + 0.05 * grad * grad
    update = new_first / (jnp.sqrt(new_second) + 1e-06) + 0.05 * weight
    return (new_first, new_second, update)


def squares(value):
    return jnp.sum(value * value)


def gelu(value):
    return 0.5 * value * (1.0 + lax.erf(value * (1.0 / math.sqrt(2.0))))


def gelu_slope(value):
    cdf = 0.5 * (1.0 + lax.erf(value * (1.0 / math.sqrt(2.0))))
    return cdf + value * (jnp.exp(-0.5 * value * value) * (1.0 / math.sqrt(2.0 * math.pi)))


def widths(shard):
    if shard % LANES:
        return (shard,)
    tiles = shard // LANES
    cut = []
    while tiles > 2:
        cut.append(2 * LANES)
        tiles -= 2
    return tuple(cut + [tiles * LANES])


def dot(left, right, dims):
    return lax.dot_general(left, right, (dims, ((), ())), preferred_element_type=F32)


def params():
    return dict(
        compiler_params=pltpu.CompilerParams(vmem_limit_bytes=VMEM),
        cost_estimate=pl.CostEstimate(flops=1, bytes_accessed=1, transcendentals=0),
    )


def take_columns(hidden, at, nz, nx, cuts):
    tokens, hidden_width = hidden.shape
    shard = hidden_width // (nz * nx)
    if shard % LANES:
        parts = [
            lax.dynamic_slice_in_dim(hidden, (z * nx + at) * shard, shard, 1).T for z in range(nz)
        ]
        whole = jnp.stack(parts)
        starts = [sum(cuts[:k]) for k in range(len(cuts))]
        return [whole[:, s : s + w] for s, w in zip(starts, cuts)]

    def body(at_ref, h_ref, *out_refs):
        start = 0
        for width, out_ref in zip(cuts, out_refs):
            part = h_ref[:, start : start + width]
            out_ref[0] = part.T
            start += width

    return pl.pallas_call(
        body,
        grid_spec=pltpu.PrefetchScalarGridSpec(
            num_scalar_prefetch=1,
            grid=(nz,),
            in_specs=[pl.BlockSpec((tokens, shard), lambda z, a: (0, z * nx + a[0]))],
            out_specs=[pl.BlockSpec((1, w, tokens), lambda z, a: (z, 0, 0)) for w in cuts],
        ),
        out_shape=[jax.ShapeDtypeStruct((nz, w, tokens), BF16) for w in cuts],
        **params(),
    )(jnp.reshape(at, (1,)).astype(jnp.int32), hidden)


def grad_out_chunk(hiddens, cots, core, scale):
    nz, width, tokens = hiddens[0].shape
    model = cots[0].shape[1]
    half = model // CORES
    count = len(hiddens)

    def body(c_ref, *refs):
        h_refs, cot_refs = refs[:count], refs[count : 2 * count]
        send_ref, keep_ref = refs[2 * count :]
        acts = [gelu(h[0].astype(F32)).astype(BF16) for h in h_refs]
        for out_ref, which in ((send_ref, 1 - c_ref[0]), (keep_ref, c_ref[0])):
            cols = pl.ds(pl.multiple_of(which * half, LANES), half)
            total = sum(dot(a, cot[:, cols], ((1,), (0,))) for a, cot in zip(acts, cot_refs))
            out_ref[0] = (total * scale).astype(BF16)

    return pl.pallas_call(
        body,
        grid_spec=pltpu.PrefetchScalarGridSpec(
            num_scalar_prefetch=1,
            grid=(nz,),
            in_specs=[pl.BlockSpec((1, width, tokens), lambda z, c: (z, 0, 0))] * count
            + [pl.BlockSpec((tokens, model), lambda z, c: (0, 0))] * count,
            out_specs=[pl.BlockSpec((1, width, half), lambda z, c: (z, 0, 0))] * 2,
        ),
        out_shape=[jax.ShapeDtypeStruct((nz, width, half), BF16)] * 2,
        **params(),
    )(core, *hiddens, *cots)


def grad_pre_chunk(hiddens, cots, mine, other, row, core, scale):
    nz, width, tokens = hiddens[0].shape
    part, model = mine.shape[1:]
    count = len(hiddens)

    def body(c_ref, *refs):
        h_refs, cot_refs = refs[:count], refs[count : 2 * count]
        mine_ref, other_ref = refs[2 * count : 2 * count + 2]
        out_refs, w_ref = refs[2 * count + 2 : -1], refs[-1]
        for at, ref in ((c_ref[0], mine_ref), (1 - c_ref[0], other_ref)):
            w_ref[pl.ds(pl.multiple_of(at * part, 16), part), :] = ref[0]
        w = w_ref[row : row + width, :]
        for h, cot, out_ref in zip(h_refs, cot_refs, out_refs):
            grad_act = dot(w, cot[...], ((1,), (1,))) * scale
            out_ref[0] = (grad_act * gelu_slope(h[0].astype(F32))).astype(BF16)

    return pl.pallas_call(
        body,
        grid_spec=pltpu.PrefetchScalarGridSpec(
            num_scalar_prefetch=1,
            grid=(nz,),
            in_specs=[pl.BlockSpec((1, width, tokens), lambda z, c: (z, 0, 0))] * count
            + [pl.BlockSpec((tokens, model), lambda z, c: (0, 0))] * count
            + [pl.BlockSpec((1, part, model), lambda z, c: (z, 0, 0))] * CORES,
            out_specs=[pl.BlockSpec((1, width, tokens), lambda z, c: (z, 0, 0))] * count,
            scratch_shapes=[pltpu.VMEM((CORES * part, model), BF16)],
        ),
        out_shape=[jax.ShapeDtypeStruct((nz, width, tokens), BF16)] * count,
        **params(),
    )(core, *hiddens, *cots, mine, other)


def grad_in_chunk(grads, inputs, core, scale):
    nz, width, tokens = grads[0].shape
    model = inputs[0].shape[0]
    count = len(grads)
    half = nz // CORES

    def body(c_ref, *refs):
        g_refs, in_refs = refs[:count], refs[count : 2 * count]
        send_ref, keep_ref = refs[2 * count :]
        left = jnp.concatenate([i[...] for i in in_refs], axis=1)
        right = jnp.concatenate([g[0] for g in g_refs], axis=1)
        total = (dot(left, right, ((1,), (1,))) * scale).astype(BF16)
        step = pl.program_id(0)

        @pl.when(step < half)
        def _():
            send_ref[0] = total

        @pl.when(step >= half)
        def _():
            keep_ref[0] = total

    def shard_at(step, c):
        return ((c[0] + 1 + step // half) % CORES * half + step % half, 0, 0)

    return pl.pallas_call(
        body,
        grid_spec=pltpu.PrefetchScalarGridSpec(
            num_scalar_prefetch=1,
            grid=(nz,),
            in_specs=[pl.BlockSpec((1, width, tokens), shard_at)] * count
            + [pl.BlockSpec((model, tokens), lambda z, c: (0, 0))] * count,
            out_specs=[
                pl.BlockSpec((1, model, width), lambda z, c: (jnp.minimum(z, half - 1), 0, 0)),
                pl.BlockSpec((1, model, width), lambda z, c: (jnp.maximum(z - half, 0), 0, 0)),
            ],
        ),
        out_shape=[jax.ShapeDtypeStruct((half, model, width), BF16)] * 2,
        **params(),
    )(core, *grads, *inputs)


def transposed(value):
    rows, cols = value.shape
    wide = 2 * LANES

    def body(in_ref, out_ref):
        out_ref[...] = in_ref[...].T

    return pl.pallas_call(
        body,
        grid=(cols // wide,),
        in_specs=[pl.BlockSpec((rows, wide), lambda n: (0, n))],
        out_specs=pl.BlockSpec((wide, rows), lambda n: (n, 0)),
        out_shape=jax.ShapeDtypeStruct((cols, rows), value.dtype),
        **params(),
    )(value)


def half_rows(weight, core):
    rows, cols = weight.shape
    part = rows // CORES
    wide = 2 * LANES

    def body(c_ref, in_ref, out_ref):
        out_ref[...] = in_ref[...].astype(BF16)

    return pl.pallas_call(
        body,
        grid_spec=pltpu.PrefetchScalarGridSpec(
            num_scalar_prefetch=1,
            grid=(cols // wide,),
            in_specs=[pl.BlockSpec((part, wide), lambda n, c: (c[0], n))],
            out_specs=pl.BlockSpec((part, wide), lambda n, c: (0, n)),
        ),
        out_shape=jax.ShapeDtypeStruct((part, cols), BF16),
        **params(),
    )(core, weight)


def stack(pieces, places):
    count = len(pieces)
    shape = pieces[0].shape

    def body(at_ref, *refs):
        for n in range(count):
            refs[count][at_ref[n]] = refs[n][...]

    whole = lambda at: (0,) * len(shape)
    return pl.pallas_call(
        body,
        grid_spec=pltpu.PrefetchScalarGridSpec(
            num_scalar_prefetch=1,
            grid=(),
            in_specs=[pl.BlockSpec(shape, whole)] * count,
            out_specs=pl.BlockSpec((count, *shape), lambda at: (0,) * (1 + len(shape))),
        ),
        out_shape=jax.ShapeDtypeStruct((count, *shape), pieces[0].dtype),
        **params(),
    )(places, *pieces)


def add_tiles(tiles):
    def body(*refs):
        refs[-1][...] = sum(ref[...] for ref in refs[:-1])

    return pl.pallas_call(
        body, out_shape=jax.ShapeDtypeStruct(tiles[0].shape, F32), **params()
    )(*tiles)


def reduce_step(place, keep, cross, from_y, from_z, shift, stage, ny, split):
    lead, nz, mid, _, high, wide = keep.shape
    bit = len(from_z)

    def zed(n, at):
        if stage == "y":
            return n
        if stage == "end":
            return at[2]
        low = at[2] % (1 << bit)
        mine = (at[2] // (1 << bit)) % 2
        return n * (2 << bit) + (1 - mine) * (1 << bit) + low

    count = {"y": nz, "z": nz >> (bit + 1), "end": 1}[stage]
    six = (lead, 1, mid, 1, high, wide)
    five = (lead, 1, mid, high, wide)
    specs = [pl.BlockSpec(six, lambda n, at: (0, zed(n, at), 0, (at[1] + shift) % ny, 0, 0))] * 2
    specs += [pl.BlockSpec(five, lambda n, at: (0, zed(n, at), 0, 0, 0))] * len(from_y)
    specs += [
        pl.BlockSpec(five, lambda n, at, j=j: (0, zed(n, at) // (2 << j), 0, 0, 0)) for j in range(bit)
    ]

    def body(at_ref, *refs):
        ins = refs[: len(specs)]
        outs = refs[len(specs) :]
        for p in range(lead):
            for m in range(mid):
                total = ins[0][p, 0, m, 0].astype(F32) + ins[1][p, 0, m, 0].astype(F32)
                for ref in ins[2:]:
                    total = total + ref[p, 0, m].astype(F32)
                total = total.astype(BF16)
                if not split:
                    outs[0][p, 0, m] = total
                    continue
                for s in range(mid):

                    @pl.when((at_ref[0] + s) % mid == m)
                    def _(s=s, total=total):
                        outs[s][p] = total

    if split:
        out_specs = [pl.BlockSpec((lead, high, wide), lambda n, at: (0, 0, 0))] * mid
        out_shape = [jax.ShapeDtypeStruct((lead, high, wide), BF16)] * mid
    else:
        out_specs = [pl.BlockSpec(five, lambda n, at: (0, n, 0, 0, 0))]
        out_shape = [jax.ShapeDtypeStruct((lead, count, mid, high, wide), BF16)]
    out = pl.pallas_call(
        body,
        grid_spec=pltpu.PrefetchScalarGridSpec(
            num_scalar_prefetch=1, grid=(count,), in_specs=specs, out_specs=out_specs
        ),
        out_shape=out_shape,
        **params(),
    )(place, keep, cross, *from_y, *from_z)
    return out if split else out[0]


def moments_kernel(core, weight, first, second, mine, other, grid, state_spec, grad_specs, owner, axis):
    block = state_spec.block_shape
    count = len(mine)

    def body(c_ref, w_ref, m_ref, v_ref, *refs):
        mine_refs, other_refs = refs[:count], refs[count : 2 * count]
        new_m_ref, new_v_ref, u_ref, sum_ref = refs[2 * count :]
        totals = [jnp.zeros((8, LANES), F32)] * 2
        start = 0
        ours = owner(pl.program_id(0)) == c_ref[0]
        for mine_ref, other_ref in zip(mine_refs, other_refs):
            size = mine_ref.size // block[1 - axis]
            shape = (size, block[1]) if axis == 0 else (block[0], size)
            at = (slice(start, start + size), slice(None))
            at = at if axis == 0 else at[::-1]
            grad = jnp.where(ours, mine_ref[...].reshape(shape), other_ref[...].reshape(shape)).astype(F32)
            weight = w_ref[at]
            new_m, new_v, update = moments(weight, m_ref[at], v_ref[at], grad)
            new_m_ref[at] = new_m
            new_v_ref[at] = new_v
            u_ref[at] = update
            for n, value in enumerate((weight, update)):
                square = value * value
                for col in range(0, shape[1], LANES):
                    totals[n] = totals[n] + square[:, col : col + LANES].reshape(-1, 8, LANES).sum(0)
            start += size

        @pl.when(pl.program_id(0) == 0)
        def _():
            sum_ref[...] = jnp.zeros_like(sum_ref)

        sum_ref[:8] += totals[0]
        sum_ref[8:] += totals[1]

    state = jax.ShapeDtypeStruct(weight.shape, F32)
    return pl.pallas_call(
        body,
        grid_spec=pltpu.PrefetchScalarGridSpec(
            num_scalar_prefetch=1,
            grid=grid,
            in_specs=[state_spec] * 3 + grad_specs * 2,
            out_specs=[state_spec] * 3 + [pl.BlockSpec((16, LANES), lambda n, c: (0, 0))],
        ),
        out_shape=[state] * 3 + [jax.ShapeDtypeStruct((16, LANES), F32)],
        **params(),
    )(core, weight, first, second, *mine, *other)


def step_weights(weight, update, tiles):
    rows, cols = weight.shape
    high = rows // 5
    count = len(tiles)

    def body(w_ref, u_ref, *refs):
        sums = sum(ref[...] for ref in refs[:count])
        ratio = jnp.sqrt(jnp.sum(sums[:8], keepdims=True)) / jnp.sqrt(jnp.sum(sums[8:], keepdims=True))
        refs[count][...] = w_ref[...] - 0.4 * ratio * u_ref[...]

    spec = pl.BlockSpec((high, cols), lambda n: (n, 0))
    tile = pl.BlockSpec((16, LANES), lambda n: (0, 0))
    return pl.pallas_call(
        body,
        grid=(rows // high,),
        in_specs=[spec] * 2 + [tile] * count,
        out_specs=spec,
        out_shape=jax.ShapeDtypeStruct(weight.shape, F32),
        **params(),
    )(weight, update, *tiles)


class Order:
    def __init__(self):
        self.last = None

    def after(self, *values):
        if self.last is None:
            return values
        return lax.optimization_barrier((*values, self.last))[:-1]

    def did(self, value):
        self.last = value


def plan(nz, nx, ny):
    def along_x(value, step):
        pairs = [
            (z * nx + x, z * nx + (x + step) % nx) for z in range(nz) for x in range(nx)
        ]
        return lax.ppermute(value, "gx", pairs)

    def along_z(value, flip):
        pairs = [(z * nx + x, (z ^ flip) * nx + x) for z in range(nz) for x in range(nx)]
        return lax.ppermute(value, "gx", pairs)

    def along_y(value, step):
        pairs = [
            (y * CORES + c, (y + step) % ny * CORES + c) for y in range(ny) for c in range(CORES)
        ]
        return lax.ppermute(value, "gy", pairs)

    def across(value):
        pairs = [(k, k ^ 1) for k in range(ny * CORES)]
        return lax.ppermute(value, "gy", pairs)

    class Reduce:
        def __init__(self, order, at, send, keep, shape):
            self.order, self.at, self.place = order, at, jnp.stack(at).astype(jnp.int32)
            self.keep = keep.reshape(shape)
            self.cross = across(send).reshape(shape)
            self.from_y = []
            self.from_z = []

        def step(self, shift, stage, split=False):
            count = len(self.from_y)
            got = self.order.after(self.keep, self.cross, *self.from_y, *self.from_z)
            out = reduce_step(
                self.place, got[0], got[1], got[2 : 2 + count], got[2 + count :], shift, stage, ny, split
            )
            self.order.did(out[0] if split else out)
            return out

        def send_y(self):
            from_y = []
            for s in range(1, ny):
                from_y.append(along_y(self.step(s, "y"), s))
            self.from_y = from_y

        def send_z(self):
            bit = len(self.from_z)
            self.from_z.append(along_z(self.step(0, "z"), 1 << bit))

        def finish(self):
            out = self.step(0, "end", True)
            self.held = [out[0]] + [along_x(out[s], s) for s in range(1, len(out))]
            if len(out) == 1:
                self.share_y(out[0])

        def share_y(self, value):
            self.held = [value] + [along_y(value, s) for s in range(1, ny)]

        def stacked(self, place, size):
            places = jnp.stack([(place - s) % size for s in range(size)]).astype(jnp.int32)
            value = stack(self.order.after(*self.held), places)
            self.order.did(value)
            return value

        def stack_x(self):
            self.share_y(self.stacked(self.at[0], nx))

        def stack_y(self):
            value = self.stacked(self.at[1], ny)
            self.held = [value, across(value)]

    def local(inputs, hidden_pre, cotangent, w_in, m_in, v_in, w_out, m_out, v_out):
        model = inputs.shape[1]
        hidden_width = hidden_pre.shape[1]
        shard = hidden_width // (nz * nx)
        rows = model // (nz * nx)
        cuts = widths(shard)
        chunks = range(len(cuts))
        last = len(cuts) - 1
        starts = [sum(cuts[:k]) for k in chunks]
        scale_in = 1.0 / math.sqrt(model)
        scale_out = 1.0 / math.sqrt(hidden_width)
        place = lax.axis_index("gx")
        side = lax.axis_index("gy")
        z, x = place // nx, place % nx
        y, c = side // CORES, side % CORES
        core = jnp.reshape(c, (1,)).astype(jnp.int32)
        order = Order()
        hops = nz.bit_length() - 1

        cots = [cotangent] + [along_x(cotangent, s) for s in range(1, nx)]
        hiddens = [[] for _ in chunks]
        sends = []
        for s in range(1, nx):
            sends.append(take_columns(*order.after(hidden_pre), (x + s) % nx, nz, nx, cuts))
            order.did(sends[-1][0])
        late = last if last > 1 else last + 1
        for k in range(late):
            hiddens[k] = [along_x(sends[s - 1][k], s) for s in range(1, nx)]

        part = half_rows(*order.after(w_out), core)
        order.did(part)
        found = {0: part}
        bit = nz // 2
        while bit:
            for key in list(found):
                found[key ^ bit] = along_z(found[key], bit)
            bit //= 2

        flipped = transposed(*order.after(inputs))
        order.did(flipped)
        own = take_columns(*order.after(hidden_pre), x, nz, nx, cuts)
        order.did(own[0])
        came = cots[1:] + hiddens[0]
        tied = lax.optimization_barrier((flipped, *[value[k] for value in sends for k in chunks], *came))
        for k in range(late, len(cuts)):
            hiddens[k] = [along_x(tied[1 + (s - 1) * len(cuts) + k], s) for s in range(1, nx)]
        columns = [flipped] + [along_x(tied[0], s) for s in range(1, nx)]
        hiddens = [[own[k]] + hiddens[k] for k in chunks]

        outs = [None for _ in chunks]
        ins = [None for _ in chunks]
        pres = [None for _ in chunks]

        def stack_weights():
            places = jnp.stack([z ^ key for key in range(nz)]).astype(jnp.int32)
            mine = stack(order.after(*[found[key] for key in range(nz)]), places)
            order.did(mine)
            return [mine, across(mine)]

        def start_out(k):
            got = order.after(*hiddens[k], *cots)
            send, keep = grad_out_chunk(got[:nx], got[nx:], core, scale_out)
            order.did(keep)
            outs[k] = Reduce(
                order, (x, y, z), send, keep, (1, nz, 1, ny, cuts[k] // ny, model // CORES)
            )

        def start_pre(k):
            got = order.after(*hiddens[k], *cots, *weights)
            pres[k] = grad_pre_chunk(got[:nx], got[nx : 2 * nx], got[-2], got[-1], starts[k], core, scale_out)
            order.did(pres[k][0])

        def start_in(k):
            got = order.after(*pres[k], *columns)
            send, keep = grad_in_chunk(got[:nx], got[nx:], core, scale_in)
            order.did(keep)
            ins[k] = Reduce(
                order, (x, y, z), send, keep, (nz // CORES, nz, nx, ny, rows // ny, cuts[k])
            )

        def sums(tile):
            tiles = order.after(*([tile] + [along_z(tile, flip) for flip in range(1, nz)]))
            tile = add_tiles(tiles)
            order.did(tile)
            return [tile] + [along_x(tile, s) for s in range(1, nx)]

        def new_weights(weight, update, tiles):
            got = order.after(weight, update, *tiles)
            value = step_weights(got[0], got[1], got[2:])
            order.did(value)
            return value

        for k in chunks:
            start_out(k)
            if k == 0:
                weights = stack_weights()
            if k > 0:
                outs[k - 1].send_z()
            outs[k].send_y()
            start_pre(k)
            if k > 0:
                outs[k - 1].send_z()
        for k in chunks[:-1]:
            outs[k].finish()
        outs[last].send_z()

        for k in chunks:
            start_in(k)
            ins[k].send_y()
            if k == 0:
                outs[last].send_z()
            elif k == 1:
                outs[last].finish()
        if last == 0:
            outs[last].finish()
        for k in chunks:
            outs[k].stack_y()
        ins[0].send_z()

        half = model // CORES
        got = order.after(
            w_out, m_out, v_out, *[outs[k].held[0] for k in chunks], *[outs[k].held[1] for k in chunks]
        )
        first_out, second_out, update_out, tile = moments_kernel(
            core,
            *got[:3],
            got[3 : 4 + last],
            got[4 + last :],
            (CORES,),
            pl.BlockSpec((shard, half), lambda n, c: (0, n)),
            [pl.BlockSpec((ny, 1, w // ny, half), lambda n, c: (0, 0, 0, 0)) for w in cuts],
            lambda n: n,
            0,
        )
        order.did(tile)
        for _ in range(hops - 1):
            ins[0].send_z()
        tiles = sums(tile)
        ins[0].finish()
        for k in range(1, len(cuts)):
            ins[k].send_z()
            ins[k - 1].stack_x()
            for _ in range(hops - 1):
                ins[k].send_z()
            ins[k - 1].stack_y()
            if k == 1:
                new_w_out = new_weights(w_out, update_out, tiles)
            ins[k].finish()
        if last == 0:
            new_w_out = new_weights(w_out, update_out, tiles)
        ins[last].stack_x()
        ins[last].stack_y()

        got = order.after(
            w_in, m_in, v_in, *[ins[k].held[0] for k in chunks], *[ins[k].held[1] for k in chunks]
        )
        mine, other = got[3 : 4 + last], got[4 + last :]
        if shard % LANES:
            joined = [
                jnp.stack([jnp.where(c == 0, a, b), jnp.where(c == 0, b, a)]) for a, b in zip(mine, other)
            ]
            grad = jnp.concatenate(joined, axis=-1).transpose(1, 4, 0, 3, 2, 5)
            grad = grad.reshape(rows, hidden_width).astype(F32)
            first_in, second_in, update_in = moments(*got[:3], grad)
            tile = jnp.concatenate(
                [
                    jnp.sum((value * value).reshape(-1, 8, LANES), axis=0)
                    for value in (w_in, update_in)
                ]
            )
        else:
            zs = nz // CORES
            first_in, second_in, update_in, tile = moments_kernel(
                core,
                *got[:3],
                mine,
                other,
                (nz * nx,),
                pl.BlockSpec((rows, shard), lambda n, c: (0, n)),
                [
                    pl.BlockSpec(
                        (ny, 1, 1, rows // ny, w), lambda n, c: (0, n % nx, n // nx % zs, 0, 0)
                    )
                    for w in cuts
                ],
                lambda n: n // nx // zs,
                1,
            )
        order.did(tile)
        new_w_in = new_weights(w_in, update_in, sums(tile))
        return (new_w_in, first_in, second_in, new_w_out, first_out, second_out)

    return local


def solution(mesh):
    gx, gy = mesh.shape["gx"], mesh.shape["gy"]
    nz = CHIPS_Z
    state = P("gx", None)
    tokens = P(("gx", "gy"), None)
    return jax.shard_map(
        plan(nz, gx // nz, gy // CORES),
        mesh=mesh,
        in_specs=(tokens,) * 3 + (state,) * 6,
        out_specs=(state,) * 6,
        check_vma=False,
    )
```

```python
import functools
import math

import jax
import jax.numpy as jnp
from jax import lax
from jax.experimental import pallas as pl
from jax.experimental.pallas import tpu as pltpu
from jax.sharding import PartitionSpec as P

BF16 = jnp.bfloat16
F32 = jnp.float32
CORES = 2
CHIPS_Z = 4
LANES = 128
PARTS = 2
VMEM = 56 * 1024 * 1024


def moments(weight, first, second, grad):
    new_first = 0.9 * first + 0.1 * grad
    new_second = 0.95 * second + 0.05 * grad * grad
    update = new_first / (jnp.sqrt(new_second) + 1e-06) + 0.05 * weight
    return (new_first, new_second, update)


def squares(value):
    return jnp.sum(value * value)


def gelu(value):
    return 0.5 * value * (1.0 + lax.erf(value * (1.0 / math.sqrt(2.0))))


def gelu_slope(value):
    cdf = 0.5 * (1.0 + lax.erf(value * (1.0 / math.sqrt(2.0))))
    return cdf + value * (jnp.exp(-0.5 * value * value) * (1.0 / math.sqrt(2.0 * math.pi)))


def widths(shard):
    if shard % LANES:
        return (shard,)
    first = shard // LANES * 2 // 5 * LANES
    return (first, shard - first)


def dot(left, right, dims):
    return lax.dot_general(left, right, (dims, ((), ())), preferred_element_type=F32)


def params():
    return dict(
        compiler_params=pltpu.CompilerParams(vmem_limit_bytes=VMEM),
        cost_estimate=pl.CostEstimate(flops=1, bytes_accessed=1, transcendentals=0),
    )


def pack(hidden, cotangent, at, nz, nx, cuts):
    tokens, hidden_width = hidden.shape
    model = cotangent.shape[1]
    shard = hidden_width // (nz * nx)
    first = cuts[0]
    if shard % LANES:
        parts = [
            lax.dynamic_slice_in_dim(hidden, (z * nx + at) * shard, shard, 1).T for z in range(nz)
        ]
        return [jnp.concatenate([cotangent.T, *parts])]

    def body(at_ref, h_ref, cot_ref, out_ref, *later_refs):
        z = pl.program_id(0)

        @pl.when(z == 0)
        def _():
            out_ref[:model] = cot_ref[...].T

        out_ref[pl.ds(pl.multiple_of(model + z * first, LANES), first)] = h_ref[:, :first].T
        start = first
        for width, later_ref in zip(cuts[1:], later_refs):
            later_ref[0] = h_ref[:, start : start + width].T
            start += width

    total = model + nz * first
    return pl.pallas_call(
        body,
        grid_spec=pltpu.PrefetchScalarGridSpec(
            num_scalar_prefetch=1,
            grid=(nz,),
            in_specs=[
                pl.BlockSpec((tokens, shard), lambda z, a: (0, z * nx + a[0])),
                pl.BlockSpec((tokens, model), lambda z, a: (0, 0)),
            ],
            out_specs=[pl.BlockSpec((total, tokens), lambda z, a: (0, 0))]
            + [pl.BlockSpec((1, w, tokens), lambda z, a: (z, 0, 0)) for w in cuts[1:]],
        ),
        out_shape=[jax.ShapeDtypeStruct((total, tokens), BF16)]
        + [jax.ShapeDtypeStruct((nz, w, tokens), BF16) for w in cuts[1:]],
        **params(),
    )(jnp.reshape(at, (1,)).astype(jnp.int32), hidden, cotangent)


class Tokens:
    def __init__(self, packs, hiddens, model, nz, width):
        tokens = packs[0].shape[1]
        self.model, self.width, self.count = model, width, len(packs)
        if hiddens is None:
            self.arrays = list(packs)
            self.specs = [pl.BlockSpec(packs[0].shape, lambda z, c: (0, 0))] * len(packs)
        else:
            self.arrays = [*packs, *hiddens]
            self.specs = [pl.BlockSpec((model, tokens), lambda z, c: (0, 0))] * len(packs)
            self.specs += [pl.BlockSpec((1, width, tokens), lambda z, c: (z, 0, 0))] * len(packs)

    def cot(self, refs, n):
        return refs[n].at[: self.model]

    def hidden(self, refs, n):
        if len(refs) == self.count:
            row = self.model + pl.program_id(0) * self.width
            return refs[n][pl.ds(pl.multiple_of(row, 16), self.width)].astype(F32)
        return refs[self.count + n][0].astype(F32)


def grad_out_chunk(tokens, core, nz, scale):
    width, model = tokens.width, tokens.model
    half = model // CORES
    high = width // PARTS
    count = len(tokens.arrays)

    def body(c_ref, *refs):
        ins, outs = refs[:count], refs[count:]
        acts = jnp.concatenate(
            [gelu(tokens.hidden(ins, n)).astype(BF16) for n in range(tokens.count)], axis=1
        )
        for which in range(2):
            cols = pl.ds(pl.multiple_of((c_ref[0] + 1 + which) % CORES * half, 16), half)
            right = jnp.concatenate([tokens.cot(ins, n)[cols, :] for n in range(tokens.count)], axis=1)
            total = (dot(acts, right, ((1,), (1,))) * scale).astype(BF16)
            for p in range(PARTS):
                value = total[p * high : (p + 1) * high]
                if which:
                    outs[PARTS][p, 0] = value
                else:
                    outs[p][0] = value

    return pl.pallas_call(
        body,
        grid_spec=pltpu.PrefetchScalarGridSpec(
            num_scalar_prefetch=1,
            grid=(nz,),
            in_specs=tokens.specs,
            out_specs=[pl.BlockSpec((1, high, half), lambda z, c: (z, 0, 0))] * PARTS
            + [pl.BlockSpec((PARTS, 1, high, half), lambda z, c: (0, z, 0, 0))],
        ),
        out_shape=[jax.ShapeDtypeStruct((nz, high, half), BF16)] * PARTS
        + [jax.ShapeDtypeStruct((PARTS, nz, high, half), BF16)],
        **params(),
    )(core, *tokens.arrays)


def grad_pre_chunk(tokens, weights, row, scale):
    nz, shard, model = weights.shape
    width = tokens.width
    count = len(tokens.arrays)
    long = tokens.arrays[0].shape[1]

    def body(c_ref, *refs):
        ins = refs[:count]
        w_ref, out_ref = refs[count:]
        w = w_ref[0, row : row + width, :]
        for n in range(tokens.count):
            grad_act = dot(w, tokens.cot(ins, n)[...], ((1,), (0,))) * scale
            out_ref[0, :, n * long : (n + 1) * long] = (
                grad_act * gelu_slope(tokens.hidden(ins, n))
            ).astype(BF16)

    return pl.pallas_call(
        body,
        grid_spec=pltpu.PrefetchScalarGridSpec(
            num_scalar_prefetch=1,
            grid=(nz,),
            in_specs=tokens.specs + [pl.BlockSpec((1, shard, model), lambda z, c: (z, 0, 0))],
            out_specs=pl.BlockSpec((1, width, tokens.count * long), lambda z, c: (z, 0, 0)),
        ),
        out_shape=jax.ShapeDtypeStruct((nz, width, tokens.count * long), BF16),
        **params(),
    )(jnp.zeros((1,), jnp.int32), *tokens.arrays, weights)


def grad_in_chunk(grads, inputs, core, scale, cut):
    nz, width, long = grads.shape
    model, tokens = inputs[0].shape
    count = len(inputs)
    half = nz // CORES
    high = model // cut

    def body(c_ref, g_ref, *refs):
        in_refs, outs = refs[:count], refs[count:]
        left = jnp.concatenate([i[...] for i in in_refs], axis=1)
        total = (dot(left, g_ref[0], ((1,), (1,))) * scale).astype(BF16)
        step = pl.program_id(0)
        for n in range(half):

            @pl.when(step == n)
            def _(n=n):
                for h in range(cut):
                    outs[n * cut + h][...] = total[h * high : (h + 1) * high]

        @pl.when(step >= half)
        def _():
            outs[-1][0] = total

    return pl.pallas_call(
        body,
        grid_spec=pltpu.PrefetchScalarGridSpec(
            num_scalar_prefetch=1,
            grid=(nz,),
            in_specs=[
                pl.BlockSpec(
                    (1, width, long),
                    lambda z, c: ((c[0] + 1 + z // half) % CORES * half + z % half, 0, 0),
                )
            ]
            + [pl.BlockSpec((model, tokens), lambda z, c: (0, 0))] * count,
            out_specs=[pl.BlockSpec((high, width), lambda z, c: (0, 0))] * (half * cut)
            + [pl.BlockSpec((1, model, width), lambda z, c: (jnp.maximum(z - half, 0), 0, 0))],
        ),
        out_shape=[jax.ShapeDtypeStruct((high, width), BF16)] * (half * cut)
        + [jax.ShapeDtypeStruct((half, model, width), BF16)],
        **params(),
    )(core, grads, *inputs)


def transposed(value):
    rows, cols = value.shape
    wide = 2 * LANES

    def body(in_ref, out_ref):
        out_ref[...] = in_ref[...].T

    return pl.pallas_call(
        body,
        grid=(cols // wide,),
        in_specs=[pl.BlockSpec((rows, wide), lambda n: (0, n))],
        out_specs=pl.BlockSpec((wide, rows), lambda n: (n, 0)),
        out_shape=jax.ShapeDtypeStruct((cols, rows), value.dtype),
        **params(),
    )(value)


def half_rows(weight, core):
    rows, cols = weight.shape
    part = rows // CORES
    wide = 2 * LANES

    def body(c_ref, in_ref, out_ref):
        out_ref[...] = in_ref[...].astype(BF16)

    return pl.pallas_call(
        body,
        grid_spec=pltpu.PrefetchScalarGridSpec(
            num_scalar_prefetch=1,
            grid=(cols // wide,),
            in_specs=[pl.BlockSpec((part, wide), lambda n, c: (c[0], n))],
            out_specs=pl.BlockSpec((part, wide), lambda n, c: (0, n)),
        ),
        out_shape=jax.ShapeDtypeStruct((part, cols), BF16),
        **params(),
    )(core, weight)


def stack(pieces, places, inner=False):
    count = len(pieces)
    shape = pieces[0].shape
    out = (shape[0], count, *shape[1:]) if inner else (count, *shape)

    def body(at_ref, *refs):
        for n in range(count):
            if inner:
                for p in range(shape[0]):
                    refs[count][p, at_ref[n]] = refs[n][p]
            else:
                refs[count][at_ref[n]] = refs[n][...]

    return pl.pallas_call(
        body,
        grid_spec=pltpu.PrefetchScalarGridSpec(
            num_scalar_prefetch=1,
            grid=(),
            in_specs=[pl.BlockSpec(shape, lambda at: (0,) * len(shape))] * count,
            out_specs=pl.BlockSpec(out, lambda at: (0,) * len(out)),
        ),
        out_shape=jax.ShapeDtypeStruct(out, pieces[0].dtype),
        **params(),
    )(places, *pieces)


def stack_rows(pieces, places):
    count = len(pieces)
    high, cols = pieces[0].shape
    wide = 2 * LANES
    parts = CORES

    def body(at_ref, *refs):
        for n in range(count):
            row = pl.multiple_of(at_ref[1, n] * high, 16)
            refs[count][at_ref[0, n], pl.ds(row, high)] = refs[n][...]

    return pl.pallas_call(
        body,
        grid_spec=pltpu.PrefetchScalarGridSpec(
            num_scalar_prefetch=1,
            grid=(cols // wide,),
            in_specs=[pl.BlockSpec((high, wide), lambda n, at: (0, n))] * count,
            out_specs=pl.BlockSpec((count // parts, parts * high, wide), lambda n, at: (0, 0, n)),
        ),
        out_shape=jax.ShapeDtypeStruct((count // parts, parts * high, cols), pieces[0].dtype),
        **params(),
    )(places, *pieces)


def add_tiles(tiles):
    def body(*refs):
        refs[-1][...] = sum(ref[...] for ref in refs[:-1])

    return pl.pallas_call(
        body, out_shape=jax.ShapeDtypeStruct(tiles[0].shape, F32), **params()
    )(*tiles)


def reduce_step(place, keep, crosses, from_y, from_z, shift, stage, ny, split):
    lead, nz, mid, _, high, wide = keep.shape
    bit = len(from_z)

    def zed(n, at):
        if stage == "y":
            return n
        if stage == "end":
            return at[2]
        low = at[2] % (1 << bit)
        mine = (at[2] // (1 << bit)) % 2
        return n * (2 << bit) + (1 - mine) * (1 << bit) + low

    count = {"y": nz, "z": nz >> (bit + 1), "end": 1}[stage]
    six = (lead, 1, mid, 1, high, wide)
    five = (lead, 1, mid, high, wide)
    specs = [pl.BlockSpec(six, lambda n, at: (0, zed(n, at), 0, (at[1] + shift) % ny, 0, 0))]
    each = len(crosses) // lead
    long = nz // each
    for h in range(len(crosses)):
        specs.append(
            pl.BlockSpec(
                six[1:],
                lambda n, at, h=h % each: (
                    jnp.clip(zed(n, at) - h * long, 0, long - 1),
                    0,
                    (at[1] + shift) % ny,
                    0,
                    0,
                ),
            )
        )
    specs += [pl.BlockSpec(five, lambda n, at: (0, zed(n, at), 0, 0, 0))] * len(from_y)
    specs += [
        pl.BlockSpec(five, lambda n, at, j=j: (0, zed(n, at) // (2 << j), 0, 0, 0)) for j in range(bit)
    ]

    def body(at_ref, *refs):
        ins = refs[: len(specs)]
        outs = refs[len(specs) :]
        for p in range(lead):
            for m in range(mid):
                total = ins[1 + p * each][0, m, 0]
                for h in range(1, each):
                    total = jnp.where(
                        zed(pl.program_id(0), at_ref) >= h * long, ins[1 + p * each + h][0, m, 0], total
                    )
                total = total.astype(F32) + ins[0][p, 0, m, 0].astype(F32)
                for ref in ins[1 + len(crosses) :]:
                    total = total + ref[p, 0, m].astype(F32)
                total = total.astype(BF16)
                if not split:
                    outs[0][p, 0, m] = total
                    continue
                for s in range(mid):

                    @pl.when((at_ref[0] + s) % mid == m)
                    def _(s=s, total=total):
                        outs[s][p] = total

    if split:
        out_specs = [pl.BlockSpec((lead, high, wide), lambda n, at: (0, 0, 0))] * mid
        out_shape = [jax.ShapeDtypeStruct((lead, high, wide), BF16)] * mid
    else:
        out_specs = [pl.BlockSpec(five, lambda n, at: (0, n, 0, 0, 0))]
        out_shape = [jax.ShapeDtypeStruct((lead, count, mid, high, wide), BF16)]
    out = pl.pallas_call(
        body,
        grid_spec=pltpu.PrefetchScalarGridSpec(
            num_scalar_prefetch=1, grid=(count,), in_specs=specs, out_specs=out_specs
        ),
        out_shape=out_shape,
        **params(),
    )(place, keep, *crosses, *from_y, *from_z)
    return out if split else out[0]


def moments_kernel(core, weight, first, second, mine, other, grid, state_spec, grad_specs, owner, axis):
    block = state_spec.block_shape
    count = len(mine)

    def body(c_ref, w_ref, m_ref, v_ref, *refs):
        mine_refs, other_refs = refs[:count], refs[count : 2 * count]
        new_m_ref, new_v_ref, u_ref, sum_ref = refs[2 * count :]
        totals = [jnp.zeros((8, LANES), F32)] * 2
        start = 0
        ours = owner(pl.program_id(0)) == c_ref[0]
        for mine_ref, other_ref in zip(mine_refs, other_refs):
            size = mine_ref.size // block[1 - axis]
            shape = (size, block[1]) if axis == 0 else (block[0], size)
            at = (slice(start, start + size), slice(None))
            at = at if axis == 0 else at[::-1]
            grad = jnp.where(ours, mine_ref[...].reshape(shape), other_ref[...].reshape(shape)).astype(F32)
            weight = w_ref[at]
            new_m, new_v, update = moments(weight, m_ref[at], v_ref[at], grad)
            new_m_ref[at] = new_m
            new_v_ref[at] = new_v
            u_ref[at] = update
            for n, value in enumerate((weight, update)):
                square = value * value
                for col in range(0, shape[1], LANES):
                    totals[n] = totals[n] + square[:, col : col + LANES].reshape(-1, 8, LANES).sum(0)
            start += size

        @pl.when(pl.program_id(0) == 0)
        def _():
            sum_ref[...] = jnp.zeros_like(sum_ref)

        sum_ref[:8] += totals[0]
        sum_ref[8:] += totals[1]

    state = jax.ShapeDtypeStruct(weight.shape, F32)
    return pl.pallas_call(
        body,
        grid_spec=pltpu.PrefetchScalarGridSpec(
            num_scalar_prefetch=1,
            grid=grid,
            in_specs=[state_spec] * 3 + grad_specs * 2,
            out_specs=[state_spec] * 3 + [pl.BlockSpec((16, LANES), lambda n, c: (0, 0))],
        ),
        out_shape=[state] * 3 + [jax.ShapeDtypeStruct((16, LANES), F32)],
        **params(),
    )(core, weight, first, second, *mine, *other)


def step_weights(weight, update, tiles):
    rows, cols = weight.shape
    high = rows // 5
    count = len(tiles)

    def body(w_ref, u_ref, *refs):
        sums = sum(ref[...] for ref in refs[:count])
        ratio = jnp.sqrt(jnp.sum(sums[:8], keepdims=True)) / jnp.sqrt(jnp.sum(sums[8:], keepdims=True))
        refs[count][...] = w_ref[...] - 0.4 * ratio * u_ref[...]

    spec = pl.BlockSpec((high, cols), lambda n: (n, 0))
    tile = pl.BlockSpec((16, LANES), lambda n: (0, 0))
    return pl.pallas_call(
        body,
        grid=(rows // high,),
        in_specs=[spec] * 2 + [tile] * count,
        out_specs=spec,
        out_shape=jax.ShapeDtypeStruct(weight.shape, F32),
        **params(),
    )(weight, update, *tiles)


class Order:
    def __init__(self):
        self.last = None

    def after(self, *values):
        if self.last is None:
            return values
        return lax.optimization_barrier((*values, self.last))[:-1]

    def did(self, value):
        self.last = value


def plan(nz, nx, ny):
    def along_x(value, step):
        pairs = [
            (z * nx + x, z * nx + (x + step) % nx) for z in range(nz) for x in range(nx)
        ]
        return lax.ppermute(value, "gx", pairs)

    def along_z(value, flip):
        pairs = [(z * nx + x, (z ^ flip) * nx + x) for z in range(nz) for x in range(nx)]
        return lax.ppermute(value, "gx", pairs)

    def along_y(value, step):
        pairs = [
            (y * CORES + c, (y + step) % ny * CORES + c) for y in range(ny) for c in range(CORES)
        ]
        return lax.ppermute(value, "gy", pairs)

    def across(value):
        pairs = [(k, k ^ 1) for k in range(ny * CORES)]
        return lax.ppermute(value, "gy", pairs)

    class Reduce:
        def __init__(self, order, at, sends, keep, shape):
            self.order, self.at, self.place = order, at, jnp.stack(at).astype(jnp.int32)
            self.keep = keep.reshape(shape)
            each = len(sends) // shape[0]
            self.crosses = [
                across(send).reshape(shape[1] // each, *shape[2:]) for send in sends
            ]
            self.from_y = []
            self.from_z = []

        def step(self, shift, stage, split=False):
            got = self.order.after(self.keep, *self.crosses, *self.from_y, *self.from_z)
            lead = 1 + len(self.crosses)
            count = lead + len(self.from_y)
            out = reduce_step(
                self.place, got[0], got[1:lead], got[lead:count], got[count:], shift, stage, ny, split
            )
            self.order.did(out[0] if split else out)
            return out

        def send_y(self):
            from_y = []
            for s in range(1, ny):
                from_y.append(along_y(self.step(s, "y"), s))
            self.from_y = from_y

        def send_z(self):
            bit = len(self.from_z)
            self.from_z.append(along_z(self.step(0, "z"), 1 << bit))

        def finish(self):
            out = self.step(0, "end", True)
            self.held = [out[0]] + [along_x(out[s], s) for s in range(1, len(out))]
            if len(out) == 1:
                self.share_y(out[0])

        def share_y(self, value):
            self.held = [value] + [along_y(value, s) for s in range(1, ny)]

        def stacked(self, place, size, inner=False):
            places = jnp.stack([(place - s) % size for s in range(size)]).astype(jnp.int32)
            value = stack(self.order.after(*self.held), places, inner)
            self.order.did(value)
            return value

        def stack_x(self):
            self.share_y(self.stacked(self.at[0], nx))

        def stack_y(self, inner=False):
            value = self.stacked(self.at[1], ny, inner)
            self.held = [value, across(value)]

    def local(inputs, hidden_pre, cotangent, w_in, m_in, v_in, w_out, m_out, v_out):
        model = inputs.shape[1]
        hidden_width = hidden_pre.shape[1]
        shard = hidden_width // (nz * nx)
        rows = model // (nz * nx)
        cuts = widths(shard)
        chunks = range(len(cuts))
        last = len(cuts) - 1
        starts = [sum(cuts[:k]) for k in chunks]
        scale_in = 1.0 / math.sqrt(model)
        scale_out = 1.0 / math.sqrt(hidden_width)
        place = lax.axis_index("gx")
        side = lax.axis_index("gy")
        z, x = place // nx, place % nx
        y, c = side // CORES, side % CORES
        core = jnp.reshape(c, (1,)).astype(jnp.int32)
        order = Order()

        packs, hiddens = [], []
        for t in range(1, nx):
            sent = pack(*order.after(hidden_pre, cotangent), (x + t) % nx, nz, nx, cuts)
            order.did(sent[0])
            packs.append(along_x(sent[0], t))
            hiddens.append([along_x(value, t) for value in sent[1:]])

        part = half_rows(*order.after(w_out), core)
        order.did(part)
        flipped = transposed(*order.after(inputs))
        order.did(flipped)
        columns = [flipped] + [along_x(flipped, t) for t in range(1, nx)]
        own = pack(*order.after(hidden_pre, cotangent), x, nz, nx, cuts)
        order.did(own[0])
        found = {0: part, nz // 2: along_z(part, nz // 2)}
        bit = nz // 4
        while bit:
            for key in list(found):
                value = found[key]
                if key:
                    (value,) = order.after(value)
                found[key ^ bit] = along_z(value, bit)
            bit //= 2
        crossed = [across(found[key]) for key in range(nz)]
        packs = [own[0]] + packs
        hiddens = [own[1:]] + hiddens

        outs = [None for _ in chunks]
        ins = [None for _ in chunks]
        pres = [None for _ in chunks]

        def stack_weights():
            pieces = order.after(*[found[key] for key in range(nz)], *crossed)
            blocks = jnp.stack([z ^ key for key in range(nz)] * CORES)
            halves = jnp.stack([c] * nz + [1 - c] * nz)
            value = stack_rows(pieces, jnp.stack([blocks, halves]).astype(jnp.int32))
            order.did(value)
            return value

        def tokens(k, *more):
            later = [] if k == 0 else [value[k - 1] for value in hiddens]
            got = order.after(*packs, *later, *more)
            count = nx + len(later)
            blocks = Tokens(got[:nx], got[nx:count] if later else None, model, nz, cuts[k])
            return blocks, got[count:]

        def start_out(k):
            *sends, keep = grad_out_chunk(tokens(k)[0], core, nz, scale_out)
            order.did(keep)
            shape = (PARTS, nz, 1, ny, cuts[k] // PARTS // ny, model // CORES)
            outs[k] = Reduce(order, (x, y, z), sends, keep, shape)

        def start_pre(k):
            blocks, got = tokens(k, weights)
            pres[k] = grad_pre_chunk(blocks, got[0], starts[k], scale_out)
            order.did(pres[k])

        def start_in(k):
            got = order.after(pres[k], *columns)
            *sends, keep = grad_in_chunk(got[0], got[1:], core, scale_in, PARTS if k else 1)
            order.did(keep)
            shape = (nz // CORES, nz, nx, ny, rows // ny, cuts[k])
            ins[k] = Reduce(order, (x, y, z), sends, keep, shape)

        def sums(tile, zs=None):
            zs = zs or [along_z(tile, flip) for flip in range(1, nz)]
            tiles = order.after(tile, *zs)
            tile = add_tiles(tiles)
            order.did(tile)
            return [tile] + [along_x(tile, s) for s in range(1, nx)]

        def new_weights(weight, update, tiles):
            got = order.after(weight, update, *tiles)
            value = step_weights(got[0], got[1], got[2:])
            order.did(value)
            return value

        start_out(0)
        outs[0].send_y()
        weights = stack_weights()
        start_pre(0)
        outs[0].send_z()
        start_in(0)
        ins[0].send_y()
        outs[0].send_z()
        if last:
            ins[0].send_z()
            start_out(1)
            outs[1].send_y()
            outs[0].finish()
            start_pre(1)
            ins[0].send_z()
            start_in(1)
            ins[1].send_y()
            ins[0].finish()
            outs[1].send_z()
            ins[0].stack_x()
            outs[0].stack_y(True)
            outs[1].send_z()
            ins[0].stack_y()
            outs[1].finish()
            ins[1].send_z()
            outs[1].stack_y(True)
            ins[1].send_z()
        else:
            outs[0].finish()
            ins[0].send_z()
            ins[0].send_z()
            outs[0].stack_y(True)

        half = model // CORES
        got = order.after(
            w_out, m_out, v_out, *[outs[k].held[0] for k in chunks], *[outs[k].held[1] for k in chunks]
        )
        first_out, second_out, update_out, tile = moments_kernel(
            core,
            *got[:3],
            got[3 : 4 + last],
            got[4 + last :],
            (CORES,),
            pl.BlockSpec((shard, half), lambda n, c: (0, n)),
            [
                pl.BlockSpec((PARTS, ny, w // PARTS // ny, half), lambda n, c: (0, 0, 0, 0)) for w in cuts
            ],
            lambda n: n,
            0,
        )
        order.did(tile)
        ins[last].finish()
        tiles = sums(tile)
        ins[last].stack_x()
        ins[last].stack_y()

        got = order.after(
            w_in, m_in, v_in, *[ins[k].held[0] for k in chunks], *[ins[k].held[1] for k in chunks]
        )
        mine, other = got[3 : 4 + last], got[4 + last :]
        if shard % LANES:
            joined = [
                jnp.stack([jnp.where(c == 0, a, b), jnp.where(c == 0, b, a)]) for a, b in zip(mine, other)
            ]
            grad = jnp.concatenate(joined, axis=-1).transpose(1, 4, 0, 3, 2, 5)
            grad = grad.reshape(rows, hidden_width).astype(F32)
            first_in, second_in, update_in = moments(*got[:3], grad)
            tile = jnp.concatenate(
                [
                    jnp.sum((value * value).reshape(-1, 8, LANES), axis=0)
                    for value in (w_in, update_in)
                ]
            )
        else:
            zs = nz // CORES
            first_in, second_in, update_in, tile = moments_kernel(
                core,
                *got[:3],
                mine,
                other,
                (nz * nx,),
                pl.BlockSpec((rows, shard), lambda n, c: (0, n)),
                [
                    pl.BlockSpec(
                        (ny, 1, 1, rows // ny, w), lambda n, c: (0, n % nx, n // nx % zs, 0, 0)
                    )
                    for w in cuts
                ],
                lambda n: n // nx // zs,
                1,
            )
        order.did(tile)
        zs = [along_z(tile, flip) for flip in range(1, nz)]
        new_w_out = new_weights(w_out, update_out, tiles)
        new_w_in = new_weights(w_in, update_in, sums(tile, zs))
        return (new_w_in, first_in, second_in, new_w_out, first_out, second_out)

    return local


def solution(mesh):
    gx, gy = mesh.shape["gx"], mesh.shape["gy"]
    nz = CHIPS_Z
    state = P("gx", None)
    tokens = P(("gx", "gy"), None)
    return jax.shard_map(
        plan(nz, gx // nz, gy // CORES),
        mesh=mesh,
        in_specs=(tokens,) * 3 + (state,) * 6,
        out_specs=(state,) * 6,
        check_vma=False,
    )
```

```python
import functools
import math

import jax
import jax.numpy as jnp
from jax import lax
from jax.experimental import pallas as pl
from jax.experimental.pallas import tpu as pltpu
from jax.sharding import PartitionSpec as P

BF16 = jnp.bfloat16
F32 = jnp.float32
CORES = 2
CHIPS_Z = 4
LANES = 128
PARTS = 2
VMEM = 24 * 1024 * 1024


def moments(weight, first, second, grad):
    new_first = 0.9 * first + 0.1 * grad
    new_second = 0.95 * second + 0.05 * grad * grad
    update = new_first / (jnp.sqrt(new_second) + 1e-06) + 0.05 * weight
    return (new_first, new_second, update)


def squares(value):
    return jnp.sum(value * value)


def gelu(value):
    return 0.5 * value * (1.0 + lax.erf(value * (1.0 / math.sqrt(2.0))))


def gelu_slope(value):
    cdf = 0.5 * (1.0 + lax.erf(value * (1.0 / math.sqrt(2.0))))
    return cdf + value * (jnp.exp(-0.5 * value * value) * (1.0 / math.sqrt(2.0 * math.pi)))


def widths(shard):
    if shard % LANES:
        return (shard,)
    first = shard // LANES * 2 // 5 * LANES
    return (first, shard - first)


def dot(left, right, dims):
    return lax.dot_general(left, right, (dims, ((), ())), preferred_element_type=F32)


def params():
    return dict(
        compiler_params=pltpu.CompilerParams(vmem_limit_bytes=VMEM),
        cost_estimate=pl.CostEstimate(flops=1, bytes_accessed=1, transcendentals=0),
    )


def pack(hidden, cotangent, at, nz, nx, cuts):
    tokens, hidden_width = hidden.shape
    model = cotangent.shape[1]
    shard = hidden_width // (nz * nx)
    first = cuts[0]
    if shard % LANES:
        parts = [
            lax.dynamic_slice_in_dim(hidden, (z * nx + at) * shard, shard, 1).T for z in range(nz)
        ]
        return [jnp.concatenate([cotangent.T, *parts])]

    def body(at_ref, h_ref, cot_ref, out_ref, *later_refs):
        z = pl.program_id(0)

        @pl.when(z == 0)
        def _():
            out_ref[:model] = cot_ref[...].T

        out_ref[pl.ds(pl.multiple_of(model + z * first, LANES), first)] = h_ref[:, :first].T
        start = first
        for width, later_ref in zip(cuts[1:], later_refs):
            later_ref[0] = h_ref[:, start : start + width].T
            start += width

    total = model + nz * first
    return pl.pallas_call(
        body,
        grid_spec=pltpu.PrefetchScalarGridSpec(
            num_scalar_prefetch=1,
            grid=(nz,),
            in_specs=[
                pl.BlockSpec((tokens, shard), lambda z, a: (0, z * nx + a[0])),
                pl.BlockSpec((tokens, model), lambda z, a: (0, 0)),
            ],
            out_specs=[pl.BlockSpec((total, tokens), lambda z, a: (0, 0))]
            + [pl.BlockSpec((1, w, tokens), lambda z, a: (z, 0, 0)) for w in cuts[1:]],
        ),
        out_shape=[jax.ShapeDtypeStruct((total, tokens), BF16)]
        + [jax.ShapeDtypeStruct((nz, w, tokens), BF16) for w in cuts[1:]],
        **params(),
    )(jnp.reshape(at, (1,)).astype(jnp.int32), hidden, cotangent)


class Tokens:
    def __init__(self, packs, hiddens, model, nz, width):
        tokens = packs[0].shape[1]
        self.model, self.width, self.count = model, width, len(packs)
        if hiddens is None:
            self.arrays = list(packs)
            self.specs = [pl.BlockSpec(packs[0].shape, lambda z, c: (0, 0))] * len(packs)
        else:
            self.arrays = [*packs, *hiddens]
            self.specs = [pl.BlockSpec((model, tokens), lambda z, c: (0, 0))] * len(packs)
            self.specs += [pl.BlockSpec((1, width, tokens), lambda z, c: (z, 0, 0))] * len(packs)

    def cot(self, refs, n):
        return refs[n].at[: self.model]

    def hidden(self, refs, n):
        if len(refs) == self.count:
            row = self.model + pl.program_id(0) * self.width
            return refs[n][pl.ds(pl.multiple_of(row, 16), self.width)].astype(F32)
        return refs[self.count + n][0].astype(F32)


def grad_out_chunk(tokens, core, nz, scale):
    width, model = tokens.width, tokens.model
    half = model // CORES
    high = width // PARTS
    count = len(tokens.arrays)

    def body(c_ref, *refs):
        ins, outs = refs[:count], refs[count:]
        acts = jnp.concatenate(
            [gelu(tokens.hidden(ins, n)).astype(BF16) for n in range(tokens.count)], axis=1
        )
        for which in range(2):
            cols = pl.ds(pl.multiple_of((c_ref[0] + 1 + which) % CORES * half, 16), half)
            right = jnp.concatenate([tokens.cot(ins, n)[cols, :] for n in range(tokens.count)], axis=1)
            total = (dot(acts, right, ((1,), (1,))) * scale).astype(BF16)
            for p in range(PARTS):
                value = total[p * high : (p + 1) * high]
                if which:
                    outs[PARTS][p, 0] = value
                else:
                    outs[p][0] = value

    return pl.pallas_call(
        body,
        grid_spec=pltpu.PrefetchScalarGridSpec(
            num_scalar_prefetch=1,
            grid=(nz,),
            in_specs=tokens.specs,
            out_specs=[pl.BlockSpec((1, high, half), lambda z, c: (z, 0, 0))] * PARTS
            + [pl.BlockSpec((PARTS, 1, high, half), lambda z, c: (0, z, 0, 0))],
        ),
        out_shape=[jax.ShapeDtypeStruct((nz, high, half), BF16)] * PARTS
        + [jax.ShapeDtypeStruct((PARTS, nz, high, half), BF16)],
        **params(),
    )(core, *tokens.arrays)


def grad_pre_chunk(tokens, weights, row, scale):
    nz, shard, model = weights.shape
    width = tokens.width
    count = len(tokens.arrays)
    long = tokens.arrays[0].shape[1]

    def body(c_ref, *refs):
        ins = refs[:count]
        w_ref, out_ref = refs[count:]
        w = w_ref[0, row : row + width, :]
        for n in range(tokens.count):
            grad_act = dot(w, tokens.cot(ins, n)[...], ((1,), (0,))) * scale
            out_ref[0, :, n * long : (n + 1) * long] = (
                grad_act * gelu_slope(tokens.hidden(ins, n))
            ).astype(BF16)

    return pl.pallas_call(
        body,
        grid_spec=pltpu.PrefetchScalarGridSpec(
            num_scalar_prefetch=1,
            grid=(nz,),
            in_specs=tokens.specs + [pl.BlockSpec((1, shard, model), lambda z, c: (z, 0, 0))],
            out_specs=pl.BlockSpec((1, width, tokens.count * long), lambda z, c: (z, 0, 0)),
        ),
        out_shape=jax.ShapeDtypeStruct((nz, width, tokens.count * long), BF16),
        **params(),
    )(jnp.zeros((1,), jnp.int32), *tokens.arrays, weights)


def grad_in_chunk(grads, inputs, core, scale, cut):
    nz, width, long = grads.shape
    model, tokens = inputs[0].shape
    count = len(inputs)
    half = nz // CORES
    high = model // cut

    def body(c_ref, g_ref, *refs):
        in_refs, outs = refs[:count], refs[count:]
        left = jnp.concatenate([i[...] for i in in_refs], axis=1)
        total = (dot(left, g_ref[0], ((1,), (1,))) * scale).astype(BF16)
        step = pl.program_id(0)
        for n in range(half):

            @pl.when(step == n)
            def _(n=n):
                for h in range(cut):
                    outs[n * cut + h][...] = total[h * high : (h + 1) * high]

        @pl.when(step >= half)
        def _():
            outs[-1][0] = total

    return pl.pallas_call(
        body,
        grid_spec=pltpu.PrefetchScalarGridSpec(
            num_scalar_prefetch=1,
            grid=(nz,),
            in_specs=[
                pl.BlockSpec(
                    (1, width, long),
                    lambda z, c: ((c[0] + 1 + z // half) % CORES * half + z % half, 0, 0),
                )
            ]
            + [pl.BlockSpec((model, tokens), lambda z, c: (0, 0))] * count,
            out_specs=[pl.BlockSpec((high, width), lambda z, c: (0, 0))] * (half * cut)
            + [pl.BlockSpec((1, model, width), lambda z, c: (jnp.maximum(z - half, 0), 0, 0))],
        ),
        out_shape=[jax.ShapeDtypeStruct((high, width), BF16)] * (half * cut)
        + [jax.ShapeDtypeStruct((half, model, width), BF16)],
        **params(),
    )(core, grads, *inputs)


def transposed(value):
    rows, cols = value.shape
    wide = 2 * LANES

    def body(in_ref, out_ref):
        out_ref[...] = in_ref[...].T

    return pl.pallas_call(
        body,
        grid=(cols // wide,),
        in_specs=[pl.BlockSpec((rows, wide), lambda n: (0, n))],
        out_specs=pl.BlockSpec((wide, rows), lambda n: (n, 0)),
        out_shape=jax.ShapeDtypeStruct((cols, rows), value.dtype),
        **params(),
    )(value)


def half_rows(weight, core):
    rows, cols = weight.shape
    part = rows // CORES
    wide = 2 * LANES

    def body(c_ref, in_ref, out_ref):
        out_ref[...] = in_ref[...].astype(BF16)

    return pl.pallas_call(
        body,
        grid_spec=pltpu.PrefetchScalarGridSpec(
            num_scalar_prefetch=1,
            grid=(cols // wide,),
            in_specs=[pl.BlockSpec((part, wide), lambda n, c: (c[0], n))],
            out_specs=pl.BlockSpec((part, wide), lambda n, c: (0, n)),
        ),
        out_shape=jax.ShapeDtypeStruct((part, cols), BF16),
        **params(),
    )(core, weight)


def stack(pieces, places, inner=False):
    count = len(pieces)
    shape = pieces[0].shape
    out = (shape[0], count, *shape[1:]) if inner else (count, *shape)

    def body(at_ref, *refs):
        for n in range(count):
            if inner:
                for p in range(shape[0]):
                    refs[count][p, at_ref[n]] = refs[n][p]
            else:
                refs[count][at_ref[n]] = refs[n][...]

    return pl.pallas_call(
        body,
        grid_spec=pltpu.PrefetchScalarGridSpec(
            num_scalar_prefetch=1,
            grid=(),
            in_specs=[pl.BlockSpec(shape, lambda at: (0,) * len(shape))] * count,
            out_specs=pl.BlockSpec(out, lambda at: (0,) * len(out)),
        ),
        out_shape=jax.ShapeDtypeStruct(out, pieces[0].dtype),
        **params(),
    )(places, *pieces)


def stack_rows(pieces, places):
    count = len(pieces)
    high, cols = pieces[0].shape
    wide = 2 * LANES
    parts = CORES

    def body(at_ref, *refs):
        for n in range(count):
            row = pl.multiple_of(at_ref[1, n] * high, 16)
            refs[count][at_ref[0, n], pl.ds(row, high)] = refs[n][...]

    return pl.pallas_call(
        body,
        grid_spec=pltpu.PrefetchScalarGridSpec(
            num_scalar_prefetch=1,
            grid=(cols // wide,),
            in_specs=[pl.BlockSpec((high, wide), lambda n, at: (0, n))] * count,
            out_specs=pl.BlockSpec((count // parts, parts * high, wide), lambda n, at: (0, 0, n)),
        ),
        out_shape=jax.ShapeDtypeStruct((count // parts, parts * high, cols), pieces[0].dtype),
        **params(),
    )(places, *pieces)


def add_tiles(tiles):
    def body(*refs):
        refs[-1][...] = sum(ref[...] for ref in refs[:-1])

    return pl.pallas_call(
        body, out_shape=jax.ShapeDtypeStruct(tiles[0].shape, F32), **params()
    )(*tiles)


def reduce_step(place, keep, crosses, from_y, from_z, shift, stage, ny, split):
    lead, nz, mid, _, high, wide = keep.shape
    bit = len(from_z)

    def zed(n, at):
        if stage == "y":
            return n
        if stage == "end":
            return at[2]
        low = at[2] % (1 << bit)
        mine = (at[2] // (1 << bit)) % 2
        return n * (2 << bit) + (1 - mine) * (1 << bit) + low

    count = {"y": nz, "z": nz >> (bit + 1), "end": 1}[stage]
    six = (lead, 1, mid, 1, high, wide)
    five = (lead, 1, mid, high, wide)
    specs = [pl.BlockSpec(six, lambda n, at: (0, zed(n, at), 0, (at[1] + shift) % ny, 0, 0))]
    each = len(crosses) // lead
    long = nz // each
    for h in range(len(crosses)):
        specs.append(
            pl.BlockSpec(
                six[1:],
                lambda n, at, h=h % each: (
                    jnp.clip(zed(n, at) - h * long, 0, long - 1),
                    0,
                    (at[1] + shift) % ny,
                    0,
                    0,
                ),
            )
        )
    specs += [pl.BlockSpec(five, lambda n, at: (0, zed(n, at), 0, 0, 0))] * len(from_y)
    specs += [
        pl.BlockSpec(five, lambda n, at, j=j: (0, zed(n, at) // (2 << j), 0, 0, 0)) for j in range(bit)
    ]

    def body(at_ref, *refs):
        ins = refs[: len(specs)]
        outs = refs[len(specs) :]
        for p in range(lead):
            for m in range(mid):
                total = ins[1 + p * each][0, m, 0]
                for h in range(1, each):
                    total = jnp.where(
                        zed(pl.program_id(0), at_ref) >= h * long, ins[1 + p * each + h][0, m, 0], total
                    )
                total = total.astype(F32) + ins[0][p, 0, m, 0].astype(F32)
                for ref in ins[1 + len(crosses) :]:
                    total = total + ref[p, 0, m].astype(F32)
                total = total.astype(BF16)
                if not split:
                    outs[0][p, 0, m] = total
                    continue
                for s in range(mid):

                    @pl.when((at_ref[0] + s) % mid == m)
                    def _(s=s, total=total):
                        outs[s][p] = total

    if split:
        out_specs = [pl.BlockSpec((lead, high, wide), lambda n, at: (0, 0, 0))] * mid
        out_shape = [jax.ShapeDtypeStruct((lead, high, wide), BF16)] * mid
    else:
        out_specs = [pl.BlockSpec(five, lambda n, at: (0, n, 0, 0, 0))]
        out_shape = [jax.ShapeDtypeStruct((lead, count, mid, high, wide), BF16)]
    out = pl.pallas_call(
        body,
        grid_spec=pltpu.PrefetchScalarGridSpec(
            num_scalar_prefetch=1, grid=(count,), in_specs=specs, out_specs=out_specs
        ),
        out_shape=out_shape,
        **params(),
    )(place, keep, *crosses, *from_y, *from_z)
    return out if split else out[0]


def moments_kernel(core, weight, first, second, mine, other, grid, state_spec, grad_specs, owner, axis):
    block = state_spec.block_shape
    count = len(mine)

    def body(c_ref, w_ref, m_ref, v_ref, *refs):
        mine_refs, other_refs = refs[:count], refs[count : 2 * count]
        new_m_ref, new_v_ref, u_ref, sum_ref = refs[2 * count :]
        totals = [jnp.zeros((8, LANES), F32)] * 2
        start = 0
        ours = owner(pl.program_id(0)) == c_ref[0]
        for mine_ref, other_ref in zip(mine_refs, other_refs):
            size = mine_ref.size // block[1 - axis]
            shape = (size, block[1]) if axis == 0 else (block[0], size)
            at = (slice(start, start + size), slice(None))
            at = at if axis == 0 else at[::-1]
            grad = jnp.where(ours, mine_ref[...].reshape(shape), other_ref[...].reshape(shape)).astype(F32)
            weight = w_ref[at]
            new_m, new_v, update = moments(weight, m_ref[at], v_ref[at], grad)
            new_m_ref[at] = new_m
            new_v_ref[at] = new_v
            u_ref[at] = update
            for n, value in enumerate((weight, update)):
                square = value * value
                for col in range(0, shape[1], LANES):
                    totals[n] = totals[n] + square[:, col : col + LANES].reshape(-1, 8, LANES).sum(0)
            start += size

        @pl.when(pl.program_id(0) == 0)
        def _():
            sum_ref[...] = jnp.zeros_like(sum_ref)

        sum_ref[:8] += totals[0]
        sum_ref[8:] += totals[1]

    state = jax.ShapeDtypeStruct(weight.shape, F32)
    return pl.pallas_call(
        body,
        grid_spec=pltpu.PrefetchScalarGridSpec(
            num_scalar_prefetch=1,
            grid=grid,
            in_specs=[state_spec] * 3 + grad_specs * 2,
            out_specs=[state_spec] * 3 + [pl.BlockSpec((16, LANES), lambda n, c: (0, 0))],
        ),
        out_shape=[state] * 3 + [jax.ShapeDtypeStruct((16, LANES), F32)],
        **params(),
    )(core, weight, first, second, *mine, *other)


def step_weights(weight, update, tiles):
    rows, cols = weight.shape
    high = rows // 5
    count = len(tiles)

    def body(w_ref, u_ref, *refs):
        sums = sum(ref[...] for ref in refs[:count])
        ratio = jnp.sqrt(jnp.sum(sums[:8], keepdims=True)) / jnp.sqrt(jnp.sum(sums[8:], keepdims=True))
        refs[count][...] = w_ref[...] - 0.4 * ratio * u_ref[...]

    spec = pl.BlockSpec((high, cols), lambda n: (n, 0))
    tile = pl.BlockSpec((16, LANES), lambda n: (0, 0))
    return pl.pallas_call(
        body,
        grid=(rows // high,),
        in_specs=[spec] * 2 + [tile] * count,
        out_specs=spec,
        out_shape=jax.ShapeDtypeStruct(weight.shape, F32),
        **params(),
    )(weight, update, *tiles)


class Order:
    def __init__(self):
        self.last = None

    def after(self, *values):
        if self.last is None:
            return values
        return lax.optimization_barrier((*values, self.last))[:-1]

    def did(self, value):
        self.last = value


def plan(nz, nx, ny):
    def along_x(value, step):
        pairs = [
            (z * nx + x, z * nx + (x + step) % nx) for z in range(nz) for x in range(nx)
        ]
        return lax.ppermute(value, "gx", pairs)

    def along_z(value, flip):
        pairs = [(z * nx + x, (z ^ flip) * nx + x) for z in range(nz) for x in range(nx)]
        return lax.ppermute(value, "gx", pairs)

    def along_y(value, step):
        pairs = [
            (y * CORES + c, (y + step) % ny * CORES + c) for y in range(ny) for c in range(CORES)
        ]
        return lax.ppermute(value, "gy", pairs)

    def across(value):
        pairs = [(k, k ^ 1) for k in range(ny * CORES)]
        return lax.ppermute(value, "gy", pairs)

    class Reduce:
        def __init__(self, order, at, sends, keep, shape):
            self.order, self.at, self.place = order, at, jnp.stack(at).astype(jnp.int32)
            self.keep = keep.reshape(shape)
            each = len(sends) // shape[0]
            self.crosses = [
                across(send).reshape(shape[1] // each, *shape[2:]) for send in sends
            ]
            self.from_y = []
            self.from_z = []

        def step(self, shift, stage, split=False):
            got = self.order.after(self.keep, *self.crosses, *self.from_y, *self.from_z)
            lead = 1 + len(self.crosses)
            count = lead + len(self.from_y)
            out = reduce_step(
                self.place, got[0], got[1:lead], got[lead:count], got[count:], shift, stage, ny, split
            )
            self.order.did(out[0] if split else out)
            return out

        def send_y(self):
            from_y = []
            for s in range(1, ny):
                from_y.append(along_y(self.step(s, "y"), s))
            self.from_y = from_y

        def send_z(self):
            bit = len(self.from_z)
            self.from_z.append(along_z(self.step(0, "z"), 1 << bit))

        def finish(self):
            out = self.step(0, "end", True)
            self.held = [out[0]] + [along_x(out[s], s) for s in range(1, len(out))]
            if len(out) == 1:
                self.share_y(out[0])

        def share_y(self, value):
            self.held = [value] + [along_y(value, s) for s in range(1, ny)]

        def stacked(self, place, size, inner=False):
            places = jnp.stack([(place - s) % size for s in range(size)]).astype(jnp.int32)
            value = stack(self.order.after(*self.held), places, inner)
            self.order.did(value)
            return value

        def stack_x(self):
            self.share_y(self.stacked(self.at[0], nx))

        def stack_y(self, inner=False):
            value = self.stacked(self.at[1], ny, inner)
            self.held = [value, across(value)]

    def local(inputs, hidden_pre, cotangent, w_in, m_in, v_in, w_out, m_out, v_out):
        model = inputs.shape[1]
        hidden_width = hidden_pre.shape[1]
        shard = hidden_width // (nz * nx)
        rows = model // (nz * nx)
        cuts = widths(shard)
        chunks = range(len(cuts))
        last = len(cuts) - 1
        starts = [sum(cuts[:k]) for k in chunks]
        scale_in = 1.0 / math.sqrt(model)
        scale_out = 1.0 / math.sqrt(hidden_width)
        place = lax.axis_index("gx")
        side = lax.axis_index("gy")
        z, x = place // nx, place % nx
        y, c = side // CORES, side % CORES
        core = jnp.reshape(c, (1,)).astype(jnp.int32)
        order = Order()

        packs, hiddens = [], []
        for t in range(1, nx):
            sent = pack(*order.after(hidden_pre, cotangent), (x + t) % nx, nz, nx, cuts)
            order.did(sent[0])
            packs.append(along_x(sent[0], t))
            hiddens.append([along_x(value, t) for value in sent[1:]])

        part = half_rows(*order.after(w_out), core)
        order.did(part)
        flipped = transposed(*order.after(inputs))
        order.did(flipped)
        columns = [flipped] + [along_x(flipped, t) for t in range(1, nx)]
        own = pack(*order.after(hidden_pre, cotangent), x, nz, nx, cuts)
        order.did(own[0])
        found = {0: part, nz // 2: along_z(part, nz // 2)}
        bit = nz // 4
        while bit:
            for key in list(found):
                value = found[key]
                if key:
                    (value,) = order.after(value)
                found[key ^ bit] = along_z(value, bit)
            bit //= 2
        crossed = [across(found[key]) for key in range(nz)]
        packs = [own[0]] + packs
        hiddens = [own[1:]] + hiddens

        outs = [None for _ in chunks]
        ins = [None for _ in chunks]
        pres = [None for _ in chunks]

        def stack_weights():
            pieces = order.after(*[found[key] for key in range(nz)], *crossed)
            blocks = jnp.stack([z ^ key for key in range(nz)] * CORES)
            halves = jnp.stack([c] * nz + [1 - c] * nz)
            value = stack_rows(pieces, jnp.stack([blocks, halves]).astype(jnp.int32))
            order.did(value)
            return value

        def tokens(k, *more):
            later = [] if k == 0 else [value[k - 1] for value in hiddens]
            got = order.after(*packs, *later, *more)
            count = nx + len(later)
            blocks = Tokens(got[:nx], got[nx:count] if later else None, model, nz, cuts[k])
            return blocks, got[count:]

        def start_out(k):
            *sends, keep = grad_out_chunk(tokens(k)[0], core, nz, scale_out)
            order.did(keep)
            shape = (PARTS, nz, 1, ny, cuts[k] // PARTS // ny, model // CORES)
            outs[k] = Reduce(order, (x, y, z), sends, keep, shape)

        def start_pre(k):
            blocks, got = tokens(k, weights)
            pres[k] = grad_pre_chunk(blocks, got[0], starts[k], scale_out)
            order.did(pres[k])

        def start_in(k):
            got = order.after(pres[k], *columns)
            *sends, keep = grad_in_chunk(got[0], got[1:], core, scale_in, PARTS if k else 1)
            order.did(keep)
            shape = (nz // CORES, nz, nx, ny, rows // ny, cuts[k])
            ins[k] = Reduce(order, (x, y, z), sends, keep, shape)

        def sums(tile, zs=None):
            zs = zs or [along_z(tile, flip) for flip in range(1, nz)]
            tiles = order.after(tile, *zs)
            tile = add_tiles(tiles)
            order.did(tile)
            return [tile] + [along_x(tile, s) for s in range(1, nx)]

        def new_weights(weight, update, tiles):
            got = order.after(weight, update, *tiles)
            value = step_weights(got[0], got[1], got[2:])
            order.did(value)
            return value

        start_out(0)
        outs[0].send_y()
        weights = stack_weights()
        start_pre(0)
        outs[0].send_z()
        start_in(0)
        ins[0].send_y()
        outs[0].send_z()
        if last:
            ins[0].send_z()
            start_out(1)
            outs[1].send_y()
            outs[0].finish()
            start_pre(1)
            ins[0].send_z()
            start_in(1)
            ins[1].send_y()
            ins[0].finish()
            outs[1].send_z()
            ins[0].stack_x()
            outs[0].stack_y(True)
            outs[1].send_z()
            ins[0].stack_y()
            outs[1].finish()
            ins[1].send_z()
            outs[1].stack_y(True)
            ins[1].send_z()
        else:
            outs[0].finish()
            ins[0].send_z()
            ins[0].send_z()
            outs[0].stack_y(True)

        half = model // CORES
        got = order.after(
            w_out, m_out, v_out, *[outs[k].held[0] for k in chunks], *[outs[k].held[1] for k in chunks]
        )
        first_out, second_out, update_out, tile = moments_kernel(
            core,
            *got[:3],
            got[3 : 4 + last],
            got[4 + last :],
            (CORES,),
            pl.BlockSpec((shard, half), lambda n, c: (0, n)),
            [
                pl.BlockSpec((PARTS, ny, w // PARTS // ny, half), lambda n, c: (0, 0, 0, 0)) for w in cuts
            ],
            lambda n: n,
            0,
        )
        order.did(tile)
        ins[last].finish()
        tiles = sums(tile)
        ins[last].stack_x()
        ins[last].stack_y()

        got = order.after(
            w_in, m_in, v_in, *[ins[k].held[0] for k in chunks], *[ins[k].held[1] for k in chunks]
        )
        mine, other = got[3 : 4 + last], got[4 + last :]
        if shard % LANES:
            joined = [
                jnp.stack([jnp.where(c == 0, a, b), jnp.where(c == 0, b, a)]) for a, b in zip(mine, other)
            ]
            grad = jnp.concatenate(joined, axis=-1).transpose(1, 4, 0, 3, 2, 5)
            grad = grad.reshape(rows, hidden_width).astype(F32)
            first_in, second_in, update_in = moments(*got[:3], grad)
            tile = jnp.concatenate(
                [
                    jnp.sum((value * value).reshape(-1, 8, LANES), axis=0)
                    for value in (w_in, update_in)
                ]
            )
        else:
            zs = nz // CORES
            first_in, second_in, update_in, tile = moments_kernel(
                core,
                *got[:3],
                mine,
                other,
                (nz * nx,),
                pl.BlockSpec((rows, shard), lambda n, c: (0, n)),
                [
                    pl.BlockSpec(
                        (ny, 1, 1, rows // ny, w), lambda n, c: (0, n % nx, n // nx % zs, 0, 0)
                    )
                    for w in cuts
                ],
                lambda n: n // nx // zs,
                1,
            )
        order.did(tile)
        zs = [along_z(tile, flip) for flip in range(1, nz)]
        new_w_out = new_weights(w_out, update_out, tiles)
        new_w_in = new_weights(w_in, update_in, sums(tile, zs))
        return (new_w_in, first_in, second_in, new_w_out, first_out, second_out)

    return local


def solution(mesh):
    gx, gy = mesh.shape["gx"], mesh.shape["gy"]
    nz = CHIPS_Z
    state = P("gx", None)
    tokens = P(("gx", "gy"), None)
    return jax.shard_map(
        plan(nz, gx // nz, gy // CORES),
        mesh=mesh,
        in_specs=(tokens,) * 3 + (state,) * 6,
        out_specs=(state,) * 6,
        check_vma=False,
    )
```

```python
import functools
import math

import jax
import jax.numpy as jnp
from jax import lax
from jax.experimental import pallas as pl
from jax.experimental.pallas import tpu as pltpu
from jax.sharding import PartitionSpec as P

BF16 = jnp.bfloat16
F32 = jnp.float32
CORES = 2
CHIPS_Z = 4
LANES = 128
PARTS = 2
VMEM = 24 * 1024 * 1024
WIDE = 56 * 1024 * 1024


def moments(weight, first, second, grad):
    new_first = 0.9 * first + 0.1 * grad
    new_second = 0.95 * second + 0.05 * grad * grad
    update = new_first / (jnp.sqrt(new_second) + 1e-06) + 0.05 * weight
    return (new_first, new_second, update)


def squares(value):
    return jnp.sum(value * value)


def gelu(value):
    return 0.5 * value * (1.0 + lax.erf(value * (1.0 / math.sqrt(2.0))))


def gelu_slope(value):
    cdf = 0.5 * (1.0 + lax.erf(value * (1.0 / math.sqrt(2.0))))
    return cdf + value * (jnp.exp(-0.5 * value * value) * (1.0 / math.sqrt(2.0 * math.pi)))


def widths(shard):
    if shard % LANES:
        return (shard,)
    first = shard // LANES * 2 // 5 * LANES
    return (first, shard - first)


def dot(left, right, dims):
    return lax.dot_general(left, right, (dims, ((), ())), preferred_element_type=F32)


def params(grant=VMEM):
    return dict(
        compiler_params=pltpu.CompilerParams(vmem_limit_bytes=grant),
        cost_estimate=pl.CostEstimate(flops=1, bytes_accessed=1, transcendentals=0),
    )


def pack(hidden, cotangent, at, nz, nx, cuts):
    tokens, hidden_width = hidden.shape
    model = cotangent.shape[1]
    shard = hidden_width // (nz * nx)
    first = cuts[0]
    if shard % LANES:
        parts = [
            lax.dynamic_slice_in_dim(hidden, (z * nx + at) * shard, shard, 1).T for z in range(nz)
        ]
        return [jnp.concatenate([cotangent.T, *parts])]

    def body(at_ref, h_ref, cot_ref, out_ref, *later_refs):
        z = pl.program_id(0)

        @pl.when(z == 0)
        def _():
            out_ref[:model] = cot_ref[...].T

        out_ref[pl.ds(pl.multiple_of(model + z * first, LANES), first)] = h_ref[:, :first].T
        start = first
        for width, later_ref in zip(cuts[1:], later_refs):
            later_ref[0] = h_ref[:, start : start + width].T
            start += width

    total = model + nz * first
    return pl.pallas_call(
        body,
        grid_spec=pltpu.PrefetchScalarGridSpec(
            num_scalar_prefetch=1,
            grid=(nz,),
            in_specs=[
                pl.BlockSpec((tokens, shard), lambda z, a: (0, z * nx + a[0])),
                pl.BlockSpec((tokens, model), lambda z, a: (0, 0)),
            ],
            out_specs=[pl.BlockSpec((total, tokens), lambda z, a: (0, 0))]
            + [pl.BlockSpec((1, w, tokens), lambda z, a: (z, 0, 0)) for w in cuts[1:]],
        ),
        out_shape=[jax.ShapeDtypeStruct((total, tokens), BF16)]
        + [jax.ShapeDtypeStruct((nz, w, tokens), BF16) for w in cuts[1:]],
        **params(),
    )(jnp.reshape(at, (1,)).astype(jnp.int32), hidden, cotangent)


class Tokens:
    def __init__(self, packs, hiddens, model, nz, width):
        tokens = packs[0].shape[1]
        self.model, self.width, self.count = model, width, len(packs)
        if hiddens is None:
            self.arrays = list(packs)
            self.specs = [pl.BlockSpec(packs[0].shape, lambda z, c: (0, 0))] * len(packs)
        else:
            self.arrays = [*packs, *hiddens]
            self.specs = [pl.BlockSpec((model, tokens), lambda z, c: (0, 0))] * len(packs)
            self.specs += [pl.BlockSpec((1, width, tokens), lambda z, c: (z, 0, 0))] * len(packs)

    def cot(self, refs, n):
        return refs[n].at[: self.model]

    def hidden(self, refs, n):
        if len(refs) == self.count:
            row = self.model + pl.program_id(0) * self.width
            return refs[n][pl.ds(pl.multiple_of(row, 16), self.width)].astype(F32)
        return refs[self.count + n][0].astype(F32)


def grad_out_chunk(tokens, core, nz, scale, parts):
    width, model = tokens.width, tokens.model
    half = model // CORES
    high = width // parts
    count = len(tokens.arrays)

    def body(c_ref, *refs):
        ins, outs = refs[:count], refs[count:]
        acts = jnp.concatenate(
            [gelu(tokens.hidden(ins, n)).astype(BF16) for n in range(tokens.count)], axis=1
        )
        for which in range(2):
            cols = pl.ds(pl.multiple_of((c_ref[0] + 1 + which) % CORES * half, 16), half)
            right = jnp.concatenate([tokens.cot(ins, n)[cols, :] for n in range(tokens.count)], axis=1)
            total = (dot(acts, right, ((1,), (1,))) * scale).astype(BF16)
            for p in range(parts):
                value = total[p * high : (p + 1) * high]
                if which:
                    outs[parts][p, 0] = value
                else:
                    outs[p][0] = value

    return pl.pallas_call(
        body,
        grid_spec=pltpu.PrefetchScalarGridSpec(
            num_scalar_prefetch=1,
            grid=(nz,),
            in_specs=tokens.specs,
            out_specs=[pl.BlockSpec((1, high, half), lambda z, c: (z, 0, 0))] * parts
            + [pl.BlockSpec((parts, 1, high, half), lambda z, c: (0, z, 0, 0))],
        ),
        out_shape=[jax.ShapeDtypeStruct((nz, high, half), BF16)] * parts
        + [jax.ShapeDtypeStruct((parts, nz, high, half), BF16)],
        **params(),
    )(core, *tokens.arrays)


def grad_pre_chunk(tokens, mine, other, nz, row, core, scale):
    part, model = mine[0].shape
    width = tokens.width
    count = len(tokens.arrays)
    long = tokens.arrays[0].shape[1]

    def body(c_ref, *refs):
        ins = refs[:count]
        out_ref, w_ref = refs[count + 2 * nz :]
        for h in range(nz):

            @pl.when((pl.program_id(0) ^ c_ref[1]) == h)
            def _(h=h):
                for at, ref in ((c_ref[0], refs[count + h]), (1 - c_ref[0], refs[count + nz + h])):
                    w_ref[pl.ds(pl.multiple_of(at * part, 16), part), :] = ref[...]

        w = w_ref[row : row + width, :]
        for n in range(tokens.count):
            grad_act = dot(w, tokens.cot(ins, n)[...], ((1,), (0,))) * scale
            out_ref[0, :, n * long : (n + 1) * long] = (
                grad_act * gelu_slope(tokens.hidden(ins, n))
            ).astype(BF16)

    w_specs = [pl.BlockSpec((part, model), lambda z, c: (0, 0))] * nz
    return pl.pallas_call(
        body,
        grid_spec=pltpu.PrefetchScalarGridSpec(
            num_scalar_prefetch=1,
            grid=(nz,),
            in_specs=tokens.specs + w_specs * 2,
            out_specs=pl.BlockSpec((1, width, tokens.count * long), lambda z, c: (z, 0, 0)),
            scratch_shapes=[pltpu.VMEM((CORES * part, model), BF16)],
        ),
        out_shape=jax.ShapeDtypeStruct((nz, width, tokens.count * long), BF16),
        **params(),
    )(core, *tokens.arrays, *mine, *other)


def grad_in_chunk(grads, inputs, core, scale, cut, block, width):
    nz, _, long = grads.shape
    model, tokens = inputs[0].shape
    count = len(inputs)
    half = nz // CORES
    high = model // cut

    def body(c_ref, g_ref, *refs):
        in_refs, outs = refs[:count], refs[count:]
        left = jnp.concatenate([i[...] for i in in_refs], axis=1)
        total = (dot(left, g_ref[0], ((1,), (1,))) * scale).astype(BF16)
        step = pl.program_id(0)
        for n in range(half):

            @pl.when(step == n)
            def _(n=n):
                for h in range(cut):
                    outs[n * cut + h][...] = total[h * high : (h + 1) * high]

        @pl.when(step >= half)
        def _():
            outs[-1][0] = total

    return pl.pallas_call(
        body,
        grid_spec=pltpu.PrefetchScalarGridSpec(
            num_scalar_prefetch=1,
            grid=(nz,),
            in_specs=[
                pl.BlockSpec(
                    (1, width, long),
                    lambda z, c: ((c[0] + 1 + z // half) % CORES * half + z % half, block, 0),
                )
            ]
            + [pl.BlockSpec((model, tokens), lambda z, c: (0, 0))] * count,
            out_specs=[pl.BlockSpec((high, width), lambda z, c: (0, 0))] * (half * cut)
            + [pl.BlockSpec((1, model, width), lambda z, c: (jnp.maximum(z - half, 0), 0, 0))],
        ),
        out_shape=[jax.ShapeDtypeStruct((high, width), BF16)] * (half * cut)
        + [jax.ShapeDtypeStruct((half, model, width), BF16)],
        **params(),
    )(core, grads, *inputs)


def transposed(value):
    rows, cols = value.shape
    wide = 2 * LANES

    def body(in_ref, out_ref):
        out_ref[...] = in_ref[...].T

    return pl.pallas_call(
        body,
        grid=(cols // wide,),
        in_specs=[pl.BlockSpec((rows, wide), lambda n: (0, n))],
        out_specs=pl.BlockSpec((wide, rows), lambda n: (n, 0)),
        out_shape=jax.ShapeDtypeStruct((cols, rows), value.dtype),
        **params(),
    )(value)


def half_rows(weight, core):
    rows, cols = weight.shape
    high = rows // CORES // 2

    def body(c_ref, in_ref, out_ref):
        out_ref[...] = in_ref[...].astype(BF16)

    return pl.pallas_call(
        body,
        grid_spec=pltpu.PrefetchScalarGridSpec(
            num_scalar_prefetch=1,
            grid=(2,),
            in_specs=[pl.BlockSpec((high, cols), lambda n, c: (c[0] * 2 + n, 0))],
            out_specs=pl.BlockSpec((high, cols), lambda n, c: (n, 0)),
        ),
        out_shape=jax.ShapeDtypeStruct((2 * high, cols), BF16),
        **params(WIDE),
    )(core, weight)


def stack(pieces, places, inner=False):
    count = len(pieces)
    shape = pieces[0].shape
    out = (shape[0], count, *shape[1:]) if inner else (count, *shape)

    def body(at_ref, *refs):
        for n in range(count):
            if inner:
                for p in range(shape[0]):
                    refs[count][p, at_ref[n]] = refs[n][p]
            else:
                refs[count][at_ref[n]] = refs[n][...]

    return pl.pallas_call(
        body,
        grid_spec=pltpu.PrefetchScalarGridSpec(
            num_scalar_prefetch=1,
            grid=(),
            in_specs=[pl.BlockSpec(shape, lambda at: (0,) * len(shape))] * count,
            out_specs=pl.BlockSpec(out, lambda at: (0,) * len(out)),
        ),
        out_shape=jax.ShapeDtypeStruct(out, pieces[0].dtype),
        **params(),
    )(places, *pieces)


def add_tiles(tiles):
    def body(*refs):
        refs[-1][...] = sum(ref[...] for ref in refs[:-1])

    return pl.pallas_call(
        body, out_shape=jax.ShapeDtypeStruct(tiles[0].shape, F32), **params()
    )(*tiles)


def reduce_step(place, keep, crosses, from_y, from_z, shift, stage, ny, split):
    lead, nz, mid, _, high, wide = keep.shape
    bit = len(from_z)

    def zed(n, at):
        if stage == "y":
            return n
        if stage == "end":
            return at[2]
        low = at[2] % (1 << bit)
        mine = (at[2] // (1 << bit)) % 2
        return n * (2 << bit) + (1 - mine) * (1 << bit) + low

    count = {"y": nz, "z": nz >> (bit + 1), "end": 1}[stage]
    six = (lead, 1, mid, 1, high, wide)
    five = (lead, 1, mid, high, wide)
    specs = [pl.BlockSpec(six, lambda n, at: (0, zed(n, at), 0, (at[1] + shift) % ny, 0, 0))]
    each = len(crosses) // lead
    long = nz // each
    for h in range(len(crosses)):
        specs.append(
            pl.BlockSpec(
                six[1:],
                lambda n, at, h=h % each: (
                    jnp.clip(zed(n, at) - h * long, 0, long - 1),
                    0,
                    (at[1] + shift) % ny,
                    0,
                    0,
                ),
            )
        )
    specs += [pl.BlockSpec(five, lambda n, at: (0, zed(n, at), 0, 0, 0))] * len(from_y)
    specs += [
        pl.BlockSpec(five, lambda n, at, j=j: (0, zed(n, at) // (2 << j), 0, 0, 0)) for j in range(bit)
    ]

    def body(at_ref, *refs):
        ins = refs[: len(specs)]
        outs = refs[len(specs) :]
        for p in range(lead):
            for m in range(mid):
                total = ins[1 + p * each][0, m, 0]
                for h in range(1, each):
                    total = jnp.where(
                        zed(pl.program_id(0), at_ref) >= h * long, ins[1 + p * each + h][0, m, 0], total
                    )
                total = total.astype(F32) + ins[0][p, 0, m, 0].astype(F32)
                for ref in ins[1 + len(crosses) :]:
                    total = total + ref[p, 0, m].astype(F32)
                total = total.astype(BF16)
                if not split:
                    outs[0][p, 0, m] = total
                    continue
                for s in range(mid):

                    @pl.when((at_ref[0] + s) % mid == m)
                    def _(s=s, total=total):
                        outs[s][p] = total

    if split:
        out_specs = [pl.BlockSpec((lead, high, wide), lambda n, at: (0, 0, 0))] * mid
        out_shape = [jax.ShapeDtypeStruct((lead, high, wide), BF16)] * mid
    else:
        out_specs = [pl.BlockSpec(five, lambda n, at: (0, n, 0, 0, 0))]
        out_shape = [jax.ShapeDtypeStruct((lead, count, mid, high, wide), BF16)]
    out = pl.pallas_call(
        body,
        grid_spec=pltpu.PrefetchScalarGridSpec(
            num_scalar_prefetch=1, grid=(count,), in_specs=specs, out_specs=out_specs
        ),
        out_shape=out_shape,
        **params(),
    )(place, keep, *crosses, *from_y, *from_z)
    return out if split else out[0]


def moments_kernel(core, weight, first, second, mine, other, grid, state_spec, grad_specs, owner, axis, tiles):
    block = state_spec.block_shape
    count = len(mine)
    long = 16 * (1 + len(tiles))

    def body(c_ref, w_ref, m_ref, v_ref, *refs):
        mine_refs, other_refs = refs[:count], refs[count : 2 * count]
        tile_refs = refs[2 * count : 2 * count + len(tiles)]
        new_m_ref, new_v_ref, u_ref, sum_ref = refs[2 * count + len(tiles) :]
        totals = [jnp.zeros((8, LANES), F32)] * 2
        start = 0
        ours = owner(pl.program_id(0)) == c_ref[0]
        for mine_ref, other_ref in zip(mine_refs, other_refs):
            size = mine_ref.size // block[1 - axis]
            shape = (size, block[1]) if axis == 0 else (block[0], size)
            at = (slice(start, start + size), slice(None))
            at = at if axis == 0 else at[::-1]
            grad = jnp.where(ours, mine_ref[...].reshape(shape), other_ref[...].reshape(shape)).astype(F32)
            weight = w_ref[at]
            new_m, new_v, update = moments(weight, m_ref[at], v_ref[at], grad)
            new_m_ref[at] = new_m
            new_v_ref[at] = new_v
            u_ref[at] = update
            for n, value in enumerate((weight, update)):
                square = value * value
                for col in range(0, shape[1], LANES):
                    totals[n] = totals[n] + square[:, col : col + LANES].reshape(-1, 8, LANES).sum(0)
            start += size

        @pl.when(pl.program_id(0) == 0)
        def _():
            sum_ref[:16] = jnp.zeros((16, LANES), F32)
            for n, tile_ref in enumerate(tile_refs):
                sum_ref[16 * (n + 1) : 16 * (n + 2)] = tile_ref[...]

        sum_ref[:8] += totals[0]
        sum_ref[8:16] += totals[1]

    state = jax.ShapeDtypeStruct(weight.shape, F32)
    return pl.pallas_call(
        body,
        grid_spec=pltpu.PrefetchScalarGridSpec(
            num_scalar_prefetch=1,
            grid=grid,
            in_specs=[state_spec] * 3
            + grad_specs * 2
            + [pl.BlockSpec((16, LANES), lambda n, c: (0, 0))] * len(tiles),
            out_specs=[state_spec] * 3 + [pl.BlockSpec((long, LANES), lambda n, c: (0, 0))],
        ),
        out_shape=[state] * 3 + [jax.ShapeDtypeStruct((long, LANES), F32)],
        **params(),
    )(core, weight, first, second, *mine, *other, *tiles)


def step_weights(weight, update, tiles, at):
    rows, cols = weight.shape
    high = rows // 5
    count = len(tiles)

    def body(w_ref, u_ref, *refs):
        sums = sum(ref[at : at + 16] for ref in refs[:count])
        ratio = jnp.sqrt(jnp.sum(sums[:8], keepdims=True)) / jnp.sqrt(jnp.sum(sums[8:], keepdims=True))
        refs[count][...] = w_ref[...] - 0.4 * ratio * u_ref[...]

    spec = pl.BlockSpec((high, cols), lambda n: (n, 0))
    tile = pl.BlockSpec(tiles[0].shape, lambda n: (0, 0))
    return pl.pallas_call(
        body,
        grid=(rows // high,),
        in_specs=[spec] * 2 + [tile] * count,
        out_specs=spec,
        out_shape=jax.ShapeDtypeStruct(weight.shape, F32),
        **params(),
    )(weight, update, *tiles)


class Order:
    def __init__(self):
        self.last = None

    def after(self, *values):
        if self.last is None:
            return values
        return lax.optimization_barrier((*values, self.last))[:-1]

    def did(self, value):
        self.last = value


def plan(nz, nx, ny):
    def along_x(value, step):
        pairs = [
            (z * nx + x, z * nx + (x + step) % nx) for z in range(nz) for x in range(nx)
        ]
        return lax.ppermute(value, "gx", pairs)

    def along_z(value, flip):
        pairs = [(z * nx + x, (z ^ flip) * nx + x) for z in range(nz) for x in range(nx)]
        return lax.ppermute(value, "gx", pairs)

    def along_y(value, step):
        pairs = [
            (y * CORES + c, (y + step) % ny * CORES + c) for y in range(ny) for c in range(CORES)
        ]
        return lax.ppermute(value, "gy", pairs)

    def across(value):
        pairs = [(k, k ^ 1) for k in range(ny * CORES)]
        return lax.ppermute(value, "gy", pairs)

    class Reduce:
        def __init__(self, order, at, sends, keep, shape):
            self.order, self.at, self.place = order, at, jnp.stack(at).astype(jnp.int32)
            self.keep = keep.reshape(shape)
            each = len(sends) // shape[0]
            self.crosses = [
                across(send).reshape(shape[1] // each, *shape[2:]) for send in sends
            ]
            self.from_y = []
            self.from_z = []

        def step(self, shift, stage, split=False):
            got = self.order.after(self.keep, *self.crosses, *self.from_y, *self.from_z)
            lead = 1 + len(self.crosses)
            count = lead + len(self.from_y)
            out = reduce_step(
                self.place, got[0], got[1:lead], got[lead:count], got[count:], shift, stage, ny, split
            )
            self.order.did(out[0] if split else out)
            return out

        def send_y(self):
            from_y = []
            for s in range(1, ny):
                from_y.append(along_y(self.step(s, "y"), s))
            self.from_y = from_y

        def send_z(self):
            bit = len(self.from_z)
            self.from_z.append(along_z(self.step(0, "z"), 1 << bit))

        def finish(self):
            out = self.step(0, "end", True)
            self.held = [out[0]] + [along_x(out[s], s) for s in range(1, len(out))]
            if len(out) == 1:
                self.share_y(out[0])

        def share_y(self, value):
            self.held = [value] + [along_y(value, s) for s in range(1, ny)]

        def stacked(self, place, size, inner=False):
            places = jnp.stack([(place - s) % size for s in range(size)]).astype(jnp.int32)
            value = stack(self.order.after(*self.held), places, inner)
            self.order.did(value)
            return value

        def stack_x(self):
            self.share_y(self.stacked(self.at[0], nx))

        def stack_y(self, inner=False):
            value = self.stacked(self.at[1], ny, inner)
            self.held = [value, across(value)]

    def local(inputs, hidden_pre, cotangent, w_in, m_in, v_in, w_out, m_out, v_out):
        model = inputs.shape[1]
        hidden_width = hidden_pre.shape[1]
        shard = hidden_width // (nz * nx)
        rows = model // (nz * nx)
        cuts = widths(shard)
        chunks = range(len(cuts))
        last = len(cuts) - 1
        starts = [sum(cuts[:k]) for k in chunks]
        scale_in = 1.0 / math.sqrt(model)
        scale_out = 1.0 / math.sqrt(hidden_width)
        place = lax.axis_index("gx")
        side = lax.axis_index("gy")
        z, x = place // nx, place % nx
        y, c = side // CORES, side % CORES
        core = jnp.reshape(c, (1,)).astype(jnp.int32)
        at_core = jnp.stack([c, z]).astype(jnp.int32)
        order = Order()

        packs, hiddens = [], []
        for t in range(1, nx):
            sent = pack(*order.after(hidden_pre, cotangent), (x + t) % nx, nz, nx, cuts)
            order.did(sent[0])
            packs.append(along_x(sent[0], t))
            hiddens.append([along_x(value, t) for value in sent[1:]])

        part = half_rows(*order.after(w_out), core)
        order.did(part)
        flipped = transposed(*order.after(inputs))
        order.did(flipped)
        columns = [flipped] + [along_x(flipped, t) for t in range(1, nx)]
        own = pack(*order.after(hidden_pre, cotangent), x, nz, nx, cuts)
        order.did(own[0])
        found = {0: part, nz // 2: along_z(part, nz // 2)}
        bit = nz // 4
        while bit:
            for key in list(found):
                value = found[key]
                if key:
                    (value,) = order.after(value)
                found[key ^ bit] = along_z(value, bit)
            bit //= 2
        found = [found[key] for key in range(nz)]
        crossed = [across(value) for value in [*order.after(*found[: nz // 2]), *found[nz // 2 :]]]
        packs = [own[0]] + packs
        hiddens = [own[1:]] + hiddens

        parts = [1] + [PARTS] * last
        outs = [None for _ in chunks]
        pieces_in = [(0, 0, cuts[0])]
        if last:
            small = cuts[1] // 3
            pieces_in += [(1, 0, 2 * small), (1, 2, small)]
        ins = [None for _ in pieces_in]
        pres = [None for _ in chunks]

        def tokens(k, *more):
            later = [] if k == 0 else [value[k - 1] for value in hiddens]
            got = order.after(*packs, *later, *more)
            count = nx + len(later)
            blocks = Tokens(got[:nx], got[nx:count] if later else None, model, nz, cuts[k])
            return blocks, got[count:]

        def start_out(k):
            blocks, _ = tokens(k, *([*crossed[: nz // 2], found[nz // 2]] if k == 0 else []))
            *sends, keep = grad_out_chunk(blocks, core, nz, scale_out, parts[k])
            order.did(keep)
            shape = (parts[k], nz, 1, ny, cuts[k] // parts[k] // ny, model // CORES)
            outs[k] = Reduce(order, (x, y, z), sends, keep, shape)

        def start_pre(k):
            blocks, got = tokens(k, *found, *crossed)
            pres[k] = grad_pre_chunk(blocks, got[:nz], got[nz:], nz, starts[k], at_core, scale_out)
            order.did(pres[k])

        def start_in(k):
            chunk, block, width = pieces_in[k]
            got = order.after(pres[chunk], *columns)
            *sends, keep = grad_in_chunk(
                got[0], got[1:], core, scale_in, PARTS if width > LANES else 1, block, width
            )
            order.did(keep)
            shape = (nz // CORES, nz, nx, ny, rows // ny, width)
            ins[k] = Reduce(order, (x, y, z), sends, keep, shape)

        def sums(tile):
            tiles = order.after(tile, *[along_z(tile, flip) for flip in range(1, nz)])
            tile = add_tiles(tiles)
            order.did(tile)
            return [tile] + [along_x(tile, t) for t in range(1, nx)]

        def new_weights(weight, update, tiles, at):
            got = order.after(weight, update, *tiles)
            value = step_weights(got[0], got[1], got[2:], at)
            order.did(value)
            return value

        def moments_out():
            half = model // CORES
            got = order.after(
                w_out, m_out, v_out, *[outs[k].held[0] for k in chunks], *[outs[k].held[1] for k in chunks]
            )
            new = moments_kernel(
                core,
                *got[:3],
                got[3 : 4 + last],
                got[4 + last :],
                (CORES,),
                pl.BlockSpec((shard, half), lambda n, c: (0, n)),
                [
                    pl.BlockSpec((p, ny, w // p // ny, half), lambda n, c: (0, 0, 0, 0))
                    for w, p in zip(cuts, parts)
                ],
                lambda n: n,
                0,
                [],
            )
            order.did(new[3])
            return new

        start_out(0)
        outs[0].send_y()
        start_pre(0)
        start_in(0)
        outs[0].send_z()
        ins[0].send_y()
        outs[0].send_z()
        ins[0].send_z()
        outs[0].finish()
        if last:
            start_out(1)
            outs[1].send_y()
            start_pre(1)
            ins[0].send_z()
            start_in(1)
            start_in(2)
            ins[1].send_y()
            ins[2].send_y()
            ins[0].finish()
            outs[1].send_z()
            ins[0].stack_x()
            outs[0].stack_y(True)
            ins[1].send_z()
            outs[1].send_z()
            ins[0].stack_y()
            ins[2].send_z()
            ins[1].send_z()
            outs[1].finish()
            ins[2].send_z()
            outs[1].stack_y(True)
            ins[1].finish()
            first_out, second_out, update_out, tile = moments_out()
            ins[2].finish()
            for n in (1, 2):
                ins[n].stack_x()
            for n in (1, 2):
                ins[n].stack_y()
        else:
            ins[0].send_z()
            outs[0].stack_y(True)
            ins[0].finish()
            first_out, second_out, update_out, tile = moments_out()
            ins[0].stack_x()
            ins[0].stack_y()

        held = [value.held for value in ins]
        got = order.after(w_in, m_in, v_in, tile, *[pair[0] for pair in held], *[pair[1] for pair in held])
        mine, other = got[4 : 4 + len(ins)], got[4 + len(ins) :]
        if shard % LANES:
            joined = [
                jnp.stack([jnp.where(c == 0, a, b), jnp.where(c == 0, b, a)]) for a, b in zip(mine, other)
            ]
            grad = jnp.concatenate(joined, axis=-1).transpose(1, 4, 0, 3, 2, 5)
            grad = grad.reshape(rows, hidden_width).astype(F32)
            first_in, second_in, update_in = moments(*got[:3], grad)
            tile = jnp.concatenate(
                [
                    jnp.sum((value * value).reshape(-1, 8, LANES), axis=0)
                    for value in (w_in, update_in)
                ]
                + [got[3]]
            )
        else:
            zs = nz // CORES
            first_in, second_in, update_in, tile = moments_kernel(
                core,
                *got[:3],
                mine,
                other,
                (nz * nx,),
                pl.BlockSpec((rows, shard), lambda n, c: (0, n)),
                [
                    pl.BlockSpec(
                        (ny, 1, 1, rows // ny, w), lambda n, c: (0, n % nx, n // nx % zs, 0, 0)
                    )
                    for _, _, w in pieces_in
                ],
                lambda n: n // nx // zs,
                1,
                [got[3]],
            )
        order.did(tile)
        tiles = sums(tile)
        new_w_in = new_weights(w_in, update_in, tiles, 0)
        new_w_out = new_weights(w_out, update_out, tiles, 16)
        return (new_w_in, first_in, second_in, new_w_out, first_out, second_out)

    return local


def solution(mesh):
    gx, gy = mesh.shape["gx"], mesh.shape["gy"]
    nz = CHIPS_Z
    state = P("gx", None)
    tokens = P(("gx", "gy"), None)
    return jax.shard_map(
        plan(nz, gx // nz, gy // CORES),
        mesh=mesh,
        in_specs=(tokens,) * 3 + (state,) * 6,
        out_specs=(state,) * 6,
        check_vma=False,
    )
```

```python
import functools
import math

import jax
import jax.numpy as jnp
from jax import lax
from jax.experimental import pallas as pl
from jax.experimental.pallas import tpu as pltpu
from jax.sharding import PartitionSpec as P

BF16 = jnp.bfloat16
F32 = jnp.float32
CORES = 2
CHIPS_Z = 4
LANES = 128
PARTS = 2
VMEM = 24 * 1024 * 1024
WIDE = 56 * 1024 * 1024


def moments(weight, first, second, grad):
    new_first = 0.9 * first + 0.1 * grad
    new_second = 0.95 * second + 0.05 * grad * grad
    update = new_first / (jnp.sqrt(new_second) + 1e-06) + 0.05 * weight
    return (new_first, new_second, update)


def squares(value):
    return jnp.sum(value * value)


def gelu(value):
    return 0.5 * value * (1.0 + lax.erf(value * (1.0 / math.sqrt(2.0))))


def gelu_slope(value):
    cdf = 0.5 * (1.0 + lax.erf(value * (1.0 / math.sqrt(2.0))))
    return cdf + value * (jnp.exp(-0.5 * value * value) * (1.0 / math.sqrt(2.0 * math.pi)))


def widths(shard):
    if shard % LANES:
        return (shard,)
    first = shard // LANES * 3 // 5 * LANES
    return (first, shard - first)


def dot(left, right, dims):
    return lax.dot_general(left, right, (dims, ((), ())), preferred_element_type=F32)


def params(grant=VMEM):
    return dict(
        compiler_params=pltpu.CompilerParams(vmem_limit_bytes=grant),
        cost_estimate=pl.CostEstimate(flops=1, bytes_accessed=1, transcendentals=0),
    )


def pack(hidden, cotangent, at, nz, nx, cuts):
    tokens, hidden_width = hidden.shape
    model = cotangent.shape[1]
    shard = hidden_width // (nz * nx)
    first = cuts[0]
    if shard % LANES:
        parts = [
            lax.dynamic_slice_in_dim(hidden, (z * nx + at) * shard, shard, 1).T for z in range(nz)
        ]
        return jnp.concatenate([cotangent.T, *parts])

    def body(at_ref, h_ref, cot_ref, out_ref):
        z = pl.program_id(0)

        @pl.when(z == 0)
        def _():
            out_ref[:model] = cot_ref[...].T

        out_ref[pl.ds(pl.multiple_of(model + z * first, LANES), first)] = h_ref[:, :first].T

    total = model + nz * first
    return pl.pallas_call(
        body,
        grid_spec=pltpu.PrefetchScalarGridSpec(
            num_scalar_prefetch=1,
            grid=(nz,),
            in_specs=[
                pl.BlockSpec((tokens, shard), lambda z, a: (0, z * nx + a[0])),
                pl.BlockSpec((tokens, model), lambda z, a: (0, 0)),
            ],
            out_specs=pl.BlockSpec((total, tokens), lambda z, a: (0, 0)),
        ),
        out_shape=jax.ShapeDtypeStruct((total, tokens), BF16),
        **params(WIDE),
    )(jnp.reshape(at, (1,)).astype(jnp.int32), hidden, cotangent)


def pack_later(hidden, at, nz, nx, cuts):
    tokens, hidden_width = hidden.shape
    shard = hidden_width // (nz * nx)
    if len(cuts) == 1:
        return []

    def body(at_ref, h_ref, *out_refs):
        start = cuts[0]
        for width, out_ref in zip(cuts[1:], out_refs):
            out_ref[0] = h_ref[:, start : start + width].T
            start += width

    return pl.pallas_call(
        body,
        grid_spec=pltpu.PrefetchScalarGridSpec(
            num_scalar_prefetch=1,
            grid=(nz,),
            in_specs=[pl.BlockSpec((tokens, shard), lambda z, a: (0, z * nx + a[0]))],
            out_specs=[pl.BlockSpec((1, w, tokens), lambda z, a: (z, 0, 0)) for w in cuts[1:]],
        ),
        out_shape=[jax.ShapeDtypeStruct((nz, w, tokens), BF16) for w in cuts[1:]],
        **params(WIDE),
    )(jnp.reshape(at, (1,)).astype(jnp.int32), hidden)


class Tokens:
    def __init__(self, packs, hiddens, model, nz, width):
        tokens = packs[0].shape[1]
        self.model, self.width, self.count = model, width, len(packs)
        if hiddens is None:
            self.arrays = list(packs)
            self.specs = [pl.BlockSpec(packs[0].shape, lambda z, c: (0, 0))] * len(packs)
        else:
            self.arrays = [*packs, *hiddens]
            self.specs = [pl.BlockSpec((model, tokens), lambda z, c: (0, 0))] * len(packs)
            self.specs += [pl.BlockSpec((1, width, tokens), lambda z, c: (z, 0, 0))] * len(packs)

    def cot(self, refs, n):
        return refs[n].at[: self.model]

    def hidden(self, refs, n):
        if len(refs) == self.count:
            row = self.model + pl.program_id(0) * self.width
            return refs[n][pl.ds(pl.multiple_of(row, 16), self.width)].astype(F32)
        return refs[self.count + n][0].astype(F32)


def grad_out_chunk(tokens, core, nz, scale, parts):
    width, model = tokens.width, tokens.model
    half = model // CORES
    high = width // parts
    count = len(tokens.arrays)

    def body(c_ref, *refs):
        ins, outs = refs[:count], refs[count:]
        acts = jnp.concatenate(
            [gelu(tokens.hidden(ins, n)).astype(BF16) for n in range(tokens.count)], axis=1
        )
        for which in range(2):
            cols = pl.ds(pl.multiple_of((c_ref[0] + 1 + which) % CORES * half, 16), half)
            right = jnp.concatenate([tokens.cot(ins, n)[cols, :] for n in range(tokens.count)], axis=1)
            total = (dot(acts, right, ((1,), (1,))) * scale).astype(BF16)
            for p in range(parts):
                value = total[p * high : (p + 1) * high]
                if which:
                    outs[parts][p, 0] = value
                else:
                    outs[p][0] = value

    return pl.pallas_call(
        body,
        grid_spec=pltpu.PrefetchScalarGridSpec(
            num_scalar_prefetch=1,
            grid=(nz,),
            in_specs=tokens.specs,
            out_specs=[pl.BlockSpec((1, high, half), lambda z, c: (z, 0, 0))] * parts
            + [pl.BlockSpec((parts, 1, high, half), lambda z, c: (0, z, 0, 0))],
        ),
        out_shape=[jax.ShapeDtypeStruct((nz, high, half), BF16)] * parts
        + [jax.ShapeDtypeStruct((parts, nz, high, half), BF16)],
        **params(),
    )(core, *tokens.arrays)


def grad_pre_chunk(tokens, mine, other, nz, row, core, scale):
    part, model = mine[0].shape
    width = tokens.width
    count = len(tokens.arrays)
    long = tokens.arrays[0].shape[1]

    def body(c_ref, *refs):
        ins = refs[:count]
        out_ref, w_ref = refs[count + 2 * nz :]
        for h in range(nz):

            @pl.when((pl.program_id(0) ^ c_ref[1]) == h)
            def _(h=h):
                for at, ref in ((c_ref[0], refs[count + h]), (1 - c_ref[0], refs[count + nz + h])):
                    w_ref[pl.ds(pl.multiple_of(at * part, 16), part), :] = ref[...]

        w = w_ref[row : row + width, :]
        for n in range(tokens.count):
            grad_act = dot(w, tokens.cot(ins, n)[...], ((1,), (0,))) * scale
            out_ref[0, :, n * long : (n + 1) * long] = (
                grad_act * gelu_slope(tokens.hidden(ins, n))
            ).astype(BF16)

    w_specs = [pl.BlockSpec((part, model), lambda z, c: (0, 0))] * nz
    return pl.pallas_call(
        body,
        grid_spec=pltpu.PrefetchScalarGridSpec(
            num_scalar_prefetch=1,
            grid=(nz,),
            in_specs=tokens.specs + w_specs * 2,
            out_specs=pl.BlockSpec((1, width, tokens.count * long), lambda z, c: (z, 0, 0)),
            scratch_shapes=[pltpu.VMEM((CORES * part, model), BF16)],
        ),
        out_shape=jax.ShapeDtypeStruct((nz, width, tokens.count * long), BF16),
        **params(),
    )(core, *tokens.arrays, *mine, *other)


def grad_in_chunk(grads, inputs, core, scale, cut, block, width):
    nz, _, long = grads.shape
    model, tokens = inputs[0].shape
    count = len(inputs)
    half = nz // CORES
    high = model // cut

    def body(c_ref, g_ref, *refs):
        in_refs, outs = refs[:count], refs[count:]
        left = jnp.concatenate([i[...] for i in in_refs], axis=1)
        total = (dot(left, g_ref[0], ((1,), (1,))) * scale).astype(BF16)
        step = pl.program_id(0)
        for n in range(half):

            @pl.when(step == n)
            def _(n=n):
                for h in range(cut):
                    outs[n * cut + h][...] = total[h * high : (h + 1) * high]

        @pl.when(step >= half)
        def _():
            outs[-1][0] = total

    return pl.pallas_call(
        body,
        grid_spec=pltpu.PrefetchScalarGridSpec(
            num_scalar_prefetch=1,
            grid=(nz,),
            in_specs=[
                pl.BlockSpec(
                    (1, width, long),
                    lambda z, c: ((c[0] + 1 + z // half) % CORES * half + z % half, block, 0),
                )
            ]
            + [pl.BlockSpec((model, tokens), lambda z, c: (0, 0))] * count,
            out_specs=[pl.BlockSpec((high, width), lambda z, c: (0, 0))] * (half * cut)
            + [pl.BlockSpec((1, model, width), lambda z, c: (jnp.maximum(z - half, 0), 0, 0))],
        ),
        out_shape=[jax.ShapeDtypeStruct((high, width), BF16)] * (half * cut)
        + [jax.ShapeDtypeStruct((half, model, width), BF16)],
        **params(),
    )(core, grads, *inputs)


def transposed(value):
    rows, cols = value.shape
    wide = 2 * LANES

    def body(in_ref, out_ref):
        out_ref[...] = in_ref[...].T

    return pl.pallas_call(
        body,
        grid=(cols // wide,),
        in_specs=[pl.BlockSpec((rows, wide), lambda n: (0, n))],
        out_specs=pl.BlockSpec((wide, rows), lambda n: (n, 0)),
        out_shape=jax.ShapeDtypeStruct((cols, rows), value.dtype),
        **params(),
    )(value)


def half_rows(weight, core):
    rows, cols = weight.shape
    high = rows // CORES // 2

    def body(c_ref, in_ref, out_ref):
        out_ref[...] = in_ref[...].astype(BF16)

    return pl.pallas_call(
        body,
        grid_spec=pltpu.PrefetchScalarGridSpec(
            num_scalar_prefetch=1,
            grid=(2,),
            in_specs=[pl.BlockSpec((high, cols), lambda n, c: (c[0] * 2 + n, 0))],
            out_specs=pl.BlockSpec((high, cols), lambda n, c: (n, 0)),
        ),
        out_shape=jax.ShapeDtypeStruct((2 * high, cols), BF16),
        **params(WIDE),
    )(core, weight)


def stack(pieces, places, inner=False):
    count = len(pieces)
    shape = pieces[0].shape
    out = (shape[0], count, *shape[1:]) if inner else (count, *shape)

    def body(at_ref, *refs):
        for n in range(count):
            if inner:
                for p in range(shape[0]):
                    refs[count][p, at_ref[n]] = refs[n][p]
            else:
                refs[count][at_ref[n]] = refs[n][...]

    return pl.pallas_call(
        body,
        grid_spec=pltpu.PrefetchScalarGridSpec(
            num_scalar_prefetch=1,
            grid=(),
            in_specs=[pl.BlockSpec(shape, lambda at: (0,) * len(shape))] * count,
            out_specs=pl.BlockSpec(out, lambda at: (0,) * len(out)),
        ),
        out_shape=jax.ShapeDtypeStruct(out, pieces[0].dtype),
        **params(),
    )(places, *pieces)


def add_tiles(tiles):
    def body(*refs):
        refs[-1][...] = sum(ref[...] for ref in refs[:-1])

    return pl.pallas_call(
        body, out_shape=jax.ShapeDtypeStruct(tiles[0].shape, F32), **params()
    )(*tiles)


def reduce_step(place, keep, crosses, from_y, from_z, shift, stage, ny, split):
    lead, nz, mid, _, high, wide = keep.shape
    bit = len(from_z)

    def zed(n, at):
        if stage == "y":
            return n
        if stage == "end":
            return at[2]
        low = at[2] % (1 << bit)
        mine = (at[2] // (1 << bit)) % 2
        return n * (2 << bit) + (1 - mine) * (1 << bit) + low

    count = {"y": nz, "z": nz >> (bit + 1), "end": 1}[stage]
    six = (lead, 1, mid, 1, high, wide)
    five = (lead, 1, mid, high, wide)
    specs = [pl.BlockSpec(six, lambda n, at: (0, zed(n, at), 0, (at[1] + shift) % ny, 0, 0))]
    each = len(crosses) // lead
    long = nz // each
    for h in range(len(crosses)):
        specs.append(
            pl.BlockSpec(
                six[1:],
                lambda n, at, h=h % each: (
                    jnp.clip(zed(n, at) - h * long, 0, long - 1),
                    0,
                    (at[1] + shift) % ny,
                    0,
                    0,
                ),
            )
        )
    specs += [pl.BlockSpec(five, lambda n, at: (0, zed(n, at), 0, 0, 0))] * len(from_y)
    specs += [
        pl.BlockSpec(five, lambda n, at, j=j: (0, zed(n, at) // (2 << j), 0, 0, 0)) for j in range(bit)
    ]

    def body(at_ref, *refs):
        ins = refs[: len(specs)]
        outs = refs[len(specs) :]
        for p in range(lead):
            for m in range(mid):
                total = ins[1 + p * each][0, m, 0]
                for h in range(1, each):
                    total = jnp.where(
                        zed(pl.program_id(0), at_ref) >= h * long, ins[1 + p * each + h][0, m, 0], total
                    )
                total = total.astype(F32) + ins[0][p, 0, m, 0].astype(F32)
                for ref in ins[1 + len(crosses) :]:
                    total = total + ref[p, 0, m].astype(F32)
                total = total.astype(BF16)
                if not split:
                    outs[0][p, 0, m] = total
                    continue
                for s in range(mid):

                    @pl.when((at_ref[0] + s) % mid == m)
                    def _(s=s, total=total):
                        outs[s][p] = total

    if split:
        out_specs = [pl.BlockSpec((lead, high, wide), lambda n, at: (0, 0, 0))] * mid
        out_shape = [jax.ShapeDtypeStruct((lead, high, wide), BF16)] * mid
    else:
        out_specs = [pl.BlockSpec(five, lambda n, at: (0, n, 0, 0, 0))]
        out_shape = [jax.ShapeDtypeStruct((lead, count, mid, high, wide), BF16)]
    out = pl.pallas_call(
        body,
        grid_spec=pltpu.PrefetchScalarGridSpec(
            num_scalar_prefetch=1, grid=(count,), in_specs=specs, out_specs=out_specs
        ),
        out_shape=out_shape,
        **params(),
    )(place, keep, *crosses, *from_y, *from_z)
    return out if split else out[0]


def moments_kernel(core, weight, first, second, mine, other, grid, state_spec, grad_specs, owner, axis, tiles):
    block = state_spec.block_shape
    count = len(mine)
    long = 16 * (1 + len(tiles))

    def body(c_ref, w_ref, m_ref, v_ref, *refs):
        mine_refs, other_refs = refs[:count], refs[count : 2 * count]
        tile_refs = refs[2 * count : 2 * count + len(tiles)]
        new_m_ref, new_v_ref, u_ref, sum_ref = refs[2 * count + len(tiles) :]
        totals = [jnp.zeros((8, LANES), F32)] * 2
        start = 0
        ours = owner(pl.program_id(0)) == c_ref[0]
        for mine_ref, other_ref in zip(mine_refs, other_refs):
            size = mine_ref.size // block[1 - axis]
            shape = (size, block[1]) if axis == 0 else (block[0], size)
            at = (slice(start, start + size), slice(None))
            at = at if axis == 0 else at[::-1]
            grad = jnp.where(ours, mine_ref[...].reshape(shape), other_ref[...].reshape(shape)).astype(F32)
            weight = w_ref[at]
            new_m, new_v, update = moments(weight, m_ref[at], v_ref[at], grad)
            new_m_ref[at] = new_m
            new_v_ref[at] = new_v
            u_ref[at] = update
            for n, value in enumerate((weight, update)):
                square = value * value
                for col in range(0, shape[1], LANES):
                    totals[n] = totals[n] + square[:, col : col + LANES].reshape(-1, 8, LANES).sum(0)
            start += size

        @pl.when(pl.program_id(0) == 0)
        def _():
            sum_ref[:16] = jnp.zeros((16, LANES), F32)
            for n, tile_ref in enumerate(tile_refs):
                sum_ref[16 * (n + 1) : 16 * (n + 2)] = tile_ref[...]

        sum_ref[:8] += totals[0]
        sum_ref[8:16] += totals[1]

    state = jax.ShapeDtypeStruct(weight.shape, F32)
    return pl.pallas_call(
        body,
        grid_spec=pltpu.PrefetchScalarGridSpec(
            num_scalar_prefetch=1,
            grid=grid,
            in_specs=[state_spec] * 3
            + grad_specs * 2
            + [pl.BlockSpec((16, LANES), lambda n, c: (0, 0))] * len(tiles),
            out_specs=[state_spec] * 3 + [pl.BlockSpec((long, LANES), lambda n, c: (0, 0))],
        ),
        out_shape=[state] * 3 + [jax.ShapeDtypeStruct((long, LANES), F32)],
        **params(),
    )(core, weight, first, second, *mine, *other, *tiles)


def step_weights(weight, update, tiles, at):
    rows, cols = weight.shape
    high = rows // 5
    count = len(tiles)

    def body(w_ref, u_ref, *refs):
        sums = sum(ref[at : at + 16] for ref in refs[:count])
        ratio = jnp.sqrt(jnp.sum(sums[:8], keepdims=True)) / jnp.sqrt(jnp.sum(sums[8:], keepdims=True))
        refs[count][...] = w_ref[...] - 0.4 * ratio * u_ref[...]

    spec = pl.BlockSpec((high, cols), lambda n: (n, 0))
    tile = pl.BlockSpec(tiles[0].shape, lambda n: (0, 0))
    return pl.pallas_call(
        body,
        grid=(rows // high,),
        in_specs=[spec] * 2 + [tile] * count,
        out_specs=spec,
        out_shape=jax.ShapeDtypeStruct(weight.shape, F32),
        **params(),
    )(weight, update, *tiles)


class Order:
    def __init__(self):
        self.last = None

    def after(self, *values):
        if self.last is None:
            return values
        return lax.optimization_barrier((*values, self.last))[:-1]

    def did(self, value):
        self.last = value


def plan(nz, nx, ny):
    def along_x(value, step):
        pairs = [
            (z * nx + x, z * nx + (x + step) % nx) for z in range(nz) for x in range(nx)
        ]
        return lax.ppermute(value, "gx", pairs)

    def along_z(value, flip):
        pairs = [(z * nx + x, (z ^ flip) * nx + x) for z in range(nz) for x in range(nx)]
        return lax.ppermute(value, "gx", pairs)

    def along_y(value, step):
        pairs = [
            (y * CORES + c, (y + step) % ny * CORES + c) for y in range(ny) for c in range(CORES)
        ]
        return lax.ppermute(value, "gy", pairs)

    def across(value):
        pairs = [(k, k ^ 1) for k in range(ny * CORES)]
        return lax.ppermute(value, "gy", pairs)

    class Reduce:
        def __init__(self, order, at, sends, keep, shape):
            self.order, self.at, self.place = order, at, jnp.stack(at).astype(jnp.int32)
            self.keep = keep.reshape(shape)
            each = len(sends) // shape[0]
            self.crosses = [
                across(send).reshape(shape[1] // each, *shape[2:]) for send in sends
            ]
            self.from_y = []
            self.from_z = []

        def step(self, shift, stage, split=False):
            got = self.order.after(self.keep, *self.crosses, *self.from_y, *self.from_z)
            lead = 1 + len(self.crosses)
            count = lead + len(self.from_y)
            out = reduce_step(
                self.place, got[0], got[1:lead], got[lead:count], got[count:], shift, stage, ny, split
            )
            self.order.did(out[0] if split else out)
            return out

        def send_y(self):
            from_y = []
            for s in range(1, ny):
                from_y.append(along_y(self.step(s, "y"), s))
            self.from_y = from_y

        def send_z(self):
            bit = len(self.from_z)
            self.from_z.append(along_z(self.step(0, "z"), 1 << bit))

        def finish(self):
            out = self.step(0, "end", True)
            self.held = [out[0]] + [along_x(out[s], s) for s in range(1, len(out))]
            if len(out) == 1:
                self.share_y(out[0])

        def share_y(self, value):
            self.held = [value] + [along_y(value, s) for s in range(1, ny)]

        def stacked(self, place, size, inner=False):
            places = jnp.stack([(place - s) % size for s in range(size)]).astype(jnp.int32)
            value = stack(self.order.after(*self.held), places, inner)
            self.order.did(value)
            return value

        def stack_x(self):
            self.share_y(self.stacked(self.at[0], nx))

        def stack_y(self, inner=False):
            value = self.stacked(self.at[1], ny, inner)
            self.held = [value, across(value)]

    def local(inputs, hidden_pre, cotangent, w_in, m_in, v_in, w_out, m_out, v_out):
        model = inputs.shape[1]
        hidden_width = hidden_pre.shape[1]
        shard = hidden_width // (nz * nx)
        rows = model // (nz * nx)
        cuts = widths(shard)
        chunks = range(len(cuts))
        last = len(cuts) - 1
        starts = [sum(cuts[:k]) for k in chunks]
        scale_in = 1.0 / math.sqrt(model)
        scale_out = 1.0 / math.sqrt(hidden_width)
        place = lax.axis_index("gx")
        side = lax.axis_index("gy")
        z, x = place // nx, place % nx
        y, c = side // CORES, side % CORES
        core = jnp.reshape(c, (1,)).astype(jnp.int32)
        at_core = jnp.stack([c, z]).astype(jnp.int32)
        order = Order()

        packs, hiddens = [], []
        for t in range(1, nx):
            sent = pack(*order.after(hidden_pre, cotangent), (x + t) % nx, nz, nx, cuts)
            order.did(sent)
            packs.append(along_x(sent, t))

        part = half_rows(*order.after(w_out), core)
        order.did(part)
        flipped = transposed(*order.after(inputs))
        order.did(flipped)
        columns = [flipped] + [along_x(flipped, t) for t in range(1, nx)]
        own = pack(*order.after(hidden_pre, cotangent), x, nz, nx, cuts)
        order.did(own)
        for t in range(nx):
            value = pack_later(*order.after(hidden_pre), (x + t) % nx, nz, nx, cuts)
            if value:
                order.did(value[0])
            hiddens.append([along_x(h, t) for h in value] if t else value)
        found = {0: part, nz // 2: along_z(part, nz // 2)}
        bit = nz // 4
        while bit:
            for key in list(found):
                value = found[key]
                if key:
                    (value,) = order.after(value)
                found[key ^ bit] = along_z(value, bit)
            bit //= 2
        found = [found[key] for key in range(nz)]
        crossed = [across(value) for value in [*order.after(*found[: nz // 2]), *found[nz // 2 :]]]
        packs = [own] + packs

        parts = [PARTS for _ in chunks]
        outs = [None for _ in chunks]
        pieces_in = [(0, 0, cuts[0])]
        if last:
            pieces_in.append((1, 0, cuts[1]))
        ins = [None for _ in pieces_in]
        pres = [None for _ in chunks]

        def tokens(k, *more):
            later = [] if k == 0 else [value[k - 1] for value in hiddens]
            got = order.after(*packs, *later, *more)
            count = nx + len(later)
            blocks = Tokens(got[:nx], got[nx:count] if later else None, model, nz, cuts[k])
            return blocks, got[count:]

        def start_out(k):
            blocks, _ = tokens(k, *([*crossed[: nz // 2], found[nz // 2]] if k == 0 else []))
            *sends, keep = grad_out_chunk(blocks, core, nz, scale_out, parts[k])
            order.did(keep)
            shape = (parts[k], nz, 1, ny, cuts[k] // parts[k] // ny, model // CORES)
            outs[k] = Reduce(order, (x, y, z), sends, keep, shape)

        def start_pre(k):
            blocks, got = tokens(k, *found, *crossed)
            pres[k] = grad_pre_chunk(blocks, got[:nz], got[nz:], nz, starts[k], at_core, scale_out)
            order.did(pres[k])

        def start_in(k):
            chunk, block, width = pieces_in[k]
            got = order.after(pres[chunk], *columns)
            *sends, keep = grad_in_chunk(
                got[0], got[1:], core, scale_in, PARTS if width > LANES else 1, block, width
            )
            order.did(keep)
            shape = (nz // CORES, nz, nx, ny, rows // ny, width)
            ins[k] = Reduce(order, (x, y, z), sends, keep, shape)

        def sums(tile):
            tiles = order.after(tile, *[along_z(tile, flip) for flip in range(1, nz)])
            tile = add_tiles(tiles)
            order.did(tile)
            return [tile] + [along_x(tile, t) for t in range(1, nx)]

        def new_weights(weight, update, tiles, at):
            got = order.after(weight, update, *tiles)
            value = step_weights(got[0], got[1], got[2:], at)
            order.did(value)
            return value

        def moments_out():
            half = model // CORES
            got = order.after(
                w_out, m_out, v_out, *[outs[k].held[0] for k in chunks], *[outs[k].held[1] for k in chunks]
            )
            new = moments_kernel(
                core,
                *got[:3],
                got[3 : 4 + last],
                got[4 + last :],
                (CORES,),
                pl.BlockSpec((shard, half), lambda n, c: (0, n)),
                [
                    pl.BlockSpec((p, ny, w // p // ny, half), lambda n, c: (0, 0, 0, 0))
                    for w, p in zip(cuts, parts)
                ],
                lambda n: n,
                0,
                [],
            )
            order.did(new[3])
            return new

        start_out(0)
        outs[0].send_y()
        start_pre(0)
        start_in(0)
        outs[0].send_z()
        ins[0].send_y()
        if last:
            start_out(1)
            outs[1].send_y()
            start_pre(1)
            outs[0].send_z()
            ins[0].send_z()
            start_in(1)
            ins[1].send_y()
            outs[1].send_z()
            ins[0].send_z()
            outs[0].finish()
            outs[1].send_z()
            ins[1].send_z()
            ins[0].finish()
            outs[0].stack_y(True)
            ins[1].send_z()
            ins[0].stack_x()
            outs[1].finish()
            ins[0].stack_y()
            ins[1].finish()
            outs[1].stack_y(True)
            ins[1].stack_x()
            first_out, second_out, update_out, tile = moments_out()
            ins[1].stack_y()
        else:
            outs[0].send_z()
            ins[0].send_z()
            outs[0].finish()
            ins[0].send_z()
            outs[0].stack_y(True)
            ins[0].finish()
            first_out, second_out, update_out, tile = moments_out()
            ins[0].stack_x()
            ins[0].stack_y()

        held = [value.held for value in ins]
        got = order.after(w_in, m_in, v_in, tile, *[pair[0] for pair in held], *[pair[1] for pair in held])
        mine, other = got[4 : 4 + len(ins)], got[4 + len(ins) :]
        if shard % LANES:
            joined = [
                jnp.stack([jnp.where(c == 0, a, b), jnp.where(c == 0, b, a)]) for a, b in zip(mine, other)
            ]
            grad = jnp.concatenate(joined, axis=-1).transpose(1, 4, 0, 3, 2, 5)
            grad = grad.reshape(rows, hidden_width).astype(F32)
            first_in, second_in, update_in = moments(*got[:3], grad)
            tile = jnp.concatenate(
                [
                    jnp.sum((value * value).reshape(-1, 8, LANES), axis=0)
                    for value in (w_in, update_in)
                ]
                + [got[3]]
            )
        else:
            zs = nz // CORES
            first_in, second_in, update_in, tile = moments_kernel(
                core,
                *got[:3],
                mine,
                other,
                (nz * nx,),
                pl.BlockSpec((rows, shard), lambda n, c: (0, n)),
                [
                    pl.BlockSpec(
                        (ny, 1, 1, rows // ny, w), lambda n, c: (0, n % nx, n // nx % zs, 0, 0)
                    )
                    for _, _, w in pieces_in
                ],
                lambda n: n // nx // zs,
                1,
                [got[3]],
            )
        order.did(tile)
        tiles = sums(tile)
        new_w_in = new_weights(w_in, update_in, tiles, 0)
        new_w_out = new_weights(w_out, update_out, tiles, 16)
        return (new_w_in, first_in, second_in, new_w_out, first_out, second_out)

    return local


def solution(mesh):
    gx, gy = mesh.shape["gx"], mesh.shape["gy"]
    nz = CHIPS_Z
    state = P("gx", None)
    tokens = P(("gx", "gy"), None)
    return jax.shard_map(
        plan(nz, gx // nz, gy // CORES),
        mesh=mesh,
        in_specs=(tokens,) * 3 + (state,) * 6,
        out_specs=(state,) * 6,
        check_vma=False,
    )
```

```python
import functools
import math

import jax
import jax.numpy as jnp
from jax import lax
from jax.experimental import pallas as pl
from jax.experimental.pallas import tpu as pltpu
from jax.sharding import PartitionSpec as P

BF16 = jnp.bfloat16
F32 = jnp.float32
CORES = 2
CHIPS_Z = 4
LANES = 128
PARTS = 2
VMEM = 24 * 1024 * 1024
WIDE = 56 * 1024 * 1024
SMALL = 8 * 1024 * 1024


def moments(weight, first, second, grad):
    new_first = 0.9 * first + 0.1 * grad
    new_second = 0.95 * second + 0.05 * grad * grad
    update = new_first / (jnp.sqrt(new_second) + 1e-06) + 0.05 * weight
    return (new_first, new_second, update)


def squares(value):
    return jnp.sum(value * value)


def gelu(value):
    return 0.5 * value * (1.0 + lax.erf(value * (1.0 / math.sqrt(2.0))))


def gelu_slope(value):
    cdf = 0.5 * (1.0 + lax.erf(value * (1.0 / math.sqrt(2.0))))
    return cdf + value * (jnp.exp(-0.5 * value * value) * (1.0 / math.sqrt(2.0 * math.pi)))


def widths(shard):
    if shard % LANES:
        return (shard,)
    first = shard // LANES * 3 // 5 * LANES
    return (first, shard - first)


def dot(left, right, dims):
    return lax.dot_general(left, right, (dims, ((), ())), preferred_element_type=F32)


def params(grant=VMEM):
    return dict(
        compiler_params=pltpu.CompilerParams(vmem_limit_bytes=grant),
        cost_estimate=pl.CostEstimate(flops=1, bytes_accessed=1, transcendentals=0),
    )


def pack(hidden, cotangent, at, nz, nx, cuts):
    tokens, hidden_width = hidden.shape
    model = cotangent.shape[1]
    shard = hidden_width // (nz * nx)
    first = cuts[0]
    if shard % LANES:
        parts = [
            lax.dynamic_slice_in_dim(hidden, (z * nx + at) * shard, shard, 1).T for z in range(nz)
        ]
        return jnp.concatenate([cotangent.T, *parts])

    def body(at_ref, h_ref, cot_ref, out_ref):
        z = pl.program_id(0)

        @pl.when(z == 0)
        def _():
            out_ref[:model] = cot_ref[...].T

        out_ref[pl.ds(pl.multiple_of(model + z * first, LANES), first)] = h_ref[:, :first].T

    total = model + nz * first
    return pl.pallas_call(
        body,
        grid_spec=pltpu.PrefetchScalarGridSpec(
            num_scalar_prefetch=1,
            grid=(nz,),
            in_specs=[
                pl.BlockSpec((tokens, shard), lambda z, a: (0, z * nx + a[0])),
                pl.BlockSpec((tokens, model), lambda z, a: (0, 0)),
            ],
            out_specs=pl.BlockSpec((total, tokens), lambda z, a: (0, 0)),
        ),
        out_shape=jax.ShapeDtypeStruct((total, tokens), BF16),
        **params(WIDE),
    )(jnp.reshape(at, (1,)).astype(jnp.int32), hidden, cotangent)


def pack_later(hidden, at, nz, nx, cuts):
    tokens, hidden_width = hidden.shape
    shard = hidden_width // (nz * nx)
    if len(cuts) == 1:
        return []

    def body(at_ref, h_ref, *out_refs):
        start = cuts[0]
        for width, out_ref in zip(cuts[1:], out_refs):
            out_ref[0] = h_ref[:, start : start + width].T
            start += width

    return pl.pallas_call(
        body,
        grid_spec=pltpu.PrefetchScalarGridSpec(
            num_scalar_prefetch=1,
            grid=(nz,),
            in_specs=[pl.BlockSpec((tokens, shard), lambda z, a: (0, z * nx + a[0]))],
            out_specs=[pl.BlockSpec((1, w, tokens), lambda z, a: (z, 0, 0)) for w in cuts[1:]],
        ),
        out_shape=[jax.ShapeDtypeStruct((nz, w, tokens), BF16) for w in cuts[1:]],
        **params(WIDE),
    )(jnp.reshape(at, (1,)).astype(jnp.int32), hidden)


class Tokens:
    def __init__(self, packs, hiddens, model, nz, width):
        tokens = packs[0].shape[1]
        self.model, self.width, self.count = model, width, len(packs)
        if hiddens is None:
            self.arrays = list(packs)
            self.specs = [pl.BlockSpec(packs[0].shape, lambda z, c: (0, 0))] * len(packs)
        else:
            self.arrays = [*packs, *hiddens]
            self.specs = [pl.BlockSpec((model, tokens), lambda z, c: (0, 0))] * len(packs)
            self.specs += [pl.BlockSpec((1, width, tokens), lambda z, c: (z, 0, 0))] * len(packs)

    def cot(self, refs, n):
        return refs[n].at[: self.model]

    def hidden(self, refs, n):
        if len(refs) == self.count:
            row = self.model + pl.program_id(0) * self.width
            return refs[n][pl.ds(pl.multiple_of(row, 16), self.width)].astype(F32)
        return refs[self.count + n][0].astype(F32)


def grad_out_chunk(tokens, core, nz, scale, parts):
    width, model = tokens.width, tokens.model
    half = model // CORES
    high = width // parts
    count = len(tokens.arrays)

    def body(c_ref, *refs):
        ins, outs = refs[:count], refs[count:]
        acts = jnp.concatenate(
            [gelu(tokens.hidden(ins, n)).astype(BF16) for n in range(tokens.count)], axis=1
        )
        for which in range(2):
            cols = pl.ds(pl.multiple_of((c_ref[0] + 1 + which) % CORES * half, 16), half)
            right = jnp.concatenate([tokens.cot(ins, n)[cols, :] for n in range(tokens.count)], axis=1)
            total = (dot(acts, right, ((1,), (1,))) * scale).astype(BF16)
            for p in range(parts):
                value = total[p * high : (p + 1) * high]
                if which:
                    outs[parts][p, 0] = value
                else:
                    outs[p][0] = value

    return pl.pallas_call(
        body,
        grid_spec=pltpu.PrefetchScalarGridSpec(
            num_scalar_prefetch=1,
            grid=(nz,),
            in_specs=tokens.specs,
            out_specs=[pl.BlockSpec((1, high, half), lambda z, c: (z, 0, 0))] * parts
            + [pl.BlockSpec((parts, 1, high, half), lambda z, c: (0, z, 0, 0))],
        ),
        out_shape=[jax.ShapeDtypeStruct((nz, high, half), BF16)] * parts
        + [jax.ShapeDtypeStruct((parts, nz, high, half), BF16)],
        **params(),
    )(core, *tokens.arrays)


def grad_pre_chunk(tokens, mine, other, nz, row, core, scale):
    part, model = mine[0].shape
    width = tokens.width
    count = len(tokens.arrays)
    long = tokens.arrays[0].shape[1]

    def body(c_ref, *refs):
        ins = refs[:count]
        out_ref, w_ref = refs[count + 2 * nz :]
        for h in range(nz):

            @pl.when((pl.program_id(0) ^ c_ref[1]) == h)
            def _(h=h):
                for at, ref in ((c_ref[0], refs[count + h]), (1 - c_ref[0], refs[count + nz + h])):
                    w_ref[pl.ds(pl.multiple_of(at * part, 16), part), :] = ref[...]

        w = w_ref[row : row + width, :]
        for n in range(tokens.count):
            grad_act = dot(w, tokens.cot(ins, n)[...], ((1,), (0,))) * scale
            out_ref[0, :, n * long : (n + 1) * long] = (
                grad_act * gelu_slope(tokens.hidden(ins, n))
            ).astype(BF16)

    w_specs = [pl.BlockSpec((part, model), lambda z, c: (0, 0))] * nz
    return pl.pallas_call(
        body,
        grid_spec=pltpu.PrefetchScalarGridSpec(
            num_scalar_prefetch=1,
            grid=(nz,),
            in_specs=tokens.specs + w_specs * 2,
            out_specs=pl.BlockSpec((1, width, tokens.count * long), lambda z, c: (z, 0, 0)),
            scratch_shapes=[pltpu.VMEM((CORES * part, model), BF16)],
        ),
        out_shape=jax.ShapeDtypeStruct((nz, width, tokens.count * long), BF16),
        **params(),
    )(core, *tokens.arrays, *mine, *other)


def grad_in_chunk(grads, inputs, core, scale, cut, block, width):
    nz, _, long = grads.shape
    model, tokens = inputs[0].shape
    count = len(inputs)
    half = nz // CORES
    high = model // cut

    def body(c_ref, g_ref, *refs):
        in_refs, outs = refs[:count], refs[count:]
        left = jnp.concatenate([i[...] for i in in_refs], axis=1)
        total = (dot(left, g_ref[0], ((1,), (1,))) * scale).astype(BF16)
        step = pl.program_id(0)
        for n in range(half):

            @pl.when(step == n)
            def _(n=n):
                for h in range(cut):
                    outs[n * cut + h][...] = total[h * high : (h + 1) * high]

        @pl.when(step >= half)
        def _():
            outs[-1][0] = total

    return pl.pallas_call(
        body,
        grid_spec=pltpu.PrefetchScalarGridSpec(
            num_scalar_prefetch=1,
            grid=(nz,),
            in_specs=[
                pl.BlockSpec(
                    (1, width, long),
                    lambda z, c: ((c[0] + 1 + z // half) % CORES * half + z % half, block, 0),
                )
            ]
            + [pl.BlockSpec((model, tokens), lambda z, c: (0, 0))] * count,
            out_specs=[pl.BlockSpec((high, width), lambda z, c: (0, 0))] * (half * cut)
            + [pl.BlockSpec((1, model, width), lambda z, c: (jnp.maximum(z - half, 0), 0, 0))],
        ),
        out_shape=[jax.ShapeDtypeStruct((high, width), BF16)] * (half * cut)
        + [jax.ShapeDtypeStruct((half, model, width), BF16)],
        **params(),
    )(core, grads, *inputs)


def transposed(value):
    rows, cols = value.shape
    wide = 2 * LANES

    def body(in_ref, out_ref):
        out_ref[...] = in_ref[...].T

    return pl.pallas_call(
        body,
        grid=(cols // wide,),
        in_specs=[pl.BlockSpec((rows, wide), lambda n: (0, n))],
        out_specs=pl.BlockSpec((wide, rows), lambda n: (n, 0)),
        out_shape=jax.ShapeDtypeStruct((cols, rows), value.dtype),
        **params(),
    )(value)


def half_rows(weight, core):
    rows, cols = weight.shape
    high = rows // CORES // 2

    def body(c_ref, in_ref, out_ref):
        out_ref[...] = in_ref[...].astype(BF16)

    return pl.pallas_call(
        body,
        grid_spec=pltpu.PrefetchScalarGridSpec(
            num_scalar_prefetch=1,
            grid=(2,),
            in_specs=[pl.BlockSpec((high, cols), lambda n, c: (c[0] * 2 + n, 0))],
            out_specs=pl.BlockSpec((high, cols), lambda n, c: (n, 0)),
        ),
        out_shape=jax.ShapeDtypeStruct((2 * high, cols), BF16),
        **params(WIDE),
    )(core, weight)


def stack(pieces, places, inner=False):
    count = len(pieces)
    shape = pieces[0].shape
    out = (shape[0], count, *shape[1:]) if inner else (count, *shape)

    def body(at_ref, *refs):
        for n in range(count):
            if inner:
                for p in range(shape[0]):
                    refs[count][p, at_ref[n]] = refs[n][p]
            else:
                refs[count][at_ref[n]] = refs[n][...]

    return pl.pallas_call(
        body,
        grid_spec=pltpu.PrefetchScalarGridSpec(
            num_scalar_prefetch=1,
            grid=(),
            in_specs=[pl.BlockSpec(shape, lambda at: (0,) * len(shape))] * count,
            out_specs=pl.BlockSpec(out, lambda at: (0,) * len(out)),
        ),
        out_shape=jax.ShapeDtypeStruct(out, pieces[0].dtype),
        **params(SMALL),
    )(places, *pieces)


def add_tiles(tiles):
    def body(*refs):
        refs[-1][...] = sum(ref[...] for ref in refs[:-1])

    return pl.pallas_call(
        body, out_shape=jax.ShapeDtypeStruct(tiles[0].shape, F32), **params(SMALL)
    )(*tiles)


def reduce_step(place, keep, crosses, from_y, from_z, shift, stage, ny, split):
    lead, nz, mid, _, high, wide = keep.shape
    bit = len(from_z)

    def zed(n, at):
        if stage == "y":
            return n
        if stage == "end":
            return at[2]
        low = at[2] % (1 << bit)
        mine = (at[2] // (1 << bit)) % 2
        return n * (2 << bit) + (1 - mine) * (1 << bit) + low

    count = {"y": nz, "z": nz >> (bit + 1), "end": 1}[stage]
    six = (lead, 1, mid, 1, high, wide)
    five = (lead, 1, mid, high, wide)
    specs = [pl.BlockSpec(six, lambda n, at: (0, zed(n, at), 0, (at[1] + shift) % ny, 0, 0))]
    each = len(crosses) // lead
    long = nz // each
    for h in range(len(crosses)):
        specs.append(
            pl.BlockSpec(
                six[1:],
                lambda n, at, h=h % each: (
                    jnp.clip(zed(n, at) - h * long, 0, long - 1),
                    0,
                    (at[1] + shift) % ny,
                    0,
                    0,
                ),
            )
        )
    specs += [pl.BlockSpec(five, lambda n, at: (0, zed(n, at), 0, 0, 0))] * len(from_y)
    specs += [
        pl.BlockSpec(five, lambda n, at, j=j: (0, zed(n, at) // (2 << j), 0, 0, 0)) for j in range(bit)
    ]

    def body(at_ref, *refs):
        ins = refs[: len(specs)]
        outs = refs[len(specs) :]
        for p in range(lead):
            for m in range(mid):
                total = ins[1 + p * each][0, m, 0]
                for h in range(1, each):
                    total = jnp.where(
                        zed(pl.program_id(0), at_ref) >= h * long, ins[1 + p * each + h][0, m, 0], total
                    )
                total = total.astype(F32) + ins[0][p, 0, m, 0].astype(F32)
                for ref in ins[1 + len(crosses) :]:
                    total = total + ref[p, 0, m].astype(F32)
                total = total.astype(BF16)
                if not split:
                    outs[0][p, 0, m] = total
                    continue
                for s in range(mid):

                    @pl.when((at_ref[0] + s) % mid == m)
                    def _(s=s, total=total):
                        outs[s][p] = total

    if split:
        out_specs = [pl.BlockSpec((lead, high, wide), lambda n, at: (0, 0, 0))] * mid
        out_shape = [jax.ShapeDtypeStruct((lead, high, wide), BF16)] * mid
    else:
        out_specs = [pl.BlockSpec(five, lambda n, at: (0, n, 0, 0, 0))]
        out_shape = [jax.ShapeDtypeStruct((lead, count, mid, high, wide), BF16)]
    out = pl.pallas_call(
        body,
        grid_spec=pltpu.PrefetchScalarGridSpec(
            num_scalar_prefetch=1, grid=(count,), in_specs=specs, out_specs=out_specs
        ),
        out_shape=out_shape,
        **params(SMALL),
    )(place, keep, *crosses, *from_y, *from_z)
    return out if split else out[0]


def moments_kernel(core, weight, first, second, mine, other, grid, state_spec, grad_specs, owner, axis, tiles):
    block = state_spec.block_shape
    count = len(mine)
    long = 16 * (1 + len(tiles))

    def body(c_ref, w_ref, m_ref, v_ref, *refs):
        mine_refs, other_refs = refs[:count], refs[count : 2 * count]
        tile_refs = refs[2 * count : 2 * count + len(tiles)]
        new_m_ref, new_v_ref, u_ref, sum_ref = refs[2 * count + len(tiles) :]
        totals = [jnp.zeros((8, LANES), F32)] * 2
        start = 0
        ours = owner(pl.program_id(0)) == c_ref[0]
        for mine_ref, other_ref in zip(mine_refs, other_refs):
            size = mine_ref.size // block[1 - axis]
            shape = (size, block[1]) if axis == 0 else (block[0], size)
            at = (slice(start, start + size), slice(None))
            at = at if axis == 0 else at[::-1]
            grad = jnp.where(ours, mine_ref[...].reshape(shape), other_ref[...].reshape(shape)).astype(F32)
            weight = w_ref[at]
            new_m, new_v, update = moments(weight, m_ref[at], v_ref[at], grad)
            new_m_ref[at] = new_m
            new_v_ref[at] = new_v
            u_ref[at] = update
            for n, value in enumerate((weight, update)):
                square = value * value
                for col in range(0, shape[1], LANES):
                    totals[n] = totals[n] + square[:, col : col + LANES].reshape(-1, 8, LANES).sum(0)
            start += size

        @pl.when(pl.program_id(0) == 0)
        def _():
            sum_ref[:16] = jnp.zeros((16, LANES), F32)
            for n, tile_ref in enumerate(tile_refs):
                sum_ref[16 * (n + 1) : 16 * (n + 2)] = tile_ref[...]

        sum_ref[:8] += totals[0]
        sum_ref[8:16] += totals[1]

    state = jax.ShapeDtypeStruct(weight.shape, F32)
    return pl.pallas_call(
        body,
        grid_spec=pltpu.PrefetchScalarGridSpec(
            num_scalar_prefetch=1,
            grid=grid,
            in_specs=[state_spec] * 3
            + grad_specs * 2
            + [pl.BlockSpec((16, LANES), lambda n, c: (0, 0))] * len(tiles),
            out_specs=[state_spec] * 3 + [pl.BlockSpec((long, LANES), lambda n, c: (0, 0))],
        ),
        out_shape=[state] * 3 + [jax.ShapeDtypeStruct((long, LANES), F32)],
        **params(),
    )(core, weight, first, second, *mine, *other, *tiles)


def step_weights(weight, update, tiles, at):
    rows, cols = weight.shape
    high = rows // 5
    count = len(tiles)

    def body(w_ref, u_ref, *refs):
        sums = sum(ref[at : at + 16] for ref in refs[:count])
        ratio = jnp.sqrt(jnp.sum(sums[:8], keepdims=True)) / jnp.sqrt(jnp.sum(sums[8:], keepdims=True))
        refs[count][...] = w_ref[...] - 0.4 * ratio * u_ref[...]

    spec = pl.BlockSpec((high, cols), lambda n: (n, 0))
    tile = pl.BlockSpec(tiles[0].shape, lambda n: (0, 0))
    return pl.pallas_call(
        body,
        grid=(rows // high,),
        in_specs=[spec] * 2 + [tile] * count,
        out_specs=spec,
        out_shape=jax.ShapeDtypeStruct(weight.shape, F32),
        **params(),
    )(weight, update, *tiles)


class Order:
    def __init__(self):
        self.last = None

    def after(self, *values):
        if self.last is None:
            return values
        return lax.optimization_barrier((*values, self.last))[:-1]

    def did(self, value):
        self.last = value


def plan(nz, nx, ny):
    def along_x(value, step):
        pairs = [
            (z * nx + x, z * nx + (x + step) % nx) for z in range(nz) for x in range(nx)
        ]
        return lax.ppermute(value, "gx", pairs)

    def along_z(value, flip):
        pairs = [(z * nx + x, (z ^ flip) * nx + x) for z in range(nz) for x in range(nx)]
        return lax.ppermute(value, "gx", pairs)

    def along_y(value, step):
        pairs = [
            (y * CORES + c, (y + step) % ny * CORES + c) for y in range(ny) for c in range(CORES)
        ]
        return lax.ppermute(value, "gy", pairs)

    def across(value):
        pairs = [(k, k ^ 1) for k in range(ny * CORES)]
        return lax.ppermute(value, "gy", pairs)

    class Reduce:
        def __init__(self, order, at, sends, keep, shape):
            self.order, self.at, self.place = order, at, jnp.stack(at).astype(jnp.int32)
            self.keep = keep.reshape(shape)
            each = len(sends) // shape[0]
            self.crosses = [
                across(send).reshape(shape[1] // each, *shape[2:]) for send in sends
            ]
            self.from_y = []
            self.from_z = []

        def step(self, shift, stage, split=False):
            got = self.order.after(self.keep, *self.crosses, *self.from_y, *self.from_z)
            lead = 1 + len(self.crosses)
            count = lead + len(self.from_y)
            out = reduce_step(
                self.place, got[0], got[1:lead], got[lead:count], got[count:], shift, stage, ny, split
            )
            self.order.did(out[0] if split else out)
            return out

        def send_y(self):
            from_y = []
            for s in range(1, ny):
                from_y.append(along_y(self.step(s, "y"), s))
            self.from_y = from_y

        def send_z(self):
            bit = len(self.from_z)
            self.from_z.append(along_z(self.step(0, "z"), 1 << bit))

        def finish(self):
            out = self.step(0, "end", True)
            self.held = [out[0]] + [along_x(out[s], s) for s in range(1, len(out))]
            if len(out) == 1:
                self.share_y(out[0])

        def share_y(self, value):
            self.held = [value] + [along_y(value, s) for s in range(1, ny)]

        def stacked(self, place, size, inner=False):
            places = jnp.stack([(place - s) % size for s in range(size)]).astype(jnp.int32)
            value = stack(self.order.after(*self.held), places, inner)
            self.order.did(value)
            return value

        def stack_x(self):
            self.share_y(self.stacked(self.at[0], nx))

        def stack_y(self, inner=False):
            value = self.stacked(self.at[1], ny, inner)
            self.held = [value, across(value)]

    def local(inputs, hidden_pre, cotangent, w_in, m_in, v_in, w_out, m_out, v_out):
        model = inputs.shape[1]
        hidden_width = hidden_pre.shape[1]
        shard = hidden_width // (nz * nx)
        rows = model // (nz * nx)
        cuts = widths(shard)
        chunks = range(len(cuts))
        last = len(cuts) - 1
        starts = [sum(cuts[:k]) for k in chunks]
        scale_in = 1.0 / math.sqrt(model)
        scale_out = 1.0 / math.sqrt(hidden_width)
        place = lax.axis_index("gx")
        side = lax.axis_index("gy")
        z, x = place // nx, place % nx
        y, c = side // CORES, side % CORES
        core = jnp.reshape(c, (1,)).astype(jnp.int32)
        at_core = jnp.stack([c, z]).astype(jnp.int32)
        order = Order()

        packs, hiddens = [], []
        for t in range(1, nx):
            sent = pack(*order.after(hidden_pre, cotangent), (x + t) % nx, nz, nx, cuts)
            order.did(sent)
            packs.append(along_x(sent, t))

        part = half_rows(*order.after(w_out), core)
        order.did(part)
        flipped = transposed(*order.after(inputs))
        order.did(flipped)
        columns = [flipped] + [along_x(flipped, t) for t in range(1, nx)]
        own = pack(*order.after(hidden_pre, cotangent), x, nz, nx, cuts)
        order.did(own)
        for t in range(nx):
            value = pack_later(*order.after(hidden_pre), (x + t) % nx, nz, nx, cuts)
            if value:
                order.did(value[0])
            hiddens.append([along_x(h, t) for h in value] if t else value)
        found = {0: part, nz // 2: along_z(part, nz // 2)}
        bit = nz // 4
        while bit:
            for key in list(found):
                value = found[key]
                if key:
                    (value,) = order.after(value)
                found[key ^ bit] = along_z(value, bit)
            bit //= 2
        found = [found[key] for key in range(nz)]
        crossed = [across(value) for value in [*order.after(*found[: nz // 2]), *found[nz // 2 :]]]
        packs = [own] + packs

        parts = [PARTS for _ in chunks]
        outs = [None for _ in chunks]
        pieces_in = [(0, 0, cuts[0])]
        if last:
            pieces_in.append((1, 0, cuts[1]))
        ins = [None for _ in pieces_in]
        pres = [None for _ in chunks]

        def tokens(k, *more):
            later = [] if k == 0 else [value[k - 1] for value in hiddens]
            got = order.after(*packs, *later, *more)
            count = nx + len(later)
            blocks = Tokens(got[:nx], got[nx:count] if later else None, model, nz, cuts[k])
            return blocks, got[count:]

        def start_out(k):
            blocks, _ = tokens(k, *([*crossed[: nz // 2], found[nz // 2]] if k == 0 else []))
            *sends, keep = grad_out_chunk(blocks, core, nz, scale_out, parts[k])
            order.did(keep)
            shape = (parts[k], nz, 1, ny, cuts[k] // parts[k] // ny, model // CORES)
            outs[k] = Reduce(order, (x, y, z), sends, keep, shape)

        def start_pre(k):
            blocks, got = tokens(k, *found, *crossed)
            pres[k] = grad_pre_chunk(blocks, got[:nz], got[nz:], nz, starts[k], at_core, scale_out)
            order.did(pres[k])

        def start_in(k):
            chunk, block, width = pieces_in[k]
            got = order.after(pres[chunk], *columns)
            *sends, keep = grad_in_chunk(
                got[0], got[1:], core, scale_in, 1, block, width
            )
            order.did(keep)
            shape = (nz // CORES, nz, nx, ny, rows // ny, width)
            ins[k] = Reduce(order, (x, y, z), sends, keep, shape)

        def sums(tile):
            tiles = order.after(tile, *[along_z(tile, flip) for flip in range(1, nz)])
            tile = add_tiles(tiles)
            order.did(tile)
            return [tile] + [along_x(tile, t) for t in range(1, nx)]

        def new_weights(weight, update, tiles, at):
            got = order.after(weight, update, *tiles)
            value = step_weights(got[0], got[1], got[2:], at)
            order.did(value)
            return value

        def moments_out(tile):
            half = model // CORES
            got = order.after(
                w_out,
                m_out,
                v_out,
                tile,
                *[outs[k].held[0] for k in chunks],
                *[outs[k].held[1] for k in chunks],
            )
            new = moments_kernel(
                core,
                *got[:3],
                got[4 : 5 + last],
                got[5 + last :],
                (CORES,),
                pl.BlockSpec((shard, half), lambda n, c: (0, n)),
                [
                    pl.BlockSpec((p, ny, w // p // ny, half), lambda n, c: (0, 0, 0, 0))
                    for w, p in zip(cuts, parts)
                ],
                lambda n: n,
                0,
                [got[3]],
            )
            order.did(new[3])
            return new

        start_out(0)
        outs[0].send_y()
        start_pre(0)
        start_in(0)
        outs[0].send_z()
        ins[0].send_y()
        if last:
            start_pre(1)
            start_in(1)
            start_out(1)
            ins[1].send_y()
            ins[0].send_z()
            outs[0].send_z()
            outs[1].send_y()
            ins[0].send_z()
            outs[0].finish()
            ins[1].send_z()
            ins[0].finish()
            ins[1].send_z()
            outs[1].send_z()
            outs[0].stack_y(True)
            ins[0].stack_x()
            ins[1].finish()
            outs[1].send_z()
            ins[0].stack_y()
            ins[1].stack_x()
            outs[1].finish()
            ins[1].stack_y()
        else:
            outs[0].send_z()
            ins[0].send_z()
            outs[0].finish()
            ins[0].send_z()
            ins[0].finish()
            ins[0].stack_x()
            ins[0].stack_y()

        held = [value.held for value in ins]
        got = order.after(w_in, m_in, v_in, *[pair[0] for pair in held], *[pair[1] for pair in held])
        mine, other = got[3 : 3 + len(ins)], got[3 + len(ins) :]
        if shard % LANES:
            joined = [
                jnp.stack([jnp.where(c == 0, a, b), jnp.where(c == 0, b, a)]) for a, b in zip(mine, other)
            ]
            grad = jnp.concatenate(joined, axis=-1).transpose(1, 4, 0, 3, 2, 5)
            grad = grad.reshape(rows, hidden_width).astype(F32)
            first_in, second_in, update_in = moments(*got[:3], grad)
            tile = jnp.concatenate(
                [
                    jnp.sum((value * value).reshape(-1, 8, LANES), axis=0)
                    for value in (w_in, update_in)
                ]
            )
        else:
            zs = nz // CORES
            first_in, second_in, update_in, tile = moments_kernel(
                core,
                *got[:3],
                mine,
                other,
                (nz * nx,),
                pl.BlockSpec((rows, shard), lambda n, c: (0, n)),
                [
                    pl.BlockSpec(
                        (ny, 1, 1, rows // ny, w), lambda n, c: (0, n % nx, n // nx % zs, 0, 0)
                    )
                    for _, _, w in pieces_in
                ],
                lambda n: n // nx // zs,
                1,
                [],
            )
        order.did(tile)

        outs[last].stack_y(True)
        first_out, second_out, update_out, tile = moments_out(tile)
        tiles = sums(tile)
        new_w_in = new_weights(w_in, update_in, tiles, 16)
        new_w_out = new_weights(w_out, update_out, tiles, 0)
        return (new_w_in, first_in, second_in, new_w_out, first_out, second_out)

    return local


def solution(mesh):
    gx, gy = mesh.shape["gx"], mesh.shape["gy"]
    nz = CHIPS_Z
    state = P("gx", None)
    tokens = P(("gx", "gy"), None)
    return jax.shard_map(
        plan(nz, gx // nz, gy // CORES),
        mesh=mesh,
        in_specs=(tokens,) * 3 + (state,) * 6,
        out_specs=(state,) * 6,
        check_vma=False,
    )
```

```python
import functools
import math

import jax
import jax.numpy as jnp
from jax import lax
from jax.experimental import pallas as pl
from jax.experimental.pallas import tpu as pltpu
from jax.sharding import PartitionSpec as P

BF16 = jnp.bfloat16
F32 = jnp.float32
CORES = 2
CHIPS_Z = 4
LANES = 128
PARTS = 2
VMEM = 24 * 1024 * 1024
WIDE = 56 * 1024 * 1024
SMALL = 8 * 1024 * 1024


def moments(weight, first, second, grad):
    new_first = 0.9 * first + 0.1 * grad
    new_second = 0.95 * second + 0.05 * grad * grad
    update = new_first / (jnp.sqrt(new_second) + 1e-06) + 0.05 * weight
    return (new_first, new_second, update)


def squares(value):
    return jnp.sum(value * value)


def gelu(value):
    return 0.5 * value * (1.0 + lax.erf(value * (1.0 / math.sqrt(2.0))))


def gelu_slope(value):
    cdf = 0.5 * (1.0 + lax.erf(value * (1.0 / math.sqrt(2.0))))
    return cdf + value * (jnp.exp(-0.5 * value * value) * (1.0 / math.sqrt(2.0 * math.pi)))


def widths(shard):
    if shard % LANES:
        return (shard,)
    first = shard // LANES * 3 // 5 * LANES
    return (first, shard - first)


def dot(left, right, dims):
    return lax.dot_general(left, right, (dims, ((), ())), preferred_element_type=F32)


def params(grant=VMEM):
    return dict(
        compiler_params=pltpu.CompilerParams(vmem_limit_bytes=grant),
        cost_estimate=pl.CostEstimate(flops=1, bytes_accessed=1, transcendentals=0),
    )


def pack(hidden, cotangent, at, nz, nx, cuts):
    tokens, hidden_width = hidden.shape
    model = cotangent.shape[1]
    shard = hidden_width // (nz * nx)
    first = cuts[0]
    if shard % LANES:
        parts = [
            lax.dynamic_slice_in_dim(hidden, (z * nx + at) * shard, shard, 1).T for z in range(nz)
        ]
        return jnp.concatenate([cotangent.T, *parts])

    def body(at_ref, h_ref, cot_ref, out_ref):
        z = pl.program_id(0)

        @pl.when(z == 0)
        def _():
            out_ref[:model] = cot_ref[...].T

        out_ref[pl.ds(pl.multiple_of(model + z * first, LANES), first)] = h_ref[:, :first].T

    total = model + nz * first
    return pl.pallas_call(
        body,
        grid_spec=pltpu.PrefetchScalarGridSpec(
            num_scalar_prefetch=1,
            grid=(nz,),
            in_specs=[
                pl.BlockSpec((tokens, shard), lambda z, a: (0, z * nx + a[0])),
                pl.BlockSpec((tokens, model), lambda z, a: (0, 0)),
            ],
            out_specs=pl.BlockSpec((total, tokens), lambda z, a: (0, 0)),
        ),
        out_shape=jax.ShapeDtypeStruct((total, tokens), BF16),
        **params(WIDE),
    )(jnp.reshape(at, (1,)).astype(jnp.int32), hidden, cotangent)


def pack_later(hidden, at, nz, nx, cuts):
    tokens, hidden_width = hidden.shape
    shard = hidden_width // (nz * nx)
    if len(cuts) == 1:
        return []

    def body(at_ref, h_ref, *out_refs):
        start = cuts[0]
        for width, out_ref in zip(cuts[1:], out_refs):
            out_ref[0] = h_ref[:, start : start + width].T
            start += width

    return pl.pallas_call(
        body,
        grid_spec=pltpu.PrefetchScalarGridSpec(
            num_scalar_prefetch=1,
            grid=(nz,),
            in_specs=[pl.BlockSpec((tokens, shard), lambda z, a: (0, z * nx + a[0]))],
            out_specs=[pl.BlockSpec((1, w, tokens), lambda z, a: (z, 0, 0)) for w in cuts[1:]],
        ),
        out_shape=[jax.ShapeDtypeStruct((nz, w, tokens), BF16) for w in cuts[1:]],
        **params(WIDE),
    )(jnp.reshape(at, (1,)).astype(jnp.int32), hidden)


class Tokens:
    def __init__(self, packs, hiddens, model, nz, width):
        tokens = packs[0].shape[1]
        self.model, self.width, self.count = model, width, len(packs)
        if hiddens is None:
            self.arrays = list(packs)
            self.specs = [pl.BlockSpec(packs[0].shape, lambda z, c: (0, 0))] * len(packs)
        else:
            self.arrays = [*packs, *hiddens]
            self.specs = [pl.BlockSpec((model, tokens), lambda z, c: (0, 0))] * len(packs)
            self.specs += [pl.BlockSpec((1, width, tokens), lambda z, c: (z, 0, 0))] * len(packs)

    def cot(self, refs, n):
        return refs[n].at[: self.model]

    def hidden(self, refs, n):
        if len(refs) == self.count:
            row = self.model + pl.program_id(0) * self.width
            return refs[n][pl.ds(pl.multiple_of(row, 16), self.width)].astype(F32)
        return refs[self.count + n][0].astype(F32)


def grad_out_chunk(tokens, core, nz, scale, parts):
    width, model = tokens.width, tokens.model
    half = model // CORES
    high = width // parts
    count = len(tokens.arrays)

    def body(c_ref, *refs):
        ins, outs = refs[:count], refs[count:]
        acts = jnp.concatenate(
            [gelu(tokens.hidden(ins, n)).astype(BF16) for n in range(tokens.count)], axis=1
        )
        for which in range(2):
            cols = pl.ds(pl.multiple_of((c_ref[0] + 1 + which) % CORES * half, 16), half)
            right = jnp.concatenate([tokens.cot(ins, n)[cols, :] for n in range(tokens.count)], axis=1)
            total = (dot(acts, right, ((1,), (1,))) * scale).astype(BF16)
            for p in range(parts):
                value = total[p * high : (p + 1) * high]
                if which:
                    outs[parts][p, 0] = value
                else:
                    outs[p][0] = value

    return pl.pallas_call(
        body,
        grid_spec=pltpu.PrefetchScalarGridSpec(
            num_scalar_prefetch=1,
            grid=(nz,),
            in_specs=tokens.specs,
            out_specs=[pl.BlockSpec((1, high, half), lambda z, c: (z, 0, 0))] * parts
            + [pl.BlockSpec((parts, 1, high, half), lambda z, c: (0, z, 0, 0))],
        ),
        out_shape=[jax.ShapeDtypeStruct((nz, high, half), BF16)] * parts
        + [jax.ShapeDtypeStruct((parts, nz, high, half), BF16)],
        **params(),
    )(core, *tokens.arrays)


def grad_pre_chunk(tokens, weights, row, core, scale):
    nz, shard, model = weights.shape
    width = tokens.width
    count = len(tokens.arrays)
    long = tokens.arrays[0].shape[1]

    def body(c_ref, *refs):
        ins = refs[:count]
        w_ref, out_ref = refs[count:]
        w = w_ref[0, row : row + width, :]
        for n in range(tokens.count):
            grad_act = dot(w, tokens.cot(ins, n)[...], ((1,), (0,))) * scale
            out_ref[0, :, n * long : (n + 1) * long] = (
                grad_act * gelu_slope(tokens.hidden(ins, n))
            ).astype(BF16)

    return pl.pallas_call(
        body,
        grid_spec=pltpu.PrefetchScalarGridSpec(
            num_scalar_prefetch=1,
            grid=(nz,),
            in_specs=tokens.specs + [pl.BlockSpec((1, shard, model), lambda z, c: (z, 0, 0))],
            out_specs=pl.BlockSpec((1, width, tokens.count * long), lambda z, c: (z, 0, 0)),
        ),
        out_shape=jax.ShapeDtypeStruct((nz, width, tokens.count * long), BF16),
        **params(),
    )(core, *tokens.arrays, weights)


def grad_in_chunk(grads, inputs, core, scale, cut, block, width):
    nz, _, long = grads.shape
    model, tokens = inputs[0].shape
    count = len(inputs)
    half = nz // CORES
    high = model // cut

    def body(c_ref, g_ref, *refs):
        in_refs, outs = refs[:count], refs[count:]
        left = jnp.concatenate([i[...] for i in in_refs], axis=1)
        total = (dot(left, g_ref[0], ((1,), (1,))) * scale).astype(BF16)
        step = pl.program_id(0)
        for n in range(half):

            @pl.when(step == n)
            def _(n=n):
                for h in range(cut):
                    outs[n * cut + h][...] = total[h * high : (h + 1) * high]

        @pl.when(step >= half)
        def _():
            outs[-1][0] = total

    return pl.pallas_call(
        body,
        grid_spec=pltpu.PrefetchScalarGridSpec(
            num_scalar_prefetch=1,
            grid=(nz,),
            in_specs=[
                pl.BlockSpec(
                    (1, width, long),
                    lambda z, c: ((c[0] + 1 + z // half) % CORES * half + z % half, block, 0),
                )
            ]
            + [pl.BlockSpec((model, tokens), lambda z, c: (0, 0))] * count,
            out_specs=[pl.BlockSpec((high, width), lambda z, c: (0, 0))] * (half * cut)
            + [pl.BlockSpec((1, model, width), lambda z, c: (jnp.maximum(z - half, 0), 0, 0))],
        ),
        out_shape=[jax.ShapeDtypeStruct((high, width), BF16)] * (half * cut)
        + [jax.ShapeDtypeStruct((half, model, width), BF16)],
        **params(),
    )(core, grads, *inputs)


def transposed(value):
    rows, cols = value.shape
    wide = 2 * LANES

    def body(in_ref, out_ref):
        out_ref[...] = in_ref[...].T

    return pl.pallas_call(
        body,
        grid=(cols // wide,),
        in_specs=[pl.BlockSpec((rows, wide), lambda n: (0, n))],
        out_specs=pl.BlockSpec((wide, rows), lambda n: (n, 0)),
        out_shape=jax.ShapeDtypeStruct((cols, rows), value.dtype),
        **params(),
    )(value)


def half_rows(weight, core):
    rows, cols = weight.shape
    high = rows // CORES // 2

    def body(c_ref, in_ref, out_ref):
        out_ref[...] = in_ref[...].astype(BF16)

    return pl.pallas_call(
        body,
        grid_spec=pltpu.PrefetchScalarGridSpec(
            num_scalar_prefetch=1,
            grid=(2,),
            in_specs=[pl.BlockSpec((high, cols), lambda n, c: (c[0] * 2 + n, 0))],
            out_specs=pl.BlockSpec((high, cols), lambda n, c: (n, 0)),
        ),
        out_shape=jax.ShapeDtypeStruct((2 * high, cols), BF16),
        **params(WIDE),
    )(core, weight)


def stack(pieces, places, inner=False):
    count = len(pieces)
    shape = pieces[0].shape
    out = (shape[0], count, *shape[1:]) if inner else (count, *shape)

    def body(at_ref, *refs):
        for n in range(count):
            if inner:
                for p in range(shape[0]):
                    refs[count][p, at_ref[n]] = refs[n][p]
            else:
                refs[count][at_ref[n]] = refs[n][...]

    return pl.pallas_call(
        body,
        grid_spec=pltpu.PrefetchScalarGridSpec(
            num_scalar_prefetch=1,
            grid=(),
            in_specs=[pl.BlockSpec(shape, lambda at: (0,) * len(shape))] * count,
            out_specs=pl.BlockSpec(out, lambda at: (0,) * len(out)),
        ),
        out_shape=jax.ShapeDtypeStruct(out, pieces[0].dtype),
        **params(SMALL),
    )(places, *pieces)


def add_tiles(tiles):
    def body(*refs):
        refs[-1][...] = sum(ref[...] for ref in refs[:-1])

    return pl.pallas_call(
        body, out_shape=jax.ShapeDtypeStruct(tiles[0].shape, F32), **params(SMALL)
    )(*tiles)


def reduce_step(place, keep, crosses, from_y, shift, ny):
    lead, nz, mid, _, high, wide = keep.shape
    six = (lead, 1, mid, 1, high, wide)
    five = (lead, 1, mid, high, wide)
    each = len(crosses) // lead
    long = nz // each
    ends = len(from_y) > 0
    specs = [pl.BlockSpec(six, lambda n, at: (0, n, 0, (at[1] + shift) % ny, 0, 0))]
    for h in range(len(crosses)):
        specs.append(
            pl.BlockSpec(
                six[1:],
                lambda n, at, h=h % each: (
                    jnp.clip(n - h * long, 0, long - 1),
                    0,
                    (at[1] + shift) % ny,
                    0,
                    0,
                ),
            )
        )
    specs += [pl.BlockSpec(five, lambda n, at: (0, n, 0, 0, 0))] * len(from_y)

    def body(at_ref, *refs):
        ins, out_ref = refs[:-1], refs[-1]
        for p in range(lead):
            for m in range(mid):
                total = ins[1 + p * each][0, m, 0]
                for h in range(1, each):
                    total = jnp.where(pl.program_id(0) >= h * long, ins[1 + p * each + h][0, m, 0], total)
                total = total.astype(F32) + ins[0][p, 0, m, 0].astype(F32)
                for ref in ins[1 + len(crosses) :]:
                    total = total + ref[p, 0, m].astype(F32)
                if ends:
                    out_ref[0, p, m] = total.astype(BF16)
                else:
                    out_ref[p, 0, m] = total.astype(BF16)

    if ends:
        out_spec = pl.BlockSpec((1, lead, mid, high, wide), lambda n, at: (n, 0, 0, 0, 0))
        shape = (nz, lead, mid, high, wide)
    else:
        out_spec = pl.BlockSpec(five, lambda n, at: (0, n, 0, 0, 0))
        shape = (lead, nz, mid, high, wide)
    return pl.pallas_call(
        body,
        grid_spec=pltpu.PrefetchScalarGridSpec(
            num_scalar_prefetch=1, grid=(nz,), in_specs=specs, out_specs=out_spec
        ),
        out_shape=jax.ShapeDtypeStruct(shape, BF16),
        **params(SMALL),
    )(place, keep, *crosses, *from_y)


def by_x(place, value):
    lead, mid, high, wide = value.shape

    def body(at_ref, in_ref, *outs):
        for s in range(mid):
            outs[s][...] = in_ref[:, (at_ref[0] + s) % mid]

    return pl.pallas_call(
        body,
        grid_spec=pltpu.PrefetchScalarGridSpec(
            num_scalar_prefetch=1,
            grid=(),
            in_specs=[pl.BlockSpec(value.shape, lambda at: (0, 0, 0, 0))],
            out_specs=[pl.BlockSpec((lead, high, wide), lambda at: (0, 0, 0))] * mid,
        ),
        out_shape=[jax.ShapeDtypeStruct((lead, high, wide), BF16)] * mid,
        **params(SMALL),
    )(place, value)


def moments_kernel(core, weight, first, second, mine, other, grid, state_spec, grad_specs, owner, axis, tiles):
    block = state_spec.block_shape
    count = len(mine)
    long = 16 * (1 + len(tiles))

    def body(c_ref, w_ref, m_ref, v_ref, *refs):
        mine_refs, other_refs = refs[:count], refs[count : 2 * count]
        tile_refs = refs[2 * count : 2 * count + len(tiles)]
        new_m_ref, new_v_ref, u_ref, sum_ref = refs[2 * count + len(tiles) :]
        totals = [jnp.zeros((8, LANES), F32)] * 2
        start = 0
        ours = owner(pl.program_id(0)) == c_ref[0]
        for mine_ref, other_ref in zip(mine_refs, other_refs):
            size = mine_ref.size // block[1 - axis]
            shape = (size, block[1]) if axis == 0 else (block[0], size)
            at = (slice(start, start + size), slice(None))
            at = at if axis == 0 else at[::-1]
            grad = jnp.where(ours, mine_ref[...].reshape(shape), other_ref[...].reshape(shape)).astype(F32)
            weight = w_ref[at]
            new_m, new_v, update = moments(weight, m_ref[at], v_ref[at], grad)
            new_m_ref[at] = new_m
            new_v_ref[at] = new_v
            u_ref[at] = update
            for n, value in enumerate((weight, update)):
                square = value * value
                for col in range(0, shape[1], LANES):
                    totals[n] = totals[n] + square[:, col : col + LANES].reshape(-1, 8, LANES).sum(0)
            start += size

        @pl.when(pl.program_id(0) == 0)
        def _():
            sum_ref[:16] = jnp.zeros((16, LANES), F32)
            for n, tile_ref in enumerate(tile_refs):
                sum_ref[16 * (n + 1) : 16 * (n + 2)] = tile_ref[...]

        sum_ref[:8] += totals[0]
        sum_ref[8:16] += totals[1]

    state = jax.ShapeDtypeStruct(weight.shape, F32)
    return pl.pallas_call(
        body,
        grid_spec=pltpu.PrefetchScalarGridSpec(
            num_scalar_prefetch=1,
            grid=grid,
            in_specs=[state_spec] * 3
            + grad_specs * 2
            + [pl.BlockSpec((16, LANES), lambda n, c: (0, 0))] * len(tiles),
            out_specs=[state_spec] * 3 + [pl.BlockSpec((long, LANES), lambda n, c: (0, 0))],
        ),
        out_shape=[state] * 3 + [jax.ShapeDtypeStruct((long, LANES), F32)],
        **params(),
    )(core, weight, first, second, *mine, *other, *tiles)


def step_weights(weight, update, tiles, at):
    rows, cols = weight.shape
    high = rows // 5
    count = len(tiles)

    def body(w_ref, u_ref, *refs):
        sums = sum(ref[at : at + 16] for ref in refs[:count])
        ratio = jnp.sqrt(jnp.sum(sums[:8], keepdims=True)) / jnp.sqrt(jnp.sum(sums[8:], keepdims=True))
        refs[count][...] = w_ref[...] - 0.4 * ratio * u_ref[...]

    spec = pl.BlockSpec((high, cols), lambda n: (n, 0))
    tile = pl.BlockSpec(tiles[0].shape, lambda n: (0, 0))
    return pl.pallas_call(
        body,
        grid=(rows // high,),
        in_specs=[spec] * 2 + [tile] * count,
        out_specs=spec,
        out_shape=jax.ShapeDtypeStruct(weight.shape, F32),
        **params(),
    )(weight, update, *tiles)


class Order:
    def __init__(self):
        self.last = None

    def after(self, *values):
        if self.last is None:
            return values
        return lax.optimization_barrier((*values, self.last))[:-1]

    def did(self, value):
        self.last = value


def plan(nz, nx, ny):
    def along_x(value, step):
        pairs = [
            (z * nx + x, z * nx + (x + step) % nx) for z in range(nz) for x in range(nx)
        ]
        return lax.ppermute(value, "gx", pairs)

    def along_z(value, flip):
        pairs = [(z * nx + x, (z ^ flip) * nx + x) for z in range(nz) for x in range(nx)]
        return lax.ppermute(value, "gx", pairs)

    def along_y(value, step):
        pairs = [
            (y * CORES + c, (y + step) % ny * CORES + c) for y in range(ny) for c in range(CORES)
        ]
        return lax.ppermute(value, "gy", pairs)

    def across(value):
        pairs = [(k, k ^ 1) for k in range(ny * CORES)]
        return lax.ppermute(value, "gy", pairs)

    class Reduce:
        def __init__(self, order, at, sends, keep, shape):
            self.order, self.at, self.place = order, at, jnp.stack(at).astype(jnp.int32)
            self.keep = keep.reshape(shape)
            each = len(sends) // shape[0]
            self.crosses = [
                across(send).reshape(shape[1] // each, *shape[2:]) for send in sends
            ]
            self.from_y = []

        def step(self, shift):
            got = self.order.after(self.keep, *self.crosses, *self.from_y)
            lead = 1 + len(self.crosses)
            out = reduce_step(self.place, got[0], got[1:lead], got[lead:], shift, ny)
            self.order.did(out)
            return out

        def send_y(self):
            self.from_y = [along_y(self.step(s), s) for s in range(1, ny)]

        def sum_z(self):
            groups = [[z * nx + x for z in range(nz)] for x in range(nx)]
            self.total = lax.psum_scatter(self.step(0), "gx", axis_index_groups=groups)

        def finish(self):
            if self.total.shape[1] == 1:
                self.share_y(self.total[:, 0])
                return
            out = by_x(self.place, *self.order.after(self.total))
            self.order.did(out[0])
            self.held = [out[0]] + [along_x(out[s], s) for s in range(1, len(out))]

        def share_y(self, value):
            self.held = [value] + [along_y(value, s) for s in range(1, ny)]

        def stacked(self, place, size, inner=False):
            places = jnp.stack([(place - s) % size for s in range(size)]).astype(jnp.int32)
            value = stack(self.order.after(*self.held), places, inner)
            self.order.did(value)
            return value

        def stack_x(self):
            self.share_y(self.stacked(self.at[0], nx))

        def stack_y(self, inner=False):
            value = self.stacked(self.at[1], ny, inner)
            self.held = [value, across(value)]

    def local(inputs, hidden_pre, cotangent, w_in, m_in, v_in, w_out, m_out, v_out):
        model = inputs.shape[1]
        hidden_width = hidden_pre.shape[1]
        shard = hidden_width // (nz * nx)
        rows = model // (nz * nx)
        cuts = widths(shard)
        chunks = range(len(cuts))
        last = len(cuts) - 1
        starts = [sum(cuts[:k]) for k in chunks]
        scale_in = 1.0 / math.sqrt(model)
        scale_out = 1.0 / math.sqrt(hidden_width)
        place = lax.axis_index("gx")
        side = lax.axis_index("gy")
        z, x = place // nx, place % nx
        y, c = side // CORES, side % CORES
        core = jnp.reshape(c, (1,)).astype(jnp.int32)
        order = Order()

        packs, hiddens = [], []
        for t in range(1, nx):
            sent = pack(*order.after(hidden_pre, cotangent), (x + t) % nx, nz, nx, cuts)
            order.did(sent)
            packs.append(along_x(sent, t))

        part = half_rows(*order.after(w_out), core)
        order.did(part)
        groups = [
            [((z * nx + x) * ny + y) * CORES + c for z in range(nz) for c in range(CORES)]
            for x in range(nx)
            for y in range(ny)
        ]
        weights = lax.all_gather(part, ("gx", "gy"), axis_index_groups=groups)
        weights = weights.reshape(nz, shard, model)
        flipped = transposed(*order.after(inputs))
        order.did(flipped)
        columns = [flipped] + [along_x(flipped, t) for t in range(1, nx)]
        own = pack(*order.after(hidden_pre, cotangent), x, nz, nx, cuts)
        order.did(own)
        for t in range(nx):
            value = pack_later(*order.after(hidden_pre), (x + t) % nx, nz, nx, cuts)
            if value:
                order.did(value[0])
            hiddens.append([along_x(h, t) for h in value] if t else value)
        packs = [own] + packs

        parts = [PARTS for _ in chunks]
        outs = [None for _ in chunks]
        pieces_in = [(0, 0, cuts[0])]
        if last:
            pieces_in.append((1, 0, cuts[1]))
        ins = [None for _ in pieces_in]
        pres = [None for _ in chunks]

        def tokens(k, *more):
            later = [] if k == 0 else [value[k - 1] for value in hiddens]
            got = order.after(*packs, *later, *more)
            count = nx + len(later)
            blocks = Tokens(got[:nx], got[nx:count] if later else None, model, nz, cuts[k])
            return blocks, got[count:]

        def start_out(k):
            blocks, _ = tokens(k)
            *sends, keep = grad_out_chunk(blocks, core, nz, scale_out, parts[k])
            order.did(keep)
            shape = (parts[k], nz, 1, ny, cuts[k] // parts[k] // ny, model // CORES)
            outs[k] = Reduce(order, (x, y, z), sends, keep, shape)

        def start_pre(k):
            blocks, got = tokens(k, weights)
            pres[k] = grad_pre_chunk(blocks, got[0], starts[k], core, scale_out)
            order.did(pres[k])

        def start_in(k):
            chunk, block, width = pieces_in[k]
            got = order.after(pres[chunk], *columns)
            *sends, keep = grad_in_chunk(
                got[0], got[1:], core, scale_in, 1, block, width
            )
            order.did(keep)
            shape = (nz // CORES, nz, nx, ny, rows // ny, width)
            ins[k] = Reduce(order, (x, y, z), sends, keep, shape)

        def sums(tile):
            tiles = order.after(tile, *[along_z(tile, flip) for flip in range(1, nz)])
            tile = add_tiles(tiles)
            order.did(tile)
            return [tile] + [along_x(tile, t) for t in range(1, nx)]

        def new_weights(weight, update, tiles, at):
            got = order.after(weight, update, *tiles)
            value = step_weights(got[0], got[1], got[2:], at)
            order.did(value)
            return value

        def moments_out(tile):
            half = model // CORES
            got = order.after(
                w_out,
                m_out,
                v_out,
                tile,
                *[outs[k].held[0] for k in chunks],
                *[outs[k].held[1] for k in chunks],
            )
            new = moments_kernel(
                core,
                *got[:3],
                got[4 : 5 + last],
                got[5 + last :],
                (CORES,),
                pl.BlockSpec((shard, half), lambda n, c: (0, n)),
                [
                    pl.BlockSpec((p, ny, w // p // ny, half), lambda n, c: (0, 0, 0, 0))
                    for w, p in zip(cuts, parts)
                ],
                lambda n: n,
                0,
                [got[3]],
            )
            order.did(new[3])
            return new

        start_out(0)
        outs[0].send_y()
        start_pre(0)
        start_in(0)
        outs[0].sum_z()
        ins[0].send_y()
        if last:
            start_pre(1)
            start_in(1)
            start_out(1)
            ins[1].send_y()
            ins[0].sum_z()
            outs[1].send_y()
            ins[1].sum_z()
            outs[0].finish()
            outs[0].stack_y(True)
            ins[0].finish()
            ins[0].stack_x()
            outs[1].sum_z()
            ins[0].stack_y()
            ins[1].finish()
            ins[1].stack_x()
            ins[1].stack_y()
            outs[1].finish()
        else:
            ins[0].sum_z()
            outs[0].finish()
            ins[0].finish()
            ins[0].stack_x()
            ins[0].stack_y()

        held = [value.held for value in ins]
        got = order.after(w_in, m_in, v_in, *[pair[0] for pair in held], *[pair[1] for pair in held])
        mine, other = got[3 : 3 + len(ins)], got[3 + len(ins) :]
        if shard % LANES:
            joined = [
                jnp.stack([jnp.where(c == 0, a, b), jnp.where(c == 0, b, a)]) for a, b in zip(mine, other)
            ]
            grad = jnp.concatenate(joined, axis=-1).transpose(1, 4, 0, 3, 2, 5)
            grad = grad.reshape(rows, hidden_width).astype(F32)
            first_in, second_in, update_in = moments(*got[:3], grad)
            tile = jnp.concatenate(
                [
                    jnp.sum((value * value).reshape(-1, 8, LANES), axis=0)
                    for value in (w_in, update_in)
                ]
            )
        else:
            zs = nz // CORES
            first_in, second_in, update_in, tile = moments_kernel(
                core,
                *got[:3],
                mine,
                other,
                (nz * nx,),
                pl.BlockSpec((rows, shard), lambda n, c: (0, n)),
                [
                    pl.BlockSpec(
                        (ny, 1, 1, rows // ny, w), lambda n, c: (0, n % nx, n // nx % zs, 0, 0)
                    )
                    for _, _, w in pieces_in
                ],
                lambda n: n // nx // zs,
                1,
                [],
            )
        order.did(tile)

        outs[last].stack_y(True)
        first_out, second_out, update_out, tile = moments_out(tile)
        tiles = sums(tile)
        new_w_in = new_weights(w_in, update_in, tiles, 16)
        new_w_out = new_weights(w_out, update_out, tiles, 0)
        return (new_w_in, first_in, second_in, new_w_out, first_out, second_out)

    return local


def solution(mesh):
    gx, gy = mesh.shape["gx"], mesh.shape["gy"]
    nz = CHIPS_Z
    state = P("gx", None)
    tokens = P(("gx", "gy"), None)
    return jax.shard_map(
        plan(nz, gx // nz, gy // CORES),
        mesh=mesh,
        in_specs=(tokens,) * 3 + (state,) * 6,
        out_specs=(state,) * 6,
        check_vma=False,
    )
```

```python
import functools
import math

import jax
import jax.numpy as jnp
from jax import lax
from jax.experimental import pallas as pl
from jax.experimental.pallas import tpu as pltpu
from jax.sharding import PartitionSpec as P

BF16 = jnp.bfloat16
F32 = jnp.float32
CORES = 2
CHIPS_Z = 4
LANES = 128
PARTS = 2
VMEM = 20 * 1024 * 1024
WIDE = 56 * 1024 * 1024
SMALL = 4 * 1024 * 1024


def moments(weight, first, second, grad):
    new_first = 0.9 * first + 0.1 * grad
    new_second = 0.95 * second + 0.05 * grad * grad
    update = new_first / (jnp.sqrt(new_second) + 1e-06) + 0.05 * weight
    return (new_first, new_second, update)


def squares(value):
    return jnp.sum(value * value)


def gelu(value):
    return 0.5 * value * (1.0 + lax.erf(value * (1.0 / math.sqrt(2.0))))


def gelu_slope(value):
    cdf = 0.5 * (1.0 + lax.erf(value * (1.0 / math.sqrt(2.0))))
    return cdf + value * (jnp.exp(-0.5 * value * value) * (1.0 / math.sqrt(2.0 * math.pi)))


def widths(shard):
    if shard % LANES:
        return (shard,)
    first = shard // LANES * 3 // 5 * LANES
    return (first, shard - first)


def dot(left, right, dims):
    return lax.dot_general(left, right, (dims, ((), ())), preferred_element_type=F32)


def params(grant=VMEM):
    return dict(
        compiler_params=pltpu.CompilerParams(vmem_limit_bytes=grant),
        cost_estimate=pl.CostEstimate(flops=1, bytes_accessed=1, transcendentals=0),
    )


def pack(hidden, cotangent, at, nz, nx, cuts):
    tokens, hidden_width = hidden.shape
    model = cotangent.shape[1]
    shard = hidden_width // (nz * nx)
    first = cuts[0]
    if shard % LANES:
        parts = [
            lax.dynamic_slice_in_dim(hidden, (z * nx + at) * shard, shard, 1).T for z in range(nz)
        ]
        return jnp.concatenate([cotangent.T, *parts])

    def body(at_ref, h_ref, cot_ref, out_ref):
        z = pl.program_id(0)

        @pl.when(z == 0)
        def _():
            out_ref[:model] = cot_ref[...].T

        out_ref[pl.ds(pl.multiple_of(model + z * first, LANES), first)] = h_ref[:, :first].T

    total = model + nz * first
    return pl.pallas_call(
        body,
        grid_spec=pltpu.PrefetchScalarGridSpec(
            num_scalar_prefetch=1,
            grid=(nz,),
            in_specs=[
                pl.BlockSpec((tokens, shard), lambda z, a: (0, z * nx + a[0])),
                pl.BlockSpec((tokens, model), lambda z, a: (0, 0)),
            ],
            out_specs=pl.BlockSpec((total, tokens), lambda z, a: (0, 0)),
        ),
        out_shape=jax.ShapeDtypeStruct((total, tokens), BF16),
        **params(WIDE),
    )(jnp.reshape(at, (1,)).astype(jnp.int32), hidden, cotangent)


def pack_later(hidden, at, nz, nx, cuts):
    tokens, hidden_width = hidden.shape
    shard = hidden_width // (nz * nx)
    if len(cuts) == 1:
        return []

    def body(at_ref, h_ref, *out_refs):
        start = cuts[0]
        for width, out_ref in zip(cuts[1:], out_refs):
            out_ref[0] = h_ref[:, start : start + width].T
            start += width

    return pl.pallas_call(
        body,
        grid_spec=pltpu.PrefetchScalarGridSpec(
            num_scalar_prefetch=1,
            grid=(nz,),
            in_specs=[pl.BlockSpec((tokens, shard), lambda z, a: (0, z * nx + a[0]))],
            out_specs=[pl.BlockSpec((1, w, tokens), lambda z, a: (z, 0, 0)) for w in cuts[1:]],
        ),
        out_shape=[jax.ShapeDtypeStruct((nz, w, tokens), BF16) for w in cuts[1:]],
        **params(WIDE),
    )(jnp.reshape(at, (1,)).astype(jnp.int32), hidden)


class Tokens:
    def __init__(self, packs, hiddens, model, nz, width):
        tokens = packs[0].shape[1]
        self.model, self.width, self.count = model, width, len(packs)
        if hiddens is None:
            self.arrays = list(packs)
            self.specs = [pl.BlockSpec(packs[0].shape, lambda z, c: (0, 0))] * len(packs)
        else:
            self.arrays = [*packs, *hiddens]
            self.specs = [pl.BlockSpec((model, tokens), lambda z, c: (0, 0))] * len(packs)
            self.specs += [pl.BlockSpec((1, width, tokens), lambda z, c: (z, 0, 0))] * len(packs)

    def cot(self, refs, n):
        return refs[n].at[: self.model]

    def hidden(self, refs, n):
        if len(refs) == self.count:
            row = self.model + pl.program_id(0) * self.width
            return refs[n][pl.ds(pl.multiple_of(row, 16), self.width)].astype(F32)
        return refs[self.count + n][0].astype(F32)


def grad_out_chunk(tokens, core, nz, scale, parts):
    width, model = tokens.width, tokens.model
    half = model // CORES
    high = width // parts
    count = len(tokens.arrays)

    def body(c_ref, *refs):
        ins, outs = refs[:count], refs[count:]
        acts = jnp.concatenate(
            [gelu(tokens.hidden(ins, n)).astype(BF16) for n in range(tokens.count)], axis=1
        )
        for which in range(2):
            cols = pl.ds(pl.multiple_of((c_ref[0] + 1 + which) % CORES * half, 16), half)
            right = jnp.concatenate([tokens.cot(ins, n)[cols, :] for n in range(tokens.count)], axis=1)
            total = (dot(acts, right, ((1,), (1,))) * scale).astype(BF16)
            for p in range(parts):
                value = total[p * high : (p + 1) * high]
                if which:
                    outs[parts][p, 0] = value
                else:
                    outs[p][0] = value

    return pl.pallas_call(
        body,
        grid_spec=pltpu.PrefetchScalarGridSpec(
            num_scalar_prefetch=1,
            grid=(nz,),
            in_specs=tokens.specs,
            out_specs=[pl.BlockSpec((1, high, half), lambda z, c: (z, 0, 0))] * parts
            + [pl.BlockSpec((parts, 1, high, half), lambda z, c: (0, z, 0, 0))],
        ),
        out_shape=[jax.ShapeDtypeStruct((nz, high, half), BF16)] * parts
        + [jax.ShapeDtypeStruct((parts, nz, high, half), BF16)],
        **params(),
    )(core, *tokens.arrays)


def grad_pre_chunk(tokens, mine, other, nz, row, core, scale):
    part, model = mine[0].shape
    width = tokens.width
    count = len(tokens.arrays)
    long = tokens.arrays[0].shape[1]

    def body(c_ref, *refs):
        ins = refs[:count]
        out_ref, w_ref = refs[count + 2 * nz :]
        for h in range(nz):

            @pl.when((pl.program_id(0) ^ c_ref[1]) == h)
            def _(h=h):
                for at, ref in ((c_ref[0], refs[count + h]), (1 - c_ref[0], refs[count + nz + h])):
                    w_ref[pl.ds(pl.multiple_of(at * part, 16), part), :] = ref[...]

        w = w_ref[row : row + width, :]
        for n in range(tokens.count):
            grad_act = dot(w, tokens.cot(ins, n)[...], ((1,), (0,))) * scale
            out_ref[0, :, n * long : (n + 1) * long] = (
                grad_act * gelu_slope(tokens.hidden(ins, n))
            ).astype(BF16)

    w_specs = [pl.BlockSpec((part, model), lambda z, c: (0, 0))] * nz
    return pl.pallas_call(
        body,
        grid_spec=pltpu.PrefetchScalarGridSpec(
            num_scalar_prefetch=1,
            grid=(nz,),
            in_specs=tokens.specs + w_specs * 2,
            out_specs=pl.BlockSpec((1, width, tokens.count * long), lambda z, c: (z, 0, 0)),
            scratch_shapes=[pltpu.VMEM((CORES * part, model), BF16)],
        ),
        out_shape=jax.ShapeDtypeStruct((nz, width, tokens.count * long), BF16),
        **params(),
    )(core, *tokens.arrays, *mine, *other)


def grad_in_chunk(grads, inputs, core, scale, cut, block, width):
    nz, _, long = grads.shape
    model, tokens = inputs[0].shape
    count = len(inputs)
    half = nz // CORES
    high = model // cut

    def body(c_ref, g_ref, *refs):
        in_refs, outs = refs[:count], refs[count:]
        left = jnp.concatenate([i[...] for i in in_refs], axis=1)
        total = (dot(left, g_ref[0], ((1,), (1,))) * scale).astype(BF16)
        step = pl.program_id(0)
        for n in range(half):

            @pl.when(step == n)
            def _(n=n):
                for h in range(cut):
                    outs[n * cut + h][...] = total[h * high : (h + 1) * high]

        @pl.when(step >= half)
        def _():
            outs[-1][0] = total

    return pl.pallas_call(
        body,
        grid_spec=pltpu.PrefetchScalarGridSpec(
            num_scalar_prefetch=1,
            grid=(nz,),
            in_specs=[
                pl.BlockSpec(
                    (1, width, long),
                    lambda z, c: ((c[0] + 1 + z // half) % CORES * half + z % half, block, 0),
                )
            ]
            + [pl.BlockSpec((model, tokens), lambda z, c: (0, 0))] * count,
            out_specs=[pl.BlockSpec((high, width), lambda z, c: (0, 0))] * (half * cut)
            + [pl.BlockSpec((1, model, width), lambda z, c: (jnp.maximum(z - half, 0), 0, 0))],
        ),
        out_shape=[jax.ShapeDtypeStruct((high, width), BF16)] * (half * cut)
        + [jax.ShapeDtypeStruct((half, model, width), BF16)],
        **params(),
    )(core, grads, *inputs)


def transposed(value):
    rows, cols = value.shape
    wide = 2 * LANES

    def body(in_ref, out_ref):
        out_ref[...] = in_ref[...].T

    return pl.pallas_call(
        body,
        grid=(cols // wide,),
        in_specs=[pl.BlockSpec((rows, wide), lambda n: (0, n))],
        out_specs=pl.BlockSpec((wide, rows), lambda n: (n, 0)),
        out_shape=jax.ShapeDtypeStruct((cols, rows), value.dtype),
        **params(),
    )(value)


def half_rows(weight, core):
    rows, cols = weight.shape
    high = rows // CORES // 2

    def body(c_ref, in_ref, out_ref):
        out_ref[...] = in_ref[...].astype(BF16)

    return pl.pallas_call(
        body,
        grid_spec=pltpu.PrefetchScalarGridSpec(
            num_scalar_prefetch=1,
            grid=(2,),
            in_specs=[pl.BlockSpec((high, cols), lambda n, c: (c[0] * 2 + n, 0))],
            out_specs=pl.BlockSpec((high, cols), lambda n, c: (n, 0)),
        ),
        out_shape=jax.ShapeDtypeStruct((2 * high, cols), BF16),
        **params(WIDE),
    )(core, weight)


def stack(pieces, places, inner=False):
    count = len(pieces)
    shape = pieces[0].shape
    out = (shape[0], count, *shape[1:]) if inner else (count, *shape)

    def body(at_ref, *refs):
        for n in range(count):
            if inner:
                for p in range(shape[0]):
                    refs[count][p, at_ref[n]] = refs[n][p]
            else:
                refs[count][at_ref[n]] = refs[n][...]

    return pl.pallas_call(
        body,
        grid_spec=pltpu.PrefetchScalarGridSpec(
            num_scalar_prefetch=1,
            grid=(),
            in_specs=[pl.BlockSpec(shape, lambda at: (0,) * len(shape))] * count,
            out_specs=pl.BlockSpec(out, lambda at: (0,) * len(out)),
        ),
        out_shape=jax.ShapeDtypeStruct(out, pieces[0].dtype),
        **params(SMALL),
    )(places, *pieces)


def add_tiles(tiles):
    def body(*refs):
        refs[-1][...] = sum(ref[...] for ref in refs[:-1])

    return pl.pallas_call(
        body, out_shape=jax.ShapeDtypeStruct(tiles[0].shape, F32), **params(SMALL)
    )(*tiles)


def reduce_step(place, keep, crosses, from_y, from_z, shift, stage, ny, split):
    lead, nz, mid, _, high, wide = keep.shape
    bit = len(from_z)

    def zed(n, at):
        if stage == "y":
            return n
        if stage == "end":
            return at[2]
        low = at[2] % (1 << bit)
        mine = (at[2] // (1 << bit)) % 2
        return n * (2 << bit) + (1 - mine) * (1 << bit) + low

    count = {"y": nz, "z": nz >> (bit + 1), "end": 1}[stage]
    six = (lead, 1, mid, 1, high, wide)
    five = (lead, 1, mid, high, wide)
    specs = [pl.BlockSpec(six, lambda n, at: (0, zed(n, at), 0, (at[1] + shift) % ny, 0, 0))]
    each = len(crosses) // lead
    long = nz // each
    for h in range(len(crosses)):
        specs.append(
            pl.BlockSpec(
                six[1:],
                lambda n, at, h=h % each: (
                    jnp.clip(zed(n, at) - h * long, 0, long - 1),
                    0,
                    (at[1] + shift) % ny,
                    0,
                    0,
                ),
            )
        )
    specs += [pl.BlockSpec(five, lambda n, at: (0, zed(n, at), 0, 0, 0))] * len(from_y)
    specs += [
        pl.BlockSpec(five, lambda n, at, j=j: (0, zed(n, at) // (2 << j), 0, 0, 0)) for j in range(bit)
    ]

    def body(at_ref, *refs):
        ins = refs[: len(specs)]
        outs = refs[len(specs) :]
        for p in range(lead):
            for m in range(mid):
                total = ins[1 + p * each][0, m, 0]
                for h in range(1, each):
                    total = jnp.where(
                        zed(pl.program_id(0), at_ref) >= h * long, ins[1 + p * each + h][0, m, 0], total
                    )
                total = total.astype(F32) + ins[0][p, 0, m, 0].astype(F32)
                for ref in ins[1 + len(crosses) :]:
                    total = total + ref[p, 0, m].astype(F32)
                total = total.astype(BF16)
                if not split:
                    outs[0][p, 0, m] = total
                    continue
                for s in range(mid):

                    @pl.when((at_ref[0] + s) % mid == m)
                    def _(s=s, total=total):
                        outs[s][p] = total

    if split:
        out_specs = [pl.BlockSpec((lead, high, wide), lambda n, at: (0, 0, 0))] * mid
        out_shape = [jax.ShapeDtypeStruct((lead, high, wide), BF16)] * mid
    else:
        out_specs = [pl.BlockSpec(five, lambda n, at: (0, n, 0, 0, 0))]
        out_shape = [jax.ShapeDtypeStruct((lead, count, mid, high, wide), BF16)]
    out = pl.pallas_call(
        body,
        grid_spec=pltpu.PrefetchScalarGridSpec(
            num_scalar_prefetch=1, grid=(count,), in_specs=specs, out_specs=out_specs
        ),
        out_shape=out_shape,
        **params(SMALL),
    )(place, keep, *crosses, *from_y, *from_z)
    return out if split else out[0]


def moments_kernel(core, weight, first, second, mine, other, grid, state_spec, grad_specs, owner, axis, tiles):
    block = state_spec.block_shape
    count = len(mine)
    long = 16 * (1 + len(tiles))

    def body(c_ref, w_ref, m_ref, v_ref, *refs):
        mine_refs, other_refs = refs[:count], refs[count : 2 * count]
        tile_refs = refs[2 * count : 2 * count + len(tiles)]
        new_m_ref, new_v_ref, u_ref, sum_ref = refs[2 * count + len(tiles) :]
        totals = [jnp.zeros((8, LANES), F32)] * 2
        start = 0
        ours = owner(pl.program_id(0)) == c_ref[0]
        for mine_ref, other_ref in zip(mine_refs, other_refs):
            size = mine_ref.size // block[1 - axis]
            shape = (size, block[1]) if axis == 0 else (block[0], size)
            at = (slice(start, start + size), slice(None))
            at = at if axis == 0 else at[::-1]
            grad = jnp.where(ours, mine_ref[...].reshape(shape), other_ref[...].reshape(shape)).astype(F32)
            weight = w_ref[at]
            new_m, new_v, update = moments(weight, m_ref[at], v_ref[at], grad)
            new_m_ref[at] = new_m
            new_v_ref[at] = new_v
            u_ref[at] = update
            for n, value in enumerate((weight, update)):
                square = value * value
                for col in range(0, shape[1], LANES):
                    totals[n] = totals[n] + square[:, col : col + LANES].reshape(-1, 8, LANES).sum(0)
            start += size

        @pl.when(pl.program_id(0) == 0)
        def _():
            sum_ref[:16] = jnp.zeros((16, LANES), F32)
            for n, tile_ref in enumerate(tile_refs):
                sum_ref[16 * (n + 1) : 16 * (n + 2)] = tile_ref[...]

        sum_ref[:8] += totals[0]
        sum_ref[8:16] += totals[1]

    state = jax.ShapeDtypeStruct(weight.shape, F32)
    return pl.pallas_call(
        body,
        grid_spec=pltpu.PrefetchScalarGridSpec(
            num_scalar_prefetch=1,
            grid=grid,
            in_specs=[state_spec] * 3
            + grad_specs * 2
            + [pl.BlockSpec((16, LANES), lambda n, c: (0, 0))] * len(tiles),
            out_specs=[state_spec] * 3 + [pl.BlockSpec((long, LANES), lambda n, c: (0, 0))],
        ),
        out_shape=[state] * 3 + [jax.ShapeDtypeStruct((long, LANES), F32)],
        **params(),
    )(core, weight, first, second, *mine, *other, *tiles)


def step_weights(weight, update, tiles, at):
    rows, cols = weight.shape
    high = rows // 5
    count = len(tiles)

    def body(w_ref, u_ref, *refs):
        sums = sum(ref[at : at + 16] for ref in refs[:count])
        ratio = jnp.sqrt(jnp.sum(sums[:8], keepdims=True)) / jnp.sqrt(jnp.sum(sums[8:], keepdims=True))
        refs[count][...] = w_ref[...] - 0.4 * ratio * u_ref[...]

    spec = pl.BlockSpec((high, cols), lambda n: (n, 0))
    tile = pl.BlockSpec(tiles[0].shape, lambda n: (0, 0))
    return pl.pallas_call(
        body,
        grid=(rows // high,),
        in_specs=[spec] * 2 + [tile] * count,
        out_specs=spec,
        out_shape=jax.ShapeDtypeStruct(weight.shape, F32),
        **params(),
    )(weight, update, *tiles)


class Order:
    def __init__(self):
        self.last = None

    def after(self, *values):
        if self.last is None:
            return values
        return lax.optimization_barrier((*values, self.last))[:-1]

    def did(self, value):
        self.last = value


def plan(nz, nx, ny):
    def along_x(value, step):
        pairs = [
            (z * nx + x, z * nx + (x + step) % nx) for z in range(nz) for x in range(nx)
        ]
        return lax.ppermute(value, "gx", pairs)

    def along_z(value, flip):
        pairs = [(z * nx + x, (z ^ flip) * nx + x) for z in range(nz) for x in range(nx)]
        return lax.ppermute(value, "gx", pairs)

    def along_y(value, step):
        pairs = [
            (y * CORES + c, (y + step) % ny * CORES + c) for y in range(ny) for c in range(CORES)
        ]
        return lax.ppermute(value, "gy", pairs)

    def across(value):
        pairs = [(k, k ^ 1) for k in range(ny * CORES)]
        return lax.ppermute(value, "gy", pairs)

    class Reduce:
        def __init__(self, order, at, sends, keep, shape):
            self.order, self.at, self.place = order, at, jnp.stack(at).astype(jnp.int32)
            self.keep = keep.reshape(shape)
            each = len(sends) // shape[0]
            self.crosses = [
                across(send).reshape(shape[1] // each, *shape[2:]) for send in sends
            ]
            self.from_y = []
            self.from_z = []

        def step(self, shift, stage, split=False):
            got = self.order.after(self.keep, *self.crosses, *self.from_y, *self.from_z)
            lead = 1 + len(self.crosses)
            count = lead + len(self.from_y)
            out = reduce_step(
                self.place, got[0], got[1:lead], got[lead:count], got[count:], shift, stage, ny, split
            )
            self.order.did(out[0] if split else out)
            return out

        def send_y(self):
            from_y = []
            for s in range(1, ny):
                from_y.append(along_y(self.step(s, "y"), s))
            self.from_y = from_y

        def send_z(self):
            bit = len(self.from_z)
            self.from_z.append(along_z(self.step(0, "z"), 1 << bit))

        def finish(self):
            out = self.step(0, "end", True)
            self.held = [out[0]] + [along_x(out[s], s) for s in range(1, len(out))]
            if len(out) == 1:
                self.share_y(out[0])

        def share_y(self, value):
            self.held = [value] + [along_y(value, s) for s in range(1, ny)]

        def stacked(self, place, size, inner=False):
            places = jnp.stack([(place - s) % size for s in range(size)]).astype(jnp.int32)
            value = stack(self.order.after(*self.held), places, inner)
            self.order.did(value)
            return value

        def stack_x(self):
            self.share_y(self.stacked(self.at[0], nx))

        def stack_y(self, inner=False):
            value = self.stacked(self.at[1], ny, inner)
            self.held = [value, across(value)]

    def local(inputs, hidden_pre, cotangent, w_in, m_in, v_in, w_out, m_out, v_out):
        model = inputs.shape[1]
        hidden_width = hidden_pre.shape[1]
        shard = hidden_width // (nz * nx)
        rows = model // (nz * nx)
        cuts = widths(shard)
        chunks = range(len(cuts))
        last = len(cuts) - 1
        starts = [sum(cuts[:k]) for k in chunks]
        scale_in = 1.0 / math.sqrt(model)
        scale_out = 1.0 / math.sqrt(hidden_width)
        place = lax.axis_index("gx")
        side = lax.axis_index("gy")
        z, x = place // nx, place % nx
        y, c = side // CORES, side % CORES
        core = jnp.reshape(c, (1,)).astype(jnp.int32)
        at_core = jnp.stack([c, z]).astype(jnp.int32)
        order = Order()

        packs, hiddens = [], []
        for t in range(1, nx):
            sent = pack(*order.after(hidden_pre, cotangent), (x + t) % nx, nz, nx, cuts)
            order.did(sent)
            packs.append(along_x(sent, t))

        part = half_rows(*order.after(w_out), core)
        order.did(part)
        flipped = transposed(*order.after(inputs))
        order.did(flipped)
        columns = [flipped] + [along_x(flipped, t) for t in range(1, nx)]
        own = pack(*order.after(hidden_pre, cotangent), x, nz, nx, cuts)
        order.did(own)
        for t in range(nx):
            value = pack_later(*order.after(hidden_pre), (x + t) % nx, nz, nx, cuts)
            if value:
                order.did(value[0])
            hiddens.append([along_x(h, t) for h in value] if t else value)
        found = {0: part, nz // 2: along_z(part, nz // 2)}
        bit = nz // 4
        while bit:
            for key in list(found):
                value = found[key]
                if key:
                    (value,) = order.after(value)
                found[key ^ bit] = along_z(value, bit)
            bit //= 2
        found = [found[key] for key in range(nz)]
        crossed = [across(value) for value in [*order.after(*found[: nz // 2]), *found[nz // 2 :]]]
        packs = [own] + packs

        parts = [2] + [2] * last
        outs = [None for _ in chunks]
        pieces_in = [(0, 0, cuts[0])]
        if last:
            pieces_in.append((1, 0, cuts[1]))
        ins = [None for _ in pieces_in]
        pres = [None for _ in chunks]

        def tokens(k, *more):
            later = [] if k == 0 else [value[k - 1] for value in hiddens]
            got = order.after(*packs, *later, *more)
            count = nx + len(later)
            blocks = Tokens(got[:nx], got[nx:count] if later else None, model, nz, cuts[k])
            return blocks, got[count:]

        def start_out(k):
            blocks, _ = tokens(k, *([*crossed[: nz // 2], found[nz // 2]] if k == 0 else []))
            *sends, keep = grad_out_chunk(blocks, core, nz, scale_out, parts[k])
            order.did(keep)
            shape = (parts[k], nz, 1, ny, cuts[k] // parts[k] // ny, model // CORES)
            outs[k] = Reduce(order, (x, y, z), sends, keep, shape)

        def start_pre(k):
            blocks, got = tokens(k, *found, *crossed)
            pres[k] = grad_pre_chunk(blocks, got[:nz], got[nz:], nz, starts[k], at_core, scale_out)
            order.did(pres[k])

        def start_in(k):
            chunk, block, width = pieces_in[k]
            got = order.after(pres[chunk], *columns)
            *sends, keep = grad_in_chunk(
                got[0], got[1:], core, scale_in, (1 if chunk else 1), block, width
            )
            order.did(keep)
            shape = (nz // CORES, nz, nx, ny, rows // ny, width)
            ins[k] = Reduce(order, (x, y, z), sends, keep, shape)

        def sums(tile):
            tiles = order.after(tile, *[along_z(tile, flip) for flip in range(1, nz)])
            tile = add_tiles(tiles)
            order.did(tile)
            return [tile] + [along_x(tile, t) for t in range(1, nx)]

        def new_weights(weight, update, tiles, at):
            got = order.after(weight, update, *tiles)
            value = step_weights(got[0], got[1], got[2:], at)
            order.did(value)
            return value

        def moments_out(tile):
            half = model // CORES
            got = order.after(
                w_out,
                m_out,
                v_out,
                tile,
                *[outs[k].held[0] for k in chunks],
                *[outs[k].held[1] for k in chunks],
            )
            new = moments_kernel(
                core,
                *got[:3],
                got[4 : 5 + last],
                got[5 + last :],
                (CORES,),
                pl.BlockSpec((shard, half), lambda n, c: (0, n)),
                [
                    pl.BlockSpec((p, ny, w // p // ny, half), lambda n, c: (0, 0, 0, 0))
                    for w, p in zip(cuts, parts)
                ],
                lambda n: n,
                0,
                [got[3]],
            )
            order.did(new[3])
            return new

        start_out(0)
        outs[0].send_y()
        start_pre(0)
        start_in(0)
        outs[0].send_z()
        ins[0].send_y()
        if last:
            start_pre(1)
            start_in(1)
            outs[0].send_z()
            start_out(1)
            ins[1].send_y()
            ins[0].send_z()
            outs[1].send_y()
            ins[1].send_z()
            ins[0].send_z()
            ins[1].send_z()
            outs[0].finish()
            outs[1].send_z()
            ins[0].finish()
            outs[0].stack_y(True)
            ins[0].stack_x()
            ins[1].finish()
            outs[1].send_z()
            ins[0].stack_y()
            ins[1].stack_x()
            outs[1].finish()
            ins[1].stack_y()
        else:
            outs[0].send_z()
            ins[0].send_z()
            outs[0].finish()
            ins[0].send_z()
            ins[0].finish()
            ins[0].stack_x()
            ins[0].stack_y()

        held = [value.held for value in ins]
        got = order.after(w_in, m_in, v_in, *[pair[0] for pair in held], *[pair[1] for pair in held])
        mine, other = got[3 : 3 + len(ins)], got[3 + len(ins) :]
        if shard % LANES:
            joined = [
                jnp.stack([jnp.where(c == 0, a, b), jnp.where(c == 0, b, a)]) for a, b in zip(mine, other)
            ]
            grad = jnp.concatenate(joined, axis=-1).transpose(1, 4, 0, 3, 2, 5)
            grad = grad.reshape(rows, hidden_width).astype(F32)
            first_in, second_in, update_in = moments(*got[:3], grad)
            tile = jnp.concatenate(
                [
                    jnp.sum((value * value).reshape(-1, 8, LANES), axis=0)
                    for value in (w_in, update_in)
                ]
            )
        else:
            zs = nz // CORES
            first_in, second_in, update_in, tile = moments_kernel(
                core,
                *got[:3],
                mine,
                other,
                (nz * nx,),
                pl.BlockSpec((rows, shard), lambda n, c: (0, n)),
                [
                    pl.BlockSpec(
                        (ny, 1, 1, rows // ny, w), lambda n, c: (0, n % nx, n // nx % zs, 0, 0)
                    )
                    for _, _, w in pieces_in
                ],
                lambda n: n // nx // zs,
                1,
                [],
            )
        order.did(tile)

        outs[last].stack_y(True)
        first_out, second_out, update_out, tile = moments_out(tile)
        tiles = sums(tile)
        new_w_in = new_weights(w_in, update_in, tiles, 16)
        new_w_out = new_weights(w_out, update_out, tiles, 0)
        return (new_w_in, first_in, second_in, new_w_out, first_out, second_out)

    return local


def solution(mesh):
    gx, gy = mesh.shape["gx"], mesh.shape["gy"]
    nz = CHIPS_Z
    state = P("gx", None)
    tokens = P(("gx", "gy"), None)
    return jax.shard_map(
        plan(nz, gx // nz, gy // CORES),
        mesh=mesh,
        in_specs=(tokens,) * 3 + (state,) * 6,
        out_specs=(state,) * 6,
        check_vma=False,
    )
```

```python
import functools
import math

import jax
import jax.numpy as jnp
from jax import lax
from jax.experimental import pallas as pl
from jax.experimental.pallas import tpu as pltpu
from jax.sharding import PartitionSpec as P

BF16 = jnp.bfloat16
F32 = jnp.float32
CORES = 2
CHIPS_Z = 4
LANES = 128
PARTS = 2
VMEM = 20 * 1024 * 1024
WIDE = 56 * 1024 * 1024
SMALL = 4 * 1024 * 1024


def moments(weight, first, second, grad):
    new_first = 0.9 * first + 0.1 * grad
    new_second = 0.95 * second + 0.05 * grad * grad
    update = new_first / (jnp.sqrt(new_second) + 1e-06) + 0.05 * weight
    return (new_first, new_second, update)


def squares(value):
    return jnp.sum(value * value)


def gelu(value):
    return 0.5 * value * (1.0 + lax.erf(value * (1.0 / math.sqrt(2.0))))


def gelu_slope(value):
    cdf = 0.5 * (1.0 + lax.erf(value * (1.0 / math.sqrt(2.0))))
    return cdf + value * (jnp.exp(-0.5 * value * value) * (1.0 / math.sqrt(2.0 * math.pi)))


def widths(shard):
    if shard % LANES:
        return (shard,)
    first = shard // LANES * 3 // 5 * LANES
    return (first, shard - first)


def dot(left, right, dims):
    return lax.dot_general(left, right, (dims, ((), ())), preferred_element_type=F32)


def params(grant=VMEM):
    return dict(
        compiler_params=pltpu.CompilerParams(vmem_limit_bytes=grant),
        cost_estimate=pl.CostEstimate(flops=1, bytes_accessed=1, transcendentals=0),
    )


def pack(hidden, cotangent, at, nz, nx, cuts):
    tokens, hidden_width = hidden.shape
    model = cotangent.shape[1]
    shard = hidden_width // (nz * nx)
    first = cuts[0]
    if shard % LANES:
        parts = [
            lax.dynamic_slice_in_dim(hidden, (z * nx + at) * shard, shard, 1).T for z in range(nz)
        ]
        return jnp.concatenate([cotangent.T, *parts])

    def body(at_ref, h_ref, cot_ref, out_ref):
        z = pl.program_id(0)

        @pl.when(z == 0)
        def _():
            out_ref[:model] = cot_ref[...].T

        out_ref[pl.ds(pl.multiple_of(model + z * first, LANES), first)] = h_ref[:, :first].T

    total = model + nz * first
    return pl.pallas_call(
        body,
        grid_spec=pltpu.PrefetchScalarGridSpec(
            num_scalar_prefetch=1,
            grid=(nz,),
            in_specs=[
                pl.BlockSpec((tokens, shard), lambda z, a: (0, z * nx + a[0])),
                pl.BlockSpec((tokens, model), lambda z, a: (0, 0)),
            ],
            out_specs=pl.BlockSpec((total, tokens), lambda z, a: (0, 0)),
        ),
        out_shape=jax.ShapeDtypeStruct((total, tokens), BF16),
        **params(WIDE),
    )(jnp.reshape(at, (1,)).astype(jnp.int32), hidden, cotangent)


def pack_later(hidden, at, nz, nx, cuts):
    tokens, hidden_width = hidden.shape
    shard = hidden_width // (nz * nx)
    if len(cuts) == 1:
        return []

    def body(at_ref, h_ref, *out_refs):
        start = cuts[0]
        for width, out_ref in zip(cuts[1:], out_refs):
            out_ref[0] = h_ref[:, start : start + width].T
            start += width

    return pl.pallas_call(
        body,
        grid_spec=pltpu.PrefetchScalarGridSpec(
            num_scalar_prefetch=1,
            grid=(nz,),
            in_specs=[pl.BlockSpec((tokens, shard), lambda z, a: (0, z * nx + a[0]))],
            out_specs=[pl.BlockSpec((1, w, tokens), lambda z, a: (z, 0, 0)) for w in cuts[1:]],
        ),
        out_shape=[jax.ShapeDtypeStruct((nz, w, tokens), BF16) for w in cuts[1:]],
        **params(WIDE),
    )(jnp.reshape(at, (1,)).astype(jnp.int32), hidden)


class Tokens:
    def __init__(self, packs, hiddens, model, nz, width):
        tokens = packs[0].shape[1]
        self.model, self.width, self.count = model, width, len(packs)
        if hiddens is None:
            self.arrays = list(packs)
            self.specs = [pl.BlockSpec(packs[0].shape, lambda z, c: (0, 0))] * len(packs)
        else:
            self.arrays = [*packs, *hiddens]
            self.specs = [pl.BlockSpec((model, tokens), lambda z, c: (0, 0))] * len(packs)
            self.specs += [pl.BlockSpec((1, width, tokens), lambda z, c: (z, 0, 0))] * len(packs)

    def cot(self, refs, n):
        return refs[n].at[: self.model]

    def hidden(self, refs, n):
        if len(refs) == self.count:
            row = self.model + pl.program_id(0) * self.width
            return refs[n][pl.ds(pl.multiple_of(row, 16), self.width)].astype(F32)
        return refs[self.count + n][0].astype(F32)


def grad_out_chunk(tokens, core, nz, scale, parts):
    width, model = tokens.width, tokens.model
    half = model // CORES
    high = width // parts
    count = len(tokens.arrays)

    def body(c_ref, *refs):
        ins, outs = refs[:count], refs[count:]
        acts = jnp.concatenate(
            [gelu(tokens.hidden(ins, n)).astype(BF16) for n in range(tokens.count)], axis=1
        )
        for which in range(2):
            cols = pl.ds(pl.multiple_of((c_ref[0] + 1 + which) % CORES * half, 16), half)
            right = jnp.concatenate([tokens.cot(ins, n)[cols, :] for n in range(tokens.count)], axis=1)
            total = (dot(acts, right, ((1,), (1,))) * scale).astype(BF16)
            for p in range(parts):
                value = total[p * high : (p + 1) * high]
                if which:
                    outs[parts][p, 0] = value
                else:
                    outs[p][0] = value

    return pl.pallas_call(
        body,
        grid_spec=pltpu.PrefetchScalarGridSpec(
            num_scalar_prefetch=1,
            grid=(nz,),
            in_specs=tokens.specs,
            out_specs=[pl.BlockSpec((1, high, half), lambda z, c: (z, 0, 0))] * parts
            + [pl.BlockSpec((parts, 1, high, half), lambda z, c: (0, z, 0, 0))],
        ),
        out_shape=[jax.ShapeDtypeStruct((nz, high, half), BF16)] * parts
        + [jax.ShapeDtypeStruct((parts, nz, high, half), BF16)],
        **params(),
    )(core, *tokens.arrays)


def grad_pre_chunk(tokens, mine, other, nz, row, core, scale):
    part, model = mine[0].shape
    width = tokens.width
    count = len(tokens.arrays)
    long = tokens.arrays[0].shape[1]

    def body(c_ref, *refs):
        ins = refs[:count]
        out_ref, w_ref = refs[count + 2 * nz :]
        for h in range(nz):

            @pl.when((pl.program_id(0) ^ c_ref[1]) == h)
            def _(h=h):
                for at, ref in ((c_ref[0], refs[count + h]), (1 - c_ref[0], refs[count + nz + h])):
                    w_ref[pl.ds(pl.multiple_of(at * part, 16), part), :] = ref[...]

        w = w_ref[row : row + width, :]
        for n in range(tokens.count):
            grad_act = dot(w, tokens.cot(ins, n)[...], ((1,), (0,))) * scale
            out_ref[0, :, n * long : (n + 1) * long] = (
                grad_act * gelu_slope(tokens.hidden(ins, n))
            ).astype(BF16)

    w_specs = [pl.BlockSpec((part, model), lambda z, c: (0, 0))] * nz
    return pl.pallas_call(
        body,
        grid_spec=pltpu.PrefetchScalarGridSpec(
            num_scalar_prefetch=1,
            grid=(nz,),
            in_specs=tokens.specs + w_specs * 2,
            out_specs=pl.BlockSpec((1, width, tokens.count * long), lambda z, c: (z, 0, 0)),
            scratch_shapes=[pltpu.VMEM((CORES * part, model), BF16)],
        ),
        out_shape=jax.ShapeDtypeStruct((nz, width, tokens.count * long), BF16),
        **params(),
    )(core, *tokens.arrays, *mine, *other)


def grad_in_chunk(grads, inputs, core, scale, cut, block, width):
    nz, _, long = grads.shape
    model, tokens = inputs[0].shape
    count = len(inputs)
    half = nz // CORES
    high = model // cut

    def body(c_ref, g_ref, *refs):
        in_refs, outs = refs[:count], refs[count:]
        left = jnp.concatenate([i[...] for i in in_refs], axis=1)
        total = (dot(left, g_ref[0], ((1,), (1,))) * scale).astype(BF16)
        step = pl.program_id(0)
        for n in range(half):

            @pl.when(step == n)
            def _(n=n):
                for h in range(cut):
                    outs[n * cut + h][...] = total[h * high : (h + 1) * high]

        @pl.when(step >= half)
        def _():
            outs[-1][0] = total

    return pl.pallas_call(
        body,
        grid_spec=pltpu.PrefetchScalarGridSpec(
            num_scalar_prefetch=1,
            grid=(nz,),
            in_specs=[
                pl.BlockSpec(
                    (1, width, long),
                    lambda z, c: ((c[0] + 1 + z // half) % CORES * half + z % half, block, 0),
                )
            ]
            + [pl.BlockSpec((model, tokens), lambda z, c: (0, 0))] * count,
            out_specs=[pl.BlockSpec((high, width), lambda z, c: (0, 0))] * (half * cut)
            + [pl.BlockSpec((1, model, width), lambda z, c: (jnp.maximum(z - half, 0), 0, 0))],
        ),
        out_shape=[jax.ShapeDtypeStruct((high, width), BF16)] * (half * cut)
        + [jax.ShapeDtypeStruct((half, model, width), BF16)],
        **params(),
    )(core, grads, *inputs)


def transposed(value):
    rows, cols = value.shape
    wide = 2 * LANES

    def body(in_ref, out_ref):
        out_ref[...] = in_ref[...].T

    return pl.pallas_call(
        body,
        grid=(cols // wide,),
        in_specs=[pl.BlockSpec((rows, wide), lambda n: (0, n))],
        out_specs=pl.BlockSpec((wide, rows), lambda n: (n, 0)),
        out_shape=jax.ShapeDtypeStruct((cols, rows), value.dtype),
        **params(),
    )(value)


def half_rows(weight, core):
    rows, cols = weight.shape
    high = rows // CORES // 2

    def body(c_ref, in_ref, out_ref):
        out_ref[...] = in_ref[...].astype(BF16)

    return pl.pallas_call(
        body,
        grid_spec=pltpu.PrefetchScalarGridSpec(
            num_scalar_prefetch=1,
            grid=(2,),
            in_specs=[pl.BlockSpec((high, cols), lambda n, c: (c[0] * 2 + n, 0))],
            out_specs=pl.BlockSpec((high, cols), lambda n, c: (n, 0)),
        ),
        out_shape=jax.ShapeDtypeStruct((2 * high, cols), BF16),
        **params(WIDE),
    )(core, weight)


def stack(pieces, places, inner=False):
    count = len(pieces)
    shape = pieces[0].shape
    out = (shape[0], count, *shape[1:]) if inner else (count, *shape)

    def body(at_ref, *refs):
        for n in range(count):
            if inner:
                for p in range(shape[0]):
                    refs[count][p, at_ref[n]] = refs[n][p]
            else:
                refs[count][at_ref[n]] = refs[n][...]

    return pl.pallas_call(
        body,
        grid_spec=pltpu.PrefetchScalarGridSpec(
            num_scalar_prefetch=1,
            grid=(),
            in_specs=[pl.BlockSpec(shape, lambda at: (0,) * len(shape))] * count,
            out_specs=pl.BlockSpec(out, lambda at: (0,) * len(out)),
        ),
        out_shape=jax.ShapeDtypeStruct(out, pieces[0].dtype),
        **params(SMALL),
    )(places, *pieces)


def add_tiles(tiles):
    def body(*refs):
        refs[-1][...] = sum(ref[...] for ref in refs[:-1])

    return pl.pallas_call(
        body, out_shape=jax.ShapeDtypeStruct(tiles[0].shape, F32), **params(SMALL)
    )(*tiles)


def reduce_step(place, keep, crosses, from_y, from_z, shift, stage, ny, split):
    lead, nz, mid, _, high, wide = keep.shape
    bit = len(from_z)

    def zed(n, at):
        if stage == "y":
            return n
        if stage == "end":
            return at[2]
        low = at[2] % (1 << bit)
        mine = (at[2] // (1 << bit)) % 2
        return n * (2 << bit) + (1 - mine) * (1 << bit) + low

    count = {"y": nz, "z": nz >> (bit + 1), "end": 1}[stage]
    six = (lead, 1, mid, 1, high, wide)
    five = (lead, 1, mid, high, wide)
    specs = [pl.BlockSpec(six, lambda n, at: (0, zed(n, at), 0, (at[1] + shift) % ny, 0, 0))]
    each = len(crosses) // lead
    long = nz // each
    for h in range(len(crosses)):
        specs.append(
            pl.BlockSpec(
                six[1:],
                lambda n, at, h=h % each: (
                    jnp.clip(zed(n, at) - h * long, 0, long - 1),
                    0,
                    (at[1] + shift) % ny,
                    0,
                    0,
                ),
            )
        )
    specs += [pl.BlockSpec(five, lambda n, at: (0, zed(n, at), 0, 0, 0))] * len(from_y)
    specs += [
        pl.BlockSpec(five, lambda n, at, j=j: (0, zed(n, at) // (2 << j), 0, 0, 0)) for j in range(bit)
    ]

    def body(at_ref, *refs):
        ins = refs[: len(specs)]
        outs = refs[len(specs) :]
        for p in range(lead):
            for m in range(mid):
                total = ins[1 + p * each][0, m, 0]
                for h in range(1, each):
                    total = jnp.where(
                        zed(pl.program_id(0), at_ref) >= h * long, ins[1 + p * each + h][0, m, 0], total
                    )
                total = total.astype(F32) + ins[0][p, 0, m, 0].astype(F32)
                for ref in ins[1 + len(crosses) :]:
                    total = total + ref[p, 0, m].astype(F32)
                total = total.astype(BF16)
                if not split:
                    outs[0][p, 0, m] = total
                    continue
                for s in range(mid):

                    @pl.when((at_ref[0] + s) % mid == m)
                    def _(s=s, total=total):
                        outs[s][p] = total

    if split:
        out_specs = [pl.BlockSpec((lead, high, wide), lambda n, at: (0, 0, 0))] * mid
        out_shape = [jax.ShapeDtypeStruct((lead, high, wide), BF16)] * mid
    else:
        out_specs = [pl.BlockSpec(five, lambda n, at: (0, n, 0, 0, 0))]
        out_shape = [jax.ShapeDtypeStruct((lead, count, mid, high, wide), BF16)]
    out = pl.pallas_call(
        body,
        grid_spec=pltpu.PrefetchScalarGridSpec(
            num_scalar_prefetch=1, grid=(count,), in_specs=specs, out_specs=out_specs
        ),
        out_shape=out_shape,
        **params(SMALL),
    )(place, keep, *crosses, *from_y, *from_z)
    return out if split else out[0]


def moments_kernel(core, weight, first, second, mine, other, grid, state_spec, grad_specs, owner, axis, tiles):
    block = state_spec.block_shape
    count = len(mine)
    long = 16 * (1 + len(tiles))

    def body(c_ref, w_ref, m_ref, v_ref, *refs):
        mine_refs, other_refs = refs[:count], refs[count : 2 * count]
        tile_refs = refs[2 * count : 2 * count + len(tiles)]
        new_m_ref, new_v_ref, u_ref, sum_ref = refs[2 * count + len(tiles) :]
        totals = [jnp.zeros((8, LANES), F32)] * 2
        start = 0
        ours = owner(pl.program_id(0)) == c_ref[0]
        for mine_ref, other_ref in zip(mine_refs, other_refs):
            size = mine_ref.size // block[1 - axis]
            shape = (size, block[1]) if axis == 0 else (block[0], size)
            at = (slice(start, start + size), slice(None))
            at = at if axis == 0 else at[::-1]
            grad = jnp.where(ours, mine_ref[...].reshape(shape), other_ref[...].reshape(shape)).astype(F32)
            weight = w_ref[at]
            new_m, new_v, update = moments(weight, m_ref[at], v_ref[at], grad)
            new_m_ref[at] = new_m
            new_v_ref[at] = new_v
            u_ref[at] = update
            for n, value in enumerate((weight, update)):
                square = value * value
                for col in range(0, shape[1], LANES):
                    totals[n] = totals[n] + square[:, col : col + LANES].reshape(-1, 8, LANES).sum(0)
            start += size

        @pl.when(pl.program_id(0) == 0)
        def _():
            sum_ref[:16] = jnp.zeros((16, LANES), F32)
            for n, tile_ref in enumerate(tile_refs):
                sum_ref[16 * (n + 1) : 16 * (n + 2)] = tile_ref[...]

        sum_ref[:8] += totals[0]
        sum_ref[8:16] += totals[1]

    state = jax.ShapeDtypeStruct(weight.shape, F32)
    return pl.pallas_call(
        body,
        grid_spec=pltpu.PrefetchScalarGridSpec(
            num_scalar_prefetch=1,
            grid=grid,
            in_specs=[state_spec] * 3
            + grad_specs * 2
            + [pl.BlockSpec((16, LANES), lambda n, c: (0, 0))] * len(tiles),
            out_specs=[state_spec] * 3 + [pl.BlockSpec((long, LANES), lambda n, c: (0, 0))],
        ),
        out_shape=[state] * 3 + [jax.ShapeDtypeStruct((long, LANES), F32)],
        **params(),
    )(core, weight, first, second, *mine, *other, *tiles)


def step_weights(weight, update, tiles, at):
    rows, cols = weight.shape
    high = rows // 5
    count = len(tiles)

    def body(w_ref, u_ref, *refs):
        sums = sum(ref[at : at + 16] for ref in refs[:count])
        ratio = jnp.sqrt(jnp.sum(sums[:8], keepdims=True)) / jnp.sqrt(jnp.sum(sums[8:], keepdims=True))
        refs[count][...] = w_ref[...] - 0.4 * ratio * u_ref[...]

    spec = pl.BlockSpec((high, cols), lambda n: (n, 0))
    tile = pl.BlockSpec(tiles[0].shape, lambda n: (0, 0))
    return pl.pallas_call(
        body,
        grid=(rows // high,),
        in_specs=[spec] * 2 + [tile] * count,
        out_specs=spec,
        out_shape=jax.ShapeDtypeStruct(weight.shape, F32),
        **params(),
    )(weight, update, *tiles)


class Order:
    def __init__(self):
        self.last = None

    def after(self, *values):
        if self.last is None:
            return values
        return lax.optimization_barrier((*values, self.last))[:-1]

    def did(self, value):
        self.last = value


def plan(nz, nx, ny):
    def along_x(value, step):
        pairs = [
            (z * nx + x, z * nx + (x + step) % nx) for z in range(nz) for x in range(nx)
        ]
        return lax.ppermute(value, "gx", pairs)

    def along_z(value, flip):
        pairs = [(z * nx + x, (z ^ flip) * nx + x) for z in range(nz) for x in range(nx)]
        return lax.ppermute(value, "gx", pairs)

    def along_y(value, step):
        pairs = [
            (y * CORES + c, (y + step) % ny * CORES + c) for y in range(ny) for c in range(CORES)
        ]
        return lax.ppermute(value, "gy", pairs)

    def across(value):
        pairs = [(k, k ^ 1) for k in range(ny * CORES)]
        return lax.ppermute(value, "gy", pairs)

    class Reduce:
        def __init__(self, order, at, sends, keep, shape):
            self.order, self.at, self.place = order, at, jnp.stack(at).astype(jnp.int32)
            self.keep = keep.reshape(shape)
            each = len(sends) // shape[0]
            self.crosses = [
                across(send).reshape(shape[1] // each, *shape[2:]) for send in sends
            ]
            self.from_y = []
            self.from_z = []

        def step(self, shift, stage, split=False):
            got = self.order.after(self.keep, *self.crosses, *self.from_y, *self.from_z)
            lead = 1 + len(self.crosses)
            count = lead + len(self.from_y)
            out = reduce_step(
                self.place, got[0], got[1:lead], got[lead:count], got[count:], shift, stage, ny, split
            )
            self.order.did(out[0] if split else out)
            return out

        def send_y(self):
            from_y = []
            for s in range(1, ny):
                from_y.append(along_y(self.step(s, "y"), s))
            self.from_y = from_y

        def send_z(self):
            bit = len(self.from_z)
            self.from_z.append(along_z(self.step(0, "z"), 1 << bit))

        def finish(self):
            out = self.step(0, "end", True)
            self.held = [out[0]] + [along_x(out[s], s) for s in range(1, len(out))]
            if len(out) == 1:
                self.share_y(out[0])

        def share_y(self, value):
            self.held = [value] + [along_y(value, s) for s in range(1, ny)]

        def stacked(self, place, size, inner=False):
            places = jnp.stack([(place - s) % size for s in range(size)]).astype(jnp.int32)
            value = stack(self.order.after(*self.held), places, inner)
            self.order.did(value)
            return value

        def stack_x(self):
            self.share_y(self.stacked(self.at[0], nx))

        def stack_y(self, inner=False):
            value = self.stacked(self.at[1], ny, inner)
            self.held = [value, across(value)]

    def local(inputs, hidden_pre, cotangent, w_in, m_in, v_in, w_out, m_out, v_out):
        model = inputs.shape[1]
        hidden_width = hidden_pre.shape[1]
        shard = hidden_width // (nz * nx)
        rows = model // (nz * nx)
        cuts = widths(shard)
        chunks = range(len(cuts))
        last = len(cuts) - 1
        starts = [sum(cuts[:k]) for k in chunks]
        scale_in = 1.0 / math.sqrt(model)
        scale_out = 1.0 / math.sqrt(hidden_width)
        place = lax.axis_index("gx")
        side = lax.axis_index("gy")
        z, x = place // nx, place % nx
        y, c = side // CORES, side % CORES
        core = jnp.reshape(c, (1,)).astype(jnp.int32)
        at_core = jnp.stack([c, z]).astype(jnp.int32)
        order = Order()

        packs, hiddens = [], []
        for t in range(1, nx):
            sent = pack(*order.after(hidden_pre, cotangent), (x + t) % nx, nz, nx, cuts)
            order.did(sent)
            packs.append(along_x(sent, t))

        part = half_rows(*order.after(w_out), core)
        order.did(part)
        flipped = transposed(*order.after(inputs))
        order.did(flipped)
        columns = [flipped] + [along_x(flipped, t) for t in range(1, nx)]
        own = pack(*order.after(hidden_pre, cotangent), x, nz, nx, cuts)
        order.did(own)
        for t in range(nx):
            value = pack_later(*order.after(hidden_pre), (x + t) % nx, nz, nx, cuts)
            if value:
                order.did(value[0])
            hiddens.append([along_x(h, t) for h in value] if t else value)
        found = {0: part, nz // 2: along_z(part, nz // 2)}
        bit = nz // 4
        while bit:
            for key in list(found):
                value = found[key]
                if key:
                    (value,) = order.after(value)
                found[key ^ bit] = along_z(value, bit)
            bit //= 2
        found = [found[key] for key in range(nz)]
        crossed = [across(value) for value in [*order.after(*found[: nz // 2]), *found[nz // 2 :]]]
        packs = [own] + packs

        parts = [2] + [2] * last
        outs = [None for _ in chunks]
        pieces_in = [(0, 0, cuts[0])]
        if last:
            pieces_in.append((1, 0, cuts[1]))
        ins = [None for _ in pieces_in]
        pres = [None for _ in chunks]

        def tokens(k, *more):
            later = [] if k == 0 else [value[k - 1] for value in hiddens]
            got = order.after(*packs, *later, *more)
            count = nx + len(later)
            blocks = Tokens(got[:nx], got[nx:count] if later else None, model, nz, cuts[k])
            return blocks, got[count:]

        def start_out(k):
            blocks, _ = tokens(k, *([*crossed[: nz // 2], found[nz // 2]] if k == 0 else []))
            *sends, keep = grad_out_chunk(blocks, core, nz, scale_out, parts[k])
            order.did(keep)
            shape = (parts[k], nz, 1, ny, cuts[k] // parts[k] // ny, model // CORES)
            outs[k] = Reduce(order, (x, y, z), sends, keep, shape)

        def start_pre(k):
            blocks, got = tokens(k, *found, *crossed)
            pres[k] = grad_pre_chunk(blocks, got[:nz], got[nz:], nz, starts[k], at_core, scale_out)
            order.did(pres[k])

        def start_in(k):
            chunk, block, width = pieces_in[k]
            got = order.after(pres[chunk], *columns)
            *sends, keep = grad_in_chunk(
                got[0], got[1:], core, scale_in, (1 if chunk else 1), block, width
            )
            order.did(keep)
            shape = (nz // CORES, nz, nx, ny, rows // ny, width)
            ins[k] = Reduce(order, (x, y, z), sends, keep, shape)

        def sums(tile):
            tiles = order.after(tile, *[along_z(tile, flip) for flip in range(1, nz)])
            tile = add_tiles(tiles)
            order.did(tile)
            return [tile] + [along_x(tile, t) for t in range(1, nx)]

        def new_weights(weight, update, tiles, at):
            got = order.after(weight, update, *tiles)
            value = step_weights(got[0], got[1], got[2:], at)
            order.did(value)
            return value

        def moments_out(tile):
            half = model // CORES
            got = order.after(
                w_out,
                m_out,
                v_out,
                tile,
                *[outs[k].held[0] for k in chunks],
                *[outs[k].held[1] for k in chunks],
            )
            new = moments_kernel(
                core,
                *got[:3],
                got[4 : 5 + last],
                got[5 + last :],
                (CORES,),
                pl.BlockSpec((shard, half), lambda n, c: (0, n)),
                [
                    pl.BlockSpec((p, ny, w // p // ny, half), lambda n, c: (0, 0, 0, 0))
                    for w, p in zip(cuts, parts)
                ],
                lambda n: n,
                0,
                [got[3]],
            )
            order.did(new[3])
            return new

        start_out(0)
        outs[0].send_y()
        start_pre(0)
        start_in(0)
        outs[0].send_z()
        ins[0].send_y()
        if last:
            start_pre(1)
            start_in(1)
            outs[0].send_z()
            start_out(1)
            ins[1].send_y()
            outs[1].send_y()
            ins[0].send_z()
            ins[1].send_z()
            ins[0].send_z()
            outs[1].send_z()
            ins[1].send_z()
            outs[0].finish()
            ins[0].finish()
            outs[1].send_z()
            ins[1].finish()
            ins[0].stack_x()
            ins[1].stack_x()
            outs[0].stack_y(True)
            ins[0].stack_y()
            outs[1].finish()
            ins[1].stack_y()
        else:
            outs[0].send_z()
            ins[0].send_z()
            outs[0].finish()
            ins[0].send_z()
            ins[0].finish()
            ins[0].stack_x()
            ins[0].stack_y()

        held = [value.held for value in ins]
        got = order.after(w_in, m_in, v_in, *[pair[0] for pair in held], *[pair[1] for pair in held])
        mine, other = got[3 : 3 + len(ins)], got[3 + len(ins) :]
        if shard % LANES:
            joined = [
                jnp.stack([jnp.where(c == 0, a, b), jnp.where(c == 0, b, a)]) for a, b in zip(mine, other)
            ]
            grad = jnp.concatenate(joined, axis=-1).transpose(1, 4, 0, 3, 2, 5)
            grad = grad.reshape(rows, hidden_width).astype(F32)
            first_in, second_in, update_in = moments(*got[:3], grad)
            tile = jnp.concatenate(
                [
                    jnp.sum((value * value).reshape(-1, 8, LANES), axis=0)
                    for value in (w_in, update_in)
                ]
            )
        else:
            zs = nz // CORES
            first_in, second_in, update_in, tile = moments_kernel(
                core,
                *got[:3],
                mine,
                other,
                (nz * nx,),
                pl.BlockSpec((rows, shard), lambda n, c: (0, n)),
                [
                    pl.BlockSpec(
                        (ny, 1, 1, rows // ny, w), lambda n, c: (0, n % nx, n // nx % zs, 0, 0)
                    )
                    for _, _, w in pieces_in
                ],
                lambda n: n // nx // zs,
                1,
                [],
            )
        order.did(tile)

        outs[last].stack_y(True)
        first_out, second_out, update_out, tile = moments_out(tile)
        tiles = sums(tile)
        new_w_in = new_weights(w_in, update_in, tiles, 16)
        new_w_out = new_weights(w_out, update_out, tiles, 0)
        return (new_w_in, first_in, second_in, new_w_out, first_out, second_out)

    return local


def solution(mesh):
    gx, gy = mesh.shape["gx"], mesh.shape["gy"]
    nz = CHIPS_Z
    state = P("gx", None)
    tokens = P(("gx", "gy"), None)
    return jax.shard_map(
        plan(nz, gx // nz, gy // CORES),
        mesh=mesh,
        in_specs=(tokens,) * 3 + (state,) * 6,
        out_specs=(state,) * 6,
        check_vma=False,
    )
```

```python
import functools
import math

import jax
import jax.numpy as jnp
from jax import lax
from jax.experimental import pallas as pl
from jax.experimental.pallas import tpu as pltpu
from jax.sharding import PartitionSpec as P

BF16 = jnp.bfloat16
F32 = jnp.float32
CORES = 2
CHIPS_Z = 4
LANES = 128
PARTS = 2
VMEM = 20 * 1024 * 1024
WIDE = 56 * 1024 * 1024
SMALL = 4 * 1024 * 1024


def moments(weight, first, second, grad):
    new_first = 0.9 * first + 0.1 * grad
    new_second = 0.95 * second + 0.05 * grad * grad
    update = new_first / (jnp.sqrt(new_second) + 1e-06) + 0.05 * weight
    return (new_first, new_second, update)


def squares(value):
    return jnp.sum(value * value)


def gelu(value):
    return 0.5 * value * (1.0 + lax.erf(value * (1.0 / math.sqrt(2.0))))


def gelu_slope(value):
    cdf = 0.5 * (1.0 + lax.erf(value * (1.0 / math.sqrt(2.0))))
    return cdf + value * (jnp.exp(-0.5 * value * value) * (1.0 / math.sqrt(2.0 * math.pi)))


def widths(shard):
    if shard % LANES:
        return (shard,)
    first = shard // LANES * 3 // 5 * LANES
    return (first, shard - first)


def dot(left, right, dims):
    return lax.dot_general(left, right, (dims, ((), ())), preferred_element_type=F32)


def params(grant=VMEM):
    return dict(
        compiler_params=pltpu.CompilerParams(vmem_limit_bytes=grant),
        cost_estimate=pl.CostEstimate(flops=1, bytes_accessed=1, transcendentals=0),
    )


def pack(hidden, cotangent, at, nz, nx, cuts):
    tokens, hidden_width = hidden.shape
    model = cotangent.shape[1]
    shard = hidden_width // (nz * nx)
    first = cuts[0]
    if shard % LANES:
        parts = [
            lax.dynamic_slice_in_dim(hidden, (z * nx + at) * shard, shard, 1).T for z in range(nz)
        ]
        return jnp.concatenate([cotangent.T, *parts])

    def body(at_ref, h_ref, cot_ref, out_ref):
        z = pl.program_id(0)

        @pl.when(z == 0)
        def _():
            out_ref[:model] = cot_ref[...].T

        out_ref[pl.ds(pl.multiple_of(model + z * first, LANES), first)] = h_ref[:, :first].T

    total = model + nz * first
    return pl.pallas_call(
        body,
        grid_spec=pltpu.PrefetchScalarGridSpec(
            num_scalar_prefetch=1,
            grid=(nz,),
            in_specs=[
                pl.BlockSpec((tokens, shard), lambda z, a: (0, z * nx + a[0])),
                pl.BlockSpec((tokens, model), lambda z, a: (0, 0)),
            ],
            out_specs=pl.BlockSpec((total, tokens), lambda z, a: (0, 0)),
        ),
        out_shape=jax.ShapeDtypeStruct((total, tokens), BF16),
        **params(WIDE),
    )(jnp.reshape(at, (1,)).astype(jnp.int32), hidden, cotangent)


def pack_later(hidden, at, nz, nx, cuts):
    tokens, hidden_width = hidden.shape
    shard = hidden_width // (nz * nx)
    if len(cuts) == 1:
        return []

    def body(at_ref, h_ref, *out_refs):
        start = cuts[0]
        for width, out_ref in zip(cuts[1:], out_refs):
            out_ref[0] = h_ref[:, start : start + width].T
            start += width

    return pl.pallas_call(
        body,
        grid_spec=pltpu.PrefetchScalarGridSpec(
            num_scalar_prefetch=1,
            grid=(nz,),
            in_specs=[pl.BlockSpec((tokens, shard), lambda z, a: (0, z * nx + a[0]))],
            out_specs=[pl.BlockSpec((1, w, tokens), lambda z, a: (z, 0, 0)) for w in cuts[1:]],
        ),
        out_shape=[jax.ShapeDtypeStruct((nz, w, tokens), BF16) for w in cuts[1:]],
        **params(WIDE),
    )(jnp.reshape(at, (1,)).astype(jnp.int32), hidden)


class Tokens:
    def __init__(self, packs, hiddens, model, nz, width):
        tokens = packs[0].shape[1]
        self.model, self.width, self.count = model, width, len(packs)
        if hiddens is None:
            self.arrays = list(packs)
            self.specs = [pl.BlockSpec(packs[0].shape, lambda z, c: (0, 0))] * len(packs)
        else:
            self.arrays = [*packs, *hiddens]
            self.specs = [pl.BlockSpec((model, tokens), lambda z, c: (0, 0))] * len(packs)
            self.specs += [pl.BlockSpec((1, width, tokens), lambda z, c: (z, 0, 0))] * len(packs)

    def cot(self, refs, n):
        return refs[n].at[: self.model]

    def hidden(self, refs, n):
        if len(refs) == self.count:
            row = self.model + pl.program_id(0) * self.width
            return refs[n][pl.ds(pl.multiple_of(row, 16), self.width)].astype(F32)
        return refs[self.count + n][0].astype(F32)


def grad_out_chunk(tokens, core, nz, scale, parts):
    width, model = tokens.width, tokens.model
    half = model // CORES
    high = width // parts
    count = len(tokens.arrays)
    long = tokens.arrays[0].shape[1]

    def body(c_ref, *refs):
        ins, outs, right_ref = refs[:count], refs[count:-1], refs[-1]

        @pl.when(pl.program_id(0) == 0)
        def _():
            for n in range(tokens.count):
                right_ref[:, n * long : (n + 1) * long] = tokens.cot(ins, n)[...]

        acts = jnp.concatenate(
            [gelu(tokens.hidden(ins, n)).astype(BF16) for n in range(tokens.count)], axis=1
        )
        for which in range(2):
            cols = pl.ds(pl.multiple_of((c_ref[0] + 1 + which) % CORES * half, 16), half)
            total = (dot(acts, right_ref[cols, :], ((1,), (1,))) * scale).astype(BF16)
            for p in range(parts):
                value = total[p * high : (p + 1) * high]
                if which:
                    outs[parts][p, 0] = value
                else:
                    outs[p][0] = value

    return pl.pallas_call(
        body,
        grid_spec=pltpu.PrefetchScalarGridSpec(
            num_scalar_prefetch=1,
            grid=(nz,),
            in_specs=tokens.specs,
            out_specs=[pl.BlockSpec((1, high, half), lambda z, c: (z, 0, 0))] * parts
            + [pl.BlockSpec((parts, 1, high, half), lambda z, c: (0, z, 0, 0))],
            scratch_shapes=[pltpu.VMEM((model, tokens.count * long), BF16)],
        ),
        out_shape=[jax.ShapeDtypeStruct((nz, high, half), BF16)] * parts
        + [jax.ShapeDtypeStruct((parts, nz, high, half), BF16)],
        **params(),
    )(core, *tokens.arrays)


def grad_pre_chunk(tokens, mine, other, nz, row, core, scale):
    part, model = mine[0].shape
    width = tokens.width
    count = len(tokens.arrays)
    long = tokens.arrays[0].shape[1]

    def body(c_ref, *refs):
        ins = refs[:count]
        out_ref, w_ref = refs[count + 2 * nz :]
        for h in range(nz):

            @pl.when((pl.program_id(0) ^ c_ref[1]) == h)
            def _(h=h):
                for at, ref in ((c_ref[0], refs[count + h]), (1 - c_ref[0], refs[count + nz + h])):
                    w_ref[pl.ds(pl.multiple_of(at * part, 16), part), :] = ref[...]

        w = w_ref[row : row + width, :]
        for n in range(tokens.count):
            grad_act = dot(w, tokens.cot(ins, n)[...], ((1,), (0,))) * scale
            out_ref[0, :, n * long : (n + 1) * long] = (
                grad_act * gelu_slope(tokens.hidden(ins, n))
            ).astype(BF16)

    w_specs = [pl.BlockSpec((part, model), lambda z, c: (0, 0))] * nz
    return pl.pallas_call(
        body,
        grid_spec=pltpu.PrefetchScalarGridSpec(
            num_scalar_prefetch=1,
            grid=(nz,),
            in_specs=tokens.specs + w_specs * 2,
            out_specs=pl.BlockSpec((1, width, tokens.count * long), lambda z, c: (z, 0, 0)),
            scratch_shapes=[pltpu.VMEM((CORES * part, model), BF16)],
        ),
        out_shape=jax.ShapeDtypeStruct((nz, width, tokens.count * long), BF16),
        **params(),
    )(core, *tokens.arrays, *mine, *other)


def grad_in_chunk(grads, inputs, core, scale, cut, block, width):
    nz, _, long = grads.shape
    model, tokens = inputs[0].shape
    count = len(inputs)
    half = nz // CORES
    high = model // cut

    def body(c_ref, g_ref, *refs):
        in_refs, outs, left_ref = refs[:count], refs[count:-1], refs[-1]
        step = pl.program_id(0)

        @pl.when(step == 0)
        def _():
            for n, in_ref in enumerate(in_refs):
                left_ref[:, n * tokens : (n + 1) * tokens] = in_ref[...]

        total = (dot(left_ref[...], g_ref[0], ((1,), (1,))) * scale).astype(BF16)
        for n in range(half):

            @pl.when(step == n)
            def _(n=n):
                for h in range(cut):
                    outs[n * cut + h][...] = total[h * high : (h + 1) * high]

        @pl.when(step >= half)
        def _():
            outs[-1][0] = total

    return pl.pallas_call(
        body,
        grid_spec=pltpu.PrefetchScalarGridSpec(
            num_scalar_prefetch=1,
            grid=(nz,),
            in_specs=[
                pl.BlockSpec(
                    (1, width, long),
                    lambda z, c: ((c[0] + 1 + z // half) % CORES * half + z % half, block, 0),
                )
            ]
            + [pl.BlockSpec((model, tokens), lambda z, c: (0, 0))] * count,
            out_specs=[pl.BlockSpec((high, width), lambda z, c: (0, 0))] * (half * cut)
            + [pl.BlockSpec((1, model, width), lambda z, c: (jnp.maximum(z - half, 0), 0, 0))],
            scratch_shapes=[pltpu.VMEM((model, count * tokens), BF16)],
        ),
        out_shape=[jax.ShapeDtypeStruct((high, width), BF16)] * (half * cut)
        + [jax.ShapeDtypeStruct((half, model, width), BF16)],
        **params(),
    )(core, grads, *inputs)


def transposed(value):
    rows, cols = value.shape
    wide = 2 * LANES

    def body(in_ref, out_ref):
        out_ref[...] = in_ref[...].T

    return pl.pallas_call(
        body,
        grid=(cols // wide,),
        in_specs=[pl.BlockSpec((rows, wide), lambda n: (0, n))],
        out_specs=pl.BlockSpec((wide, rows), lambda n: (n, 0)),
        out_shape=jax.ShapeDtypeStruct((cols, rows), value.dtype),
        **params(),
    )(value)


def half_rows(weight, core):
    rows, cols = weight.shape
    high = rows // CORES // 2

    def body(c_ref, in_ref, out_ref):
        out_ref[...] = in_ref[...].astype(BF16)

    return pl.pallas_call(
        body,
        grid_spec=pltpu.PrefetchScalarGridSpec(
            num_scalar_prefetch=1,
            grid=(2,),
            in_specs=[pl.BlockSpec((high, cols), lambda n, c: (c[0] * 2 + n, 0))],
            out_specs=pl.BlockSpec((high, cols), lambda n, c: (n, 0)),
        ),
        out_shape=jax.ShapeDtypeStruct((2 * high, cols), BF16),
        **params(WIDE),
    )(core, weight)


def stack(pieces, places, inner=False):
    count = len(pieces)
    shape = pieces[0].shape
    out = (shape[0], count, *shape[1:]) if inner else (count, *shape)

    def body(at_ref, *refs):
        for n in range(count):
            if inner:
                for p in range(shape[0]):
                    refs[count][p, at_ref[n]] = refs[n][p]
            else:
                refs[count][at_ref[n]] = refs[n][...]

    return pl.pallas_call(
        body,
        grid_spec=pltpu.PrefetchScalarGridSpec(
            num_scalar_prefetch=1,
            grid=(),
            in_specs=[pl.BlockSpec(shape, lambda at: (0,) * len(shape))] * count,
            out_specs=pl.BlockSpec(out, lambda at: (0,) * len(out)),
        ),
        out_shape=jax.ShapeDtypeStruct(out, pieces[0].dtype),
        **params(SMALL),
    )(places, *pieces)


def add_tiles(tiles):
    def body(*refs):
        refs[-1][...] = sum(ref[...] for ref in refs[:-1])

    return pl.pallas_call(
        body, out_shape=jax.ShapeDtypeStruct(tiles[0].shape, F32), **params(SMALL)
    )(*tiles)


def reduce_step(place, keep, crosses, from_y, from_z, shift, stage, ny, split):
    lead, nz, mid, _, high, wide = keep.shape
    bit = len(from_z)

    def zed(n, at):
        if stage == "y":
            return n
        if stage == "end":
            return at[2]
        low = at[2] % (1 << bit)
        mine = (at[2] // (1 << bit)) % 2
        return n * (2 << bit) + (1 - mine) * (1 << bit) + low

    count = {"y": nz, "z": nz >> (bit + 1), "end": 1}[stage]
    six = (lead, 1, mid, 1, high, wide)
    five = (lead, 1, mid, high, wide)
    specs = [pl.BlockSpec(six, lambda n, at: (0, zed(n, at), 0, (at[1] + shift) % ny, 0, 0))]
    each = len(crosses) // lead
    long = nz // each
    for h in range(len(crosses)):
        specs.append(
            pl.BlockSpec(
                six[1:],
                lambda n, at, h=h % each: (
                    jnp.clip(zed(n, at) - h * long, 0, long - 1),
                    0,
                    (at[1] + shift) % ny,
                    0,
                    0,
                ),
            )
        )
    specs += [pl.BlockSpec(five, lambda n, at: (0, zed(n, at), 0, 0, 0))] * len(from_y)
    specs += [
        pl.BlockSpec(five, lambda n, at, j=j: (0, zed(n, at) // (2 << j), 0, 0, 0)) for j in range(bit)
    ]

    def body(at_ref, *refs):
        ins = refs[: len(specs)]
        outs = refs[len(specs) :]
        for p in range(lead):
            for m in range(mid):
                total = ins[1 + p * each][0, m, 0]
                for h in range(1, each):
                    total = jnp.where(
                        zed(pl.program_id(0), at_ref) >= h * long, ins[1 + p * each + h][0, m, 0], total
                    )
                total = total.astype(F32) + ins[0][p, 0, m, 0].astype(F32)
                for ref in ins[1 + len(crosses) :]:
                    total = total + ref[p, 0, m].astype(F32)
                total = total.astype(BF16)
                if not split:
                    outs[0][p, 0, m] = total
                    continue
                for s in range(mid):

                    @pl.when((at_ref[0] + s) % mid == m)
                    def _(s=s, total=total):
                        outs[s][p] = total

    if split:
        out_specs = [pl.BlockSpec((lead, high, wide), lambda n, at: (0, 0, 0))] * mid
        out_shape = [jax.ShapeDtypeStruct((lead, high, wide), BF16)] * mid
    else:
        out_specs = [pl.BlockSpec(five, lambda n, at: (0, n, 0, 0, 0))]
        out_shape = [jax.ShapeDtypeStruct((lead, count, mid, high, wide), BF16)]
    out = pl.pallas_call(
        body,
        grid_spec=pltpu.PrefetchScalarGridSpec(
            num_scalar_prefetch=1, grid=(count,), in_specs=specs, out_specs=out_specs
        ),
        out_shape=out_shape,
        **params(SMALL),
    )(place, keep, *crosses, *from_y, *from_z)
    return out if split else out[0]


def moments_kernel(core, weight, first, second, mine, other, grid, state_spec, grad_specs, owner, axis, tiles):
    block = state_spec.block_shape
    count = len(mine)
    long = 16 * (1 + len(tiles))

    def body(c_ref, w_ref, m_ref, v_ref, *refs):
        mine_refs, other_refs = refs[:count], refs[count : 2 * count]
        tile_refs = refs[2 * count : 2 * count + len(tiles)]
        new_m_ref, new_v_ref, u_ref, sum_ref = refs[2 * count + len(tiles) :]
        totals = [jnp.zeros((8, LANES), F32)] * 2
        start = 0
        ours = owner(pl.program_id(0)) == c_ref[0]
        for mine_ref, other_ref in zip(mine_refs, other_refs):
            size = mine_ref.size // block[1 - axis]
            shape = (size, block[1]) if axis == 0 else (block[0], size)
            at = (slice(start, start + size), slice(None))
            at = at if axis == 0 else at[::-1]
            grad = jnp.where(ours, mine_ref[...].reshape(shape), other_ref[...].reshape(shape)).astype(F32)
            weight = w_ref[at]
            new_m, new_v, update = moments(weight, m_ref[at], v_ref[at], grad)
            new_m_ref[at] = new_m
            new_v_ref[at] = new_v
            u_ref[at] = update
            for n, value in enumerate((weight, update)):
                square = value * value
                for col in range(0, shape[1], LANES):
                    totals[n] = totals[n] + square[:, col : col + LANES].reshape(-1, 8, LANES).sum(0)
            start += size

        @pl.when(pl.program_id(0) == 0)
        def _():
            sum_ref[:16] = jnp.zeros((16, LANES), F32)
            for n, tile_ref in enumerate(tile_refs):
                sum_ref[16 * (n + 1) : 16 * (n + 2)] = tile_ref[...]

        sum_ref[:8] += totals[0]
        sum_ref[8:16] += totals[1]

    state = jax.ShapeDtypeStruct(weight.shape, F32)
    return pl.pallas_call(
        body,
        grid_spec=pltpu.PrefetchScalarGridSpec(
            num_scalar_prefetch=1,
            grid=grid,
            in_specs=[state_spec] * 3
            + grad_specs * 2
            + [pl.BlockSpec((16, LANES), lambda n, c: (0, 0))] * len(tiles),
            out_specs=[state_spec] * 3 + [pl.BlockSpec((long, LANES), lambda n, c: (0, 0))],
        ),
        out_shape=[state] * 3 + [jax.ShapeDtypeStruct((long, LANES), F32)],
        **params(),
    )(core, weight, first, second, *mine, *other, *tiles)


def step_weights(weight, update, tiles, at):
    rows, cols = weight.shape
    high = rows // 5
    count = len(tiles)

    def body(w_ref, u_ref, *refs):
        sums = sum(ref[at : at + 16] for ref in refs[:count])
        ratio = jnp.sqrt(jnp.sum(sums[:8], keepdims=True)) / jnp.sqrt(jnp.sum(sums[8:], keepdims=True))
        refs[count][...] = w_ref[...] - 0.4 * ratio * u_ref[...]

    spec = pl.BlockSpec((high, cols), lambda n: (n, 0))
    tile = pl.BlockSpec(tiles[0].shape, lambda n: (0, 0))
    return pl.pallas_call(
        body,
        grid=(rows // high,),
        in_specs=[spec] * 2 + [tile] * count,
        out_specs=spec,
        out_shape=jax.ShapeDtypeStruct(weight.shape, F32),
        **params(),
    )(weight, update, *tiles)


class Order:
    def __init__(self):
        self.last = None

    def after(self, *values):
        if self.last is None:
            return values
        return lax.optimization_barrier((*values, self.last))[:-1]

    def did(self, value):
        self.last = value


def plan(nz, nx, ny):
    def along_x(value, step):
        pairs = [
            (z * nx + x, z * nx + (x + step) % nx) for z in range(nz) for x in range(nx)
        ]
        return lax.ppermute(value, "gx", pairs)

    def along_z(value, flip):
        pairs = [(z * nx + x, (z ^ flip) * nx + x) for z in range(nz) for x in range(nx)]
        return lax.ppermute(value, "gx", pairs)

    def along_y(value, step):
        pairs = [
            (y * CORES + c, (y + step) % ny * CORES + c) for y in range(ny) for c in range(CORES)
        ]
        return lax.ppermute(value, "gy", pairs)

    def across(value):
        pairs = [(k, k ^ 1) for k in range(ny * CORES)]
        return lax.ppermute(value, "gy", pairs)

    class Reduce:
        def __init__(self, order, at, sends, keep, shape):
            self.order, self.at, self.place = order, at, jnp.stack(at).astype(jnp.int32)
            self.keep = keep.reshape(shape)
            each = len(sends) // shape[0]
            self.crosses = [
                across(send).reshape(shape[1] // each, *shape[2:]) for send in sends
            ]
            self.from_y = []
            self.from_z = []

        def step(self, shift, stage, split=False):
            got = self.order.after(self.keep, *self.crosses, *self.from_y, *self.from_z)
            lead = 1 + len(self.crosses)
            count = lead + len(self.from_y)
            out = reduce_step(
                self.place, got[0], got[1:lead], got[lead:count], got[count:], shift, stage, ny, split
            )
            self.order.did(out[0] if split else out)
            return out

        def send_y(self):
            from_y = []
            for s in range(1, ny):
                from_y.append(along_y(self.step(s, "y"), s))
            self.from_y = from_y

        def send_z(self):
            bit = len(self.from_z)
            self.from_z.append(along_z(self.step(0, "z"), 1 << bit))

        def finish(self):
            out = self.step(0, "end", True)
            self.held = [out[0]] + [along_x(out[s], s) for s in range(1, len(out))]
            if len(out) == 1:
                self.share_y(out[0])

        def share_y(self, value):
            self.held = [value] + [along_y(value, s) for s in range(1, ny)]

        def stacked(self, place, size, inner=False):
            places = jnp.stack([(place - s) % size for s in range(size)]).astype(jnp.int32)
            value = stack(self.order.after(*self.held), places, inner)
            self.order.did(value)
            return value

        def stack_x(self):
            self.share_y(self.stacked(self.at[0], nx))

        def stack_y(self, inner=False):
            value = self.stacked(self.at[1], ny, inner)
            self.held = [value, across(value)]

    def local(inputs, hidden_pre, cotangent, w_in, m_in, v_in, w_out, m_out, v_out):
        model = inputs.shape[1]
        hidden_width = hidden_pre.shape[1]
        shard = hidden_width // (nz * nx)
        rows = model // (nz * nx)
        cuts = widths(shard)
        chunks = range(len(cuts))
        last = len(cuts) - 1
        starts = [sum(cuts[:k]) for k in chunks]
        scale_in = 1.0 / math.sqrt(model)
        scale_out = 1.0 / math.sqrt(hidden_width)
        place = lax.axis_index("gx")
        side = lax.axis_index("gy")
        z, x = place // nx, place % nx
        y, c = side // CORES, side % CORES
        core = jnp.reshape(c, (1,)).astype(jnp.int32)
        at_core = jnp.stack([c, z]).astype(jnp.int32)
        order = Order()

        packs, hiddens = [], []
        for t in range(1, nx):
            sent = pack(*order.after(hidden_pre, cotangent), (x + t) % nx, nz, nx, cuts)
            order.did(sent)
            packs.append(along_x(sent, t))

        part = half_rows(*order.after(w_out), core)
        order.did(part)
        flipped = transposed(*order.after(inputs))
        order.did(flipped)
        columns = [flipped] + [along_x(flipped, t) for t in range(1, nx)]
        own = pack(*order.after(hidden_pre, cotangent), x, nz, nx, cuts)
        order.did(own)
        for t in range(nx):
            value = pack_later(*order.after(hidden_pre), (x + t) % nx, nz, nx, cuts)
            if value:
                order.did(value[0])
            hiddens.append([along_x(h, t) for h in value] if t else value)
        found = {0: part, nz // 2: along_z(part, nz // 2)}
        bit = nz // 4
        while bit:
            for key in list(found):
                value = found[key]
                if key:
                    (value,) = order.after(value)
                found[key ^ bit] = along_z(value, bit)
            bit //= 2
        found = [found[key] for key in range(nz)]
        crossed = [across(value) for value in [*order.after(*found[: nz // 2]), *found[nz // 2 :]]]
        packs = [own] + packs

        parts = [2] + [2] * last
        outs = [None for _ in chunks]
        pieces_in = [(0, 0, cuts[0])]
        if last:
            pieces_in.append((1, 0, cuts[1]))
        ins = [None for _ in pieces_in]
        pres = [None for _ in chunks]

        def tokens(k, *more):
            later = [] if k == 0 else [value[k - 1] for value in hiddens]
            got = order.after(*packs, *later, *more)
            count = nx + len(later)
            blocks = Tokens(got[:nx], got[nx:count] if later else None, model, nz, cuts[k])
            return blocks, got[count:]

        def start_out(k):
            blocks, _ = tokens(k, *([*crossed[: nz // 2], found[nz // 2]] if k == 0 else []))
            *sends, keep = grad_out_chunk(blocks, core, nz, scale_out, parts[k])
            order.did(keep)
            shape = (parts[k], nz, 1, ny, cuts[k] // parts[k] // ny, model // CORES)
            outs[k] = Reduce(order, (x, y, z), sends, keep, shape)

        def start_pre(k):
            blocks, got = tokens(k, *found, *crossed)
            pres[k] = grad_pre_chunk(blocks, got[:nz], got[nz:], nz, starts[k], at_core, scale_out)
            order.did(pres[k])

        def start_in(k):
            chunk, block, width = pieces_in[k]
            got = order.after(pres[chunk], *columns)
            *sends, keep = grad_in_chunk(
                got[0], got[1:], core, scale_in, (1 if chunk else 1), block, width
            )
            order.did(keep)
            shape = (nz // CORES, nz, nx, ny, rows // ny, width)
            ins[k] = Reduce(order, (x, y, z), sends, keep, shape)

        def sums(tile):
            tiles = order.after(tile, *[along_z(tile, flip) for flip in range(1, nz)])
            tile = add_tiles(tiles)
            order.did(tile)
            return [tile] + [along_x(tile, t) for t in range(1, nx)]

        def new_weights(weight, update, tiles, at):
            got = order.after(weight, update, *tiles)
            value = step_weights(got[0], got[1], got[2:], at)
            order.did(value)
            return value

        def moments_out(tile):
            half = model // CORES
            got = order.after(
                w_out,
                m_out,
                v_out,
                tile,
                *[outs[k].held[0] for k in chunks],
                *[outs[k].held[1] for k in chunks],
            )
            new = moments_kernel(
                core,
                *got[:3],
                got[4 : 5 + last],
                got[5 + last :],
                (CORES,),
                pl.BlockSpec((shard, half), lambda n, c: (0, n)),
                [
                    pl.BlockSpec((p, ny, w // p // ny, half), lambda n, c: (0, 0, 0, 0))
                    for w, p in zip(cuts, parts)
                ],
                lambda n: n,
                0,
                [got[3]],
            )
            order.did(new[3])
            return new

        start_out(0)
        outs[0].send_y()
        start_pre(0)
        start_in(0)
        outs[0].send_z()
        ins[0].send_y()
        if last:
            start_pre(1)
            start_in(1)
            outs[0].send_z()
            start_out(1)
            ins[1].send_y()
            outs[1].send_y()
            ins[0].send_z()
            ins[1].send_z()
            outs[0].finish()
            ins[0].send_z()
            outs[1].send_z()
            ins[1].send_z()
            ins[0].finish()
            outs[0].stack_y(True)
            outs[1].send_z()
            ins[1].finish()
            ins[1].stack_x()
            ins[0].stack_x()
            ins[0].stack_y()
            outs[1].finish()
            ins[1].stack_y()
        else:
            outs[0].send_z()
            ins[0].send_z()
            outs[0].finish()
            ins[0].send_z()
            ins[0].finish()
            ins[0].stack_x()
            ins[0].stack_y()

        held = [value.held for value in ins]
        got = order.after(w_in, m_in, v_in, *[pair[0] for pair in held], *[pair[1] for pair in held])
        mine, other = got[3 : 3 + len(ins)], got[3 + len(ins) :]
        if shard % LANES:
            joined = [
                jnp.stack([jnp.where(c == 0, a, b), jnp.where(c == 0, b, a)]) for a, b in zip(mine, other)
            ]
            grad = jnp.concatenate(joined, axis=-1).transpose(1, 4, 0, 3, 2, 5)
            grad = grad.reshape(rows, hidden_width).astype(F32)
            first_in, second_in, update_in = moments(*got[:3], grad)
            tile = jnp.concatenate(
                [
                    jnp.sum((value * value).reshape(-1, 8, LANES), axis=0)
                    for value in (w_in, update_in)
                ]
            )
        else:
            zs = nz // CORES
            first_in, second_in, update_in, tile = moments_kernel(
                core,
                *got[:3],
                mine,
                other,
                (nz * nx,),
                pl.BlockSpec((rows, shard), lambda n, c: (0, n)),
                [
                    pl.BlockSpec(
                        (ny, 1, 1, rows // ny, w), lambda n, c: (0, n % nx, n // nx % zs, 0, 0)
                    )
                    for _, _, w in pieces_in
                ],
                lambda n: n // nx // zs,
                1,
                [],
            )
        order.did(tile)

        outs[last].stack_y(True)
        first_out, second_out, update_out, tile = moments_out(tile)
        tiles = sums(tile)
        new_w_in = new_weights(w_in, update_in, tiles, 16)
        new_w_out = new_weights(w_out, update_out, tiles, 0)
        return (new_w_in, first_in, second_in, new_w_out, first_out, second_out)

    return local


def solution(mesh):
    gx, gy = mesh.shape["gx"], mesh.shape["gy"]
    nz = CHIPS_Z
    state = P("gx", None)
    tokens = P(("gx", "gy"), None)
    return jax.shard_map(
        plan(nz, gx // nz, gy // CORES),
        mesh=mesh,
        in_specs=(tokens,) * 3 + (state,) * 6,
        out_specs=(state,) * 6,
        check_vma=False,
    )
```

```python
import functools
import math

import jax
import jax.numpy as jnp
from jax import lax
from jax.experimental import pallas as pl
from jax.experimental.pallas import tpu as pltpu
from jax.sharding import PartitionSpec as P

BF16 = jnp.bfloat16
F32 = jnp.float32
CORES = 2
CHIPS_Z = 4
LANES = 128
PARTS = 2
VMEM = 16 * 1024 * 1024
WIDE = 56 * 1024 * 1024
SMALL = 4 * 1024 * 1024
STATE = 8 * 1024 * 1024


def moments(weight, first, second, grad):
    new_first = 0.9 * first + 0.1 * grad
    new_second = 0.95 * second + 0.05 * grad * grad
    update = new_first / (jnp.sqrt(new_second) + 1e-06) + 0.05 * weight
    return (new_first, new_second, update)


def squares(value):
    return jnp.sum(value * value)


def gelu(value):
    return 0.5 * value * (1.0 + lax.erf(value * (1.0 / math.sqrt(2.0))))


def gelu_slope(value):
    cdf = 0.5 * (1.0 + lax.erf(value * (1.0 / math.sqrt(2.0))))
    return cdf + value * (jnp.exp(-0.5 * value * value) * (1.0 / math.sqrt(2.0 * math.pi)))


def widths(shard):
    if shard % LANES:
        return (shard,)
    first = shard // LANES * 3 // 5 * LANES
    return (first, shard - first)


def dot(left, right, dims):
    return lax.dot_general(left, right, (dims, ((), ())), preferred_element_type=F32)


def params(grant=VMEM):
    return dict(
        compiler_params=pltpu.CompilerParams(vmem_limit_bytes=grant),
        cost_estimate=pl.CostEstimate(flops=1, bytes_accessed=1, transcendentals=0),
    )


def pack(hidden, cotangent, at, nz, nx, cuts):
    tokens, hidden_width = hidden.shape
    model = cotangent.shape[1]
    shard = hidden_width // (nz * nx)
    first = cuts[0]
    if shard % LANES:
        parts = [
            lax.dynamic_slice_in_dim(hidden, (z * nx + at) * shard, shard, 1).T for z in range(nz)
        ]
        return jnp.concatenate([cotangent.T, *parts])

    def body(at_ref, h_ref, cot_ref, out_ref):
        z = pl.program_id(0)

        @pl.when(z == 0)
        def _():
            out_ref[:model] = cot_ref[...].T

        out_ref[pl.ds(pl.multiple_of(model + z * first, LANES), first)] = h_ref[:, :first].T

    total = model + nz * first
    return pl.pallas_call(
        body,
        grid_spec=pltpu.PrefetchScalarGridSpec(
            num_scalar_prefetch=1,
            grid=(nz,),
            in_specs=[
                pl.BlockSpec((tokens, shard), lambda z, a: (0, z * nx + a[0])),
                pl.BlockSpec((tokens, model), lambda z, a: (0, 0)),
            ],
            out_specs=pl.BlockSpec((total, tokens), lambda z, a: (0, 0)),
        ),
        out_shape=jax.ShapeDtypeStruct((total, tokens), BF16),
        **params(WIDE),
    )(jnp.reshape(at, (1,)).astype(jnp.int32), hidden, cotangent)


def pack_later(hidden, at, nz, nx, cuts):
    tokens, hidden_width = hidden.shape
    shard = hidden_width // (nz * nx)
    if len(cuts) == 1:
        return []

    def body(at_ref, h_ref, *out_refs):
        start = cuts[0]
        for width, out_ref in zip(cuts[1:], out_refs):
            out_ref[0] = h_ref[:, start : start + width].T
            start += width

    return pl.pallas_call(
        body,
        grid_spec=pltpu.PrefetchScalarGridSpec(
            num_scalar_prefetch=1,
            grid=(nz,),
            in_specs=[pl.BlockSpec((tokens, shard), lambda z, a: (0, z * nx + a[0]))],
            out_specs=[pl.BlockSpec((1, w, tokens), lambda z, a: (z, 0, 0)) for w in cuts[1:]],
        ),
        out_shape=[jax.ShapeDtypeStruct((nz, w, tokens), BF16) for w in cuts[1:]],
        **params(WIDE),
    )(jnp.reshape(at, (1,)).astype(jnp.int32), hidden)


def once(shape, index_map):
    return pl.BlockSpec(shape, index_map, pipeline_mode=pl.Buffered(1))


class Tokens:
    def __init__(self, packs, hiddens, model, nz, width):
        tokens = packs[0].shape[1]
        self.model, self.width, self.count = model, width, len(packs)
        if hiddens is None:
            self.arrays = list(packs)
            self.specs = [once(packs[0].shape, lambda z, c: (0, 0))] * len(packs)
        else:
            self.arrays = [*packs, *hiddens]
            self.specs = [once((model, tokens), lambda z, c: (0, 0))] * len(packs)
            self.specs += [pl.BlockSpec((1, width, tokens), lambda z, c: (z, 0, 0))] * len(packs)

    def cot(self, refs, n):
        return refs[n].at[: self.model]

    def hidden(self, refs, n):
        if len(refs) == self.count:
            row = self.model + pl.program_id(0) * self.width
            return refs[n][pl.ds(pl.multiple_of(row, 16), self.width)].astype(F32)
        return refs[self.count + n][0].astype(F32)


def grad_out_chunk(tokens, core, nz, scale, parts):
    width, model = tokens.width, tokens.model
    half = model // CORES
    high = width // parts
    count = len(tokens.arrays)

    def body(c_ref, *refs):
        ins, outs = refs[:count], refs[count:]
        acts = jnp.concatenate(
            [gelu(tokens.hidden(ins, n)).astype(BF16) for n in range(tokens.count)], axis=1
        )
        for which in range(2):
            cols = pl.ds(pl.multiple_of((c_ref[0] + 1 + which) % CORES * half, 16), half)
            right = jnp.concatenate([tokens.cot(ins, n)[cols, :] for n in range(tokens.count)], axis=1)
            total = (dot(acts, right, ((1,), (1,))) * scale).astype(BF16)
            for p in range(parts):
                value = total[p * high : (p + 1) * high]
                if which:
                    outs[parts][p, 0] = value
                else:
                    outs[p][0] = value

    return pl.pallas_call(
        body,
        grid_spec=pltpu.PrefetchScalarGridSpec(
            num_scalar_prefetch=1,
            grid=(nz,),
            in_specs=tokens.specs,
            out_specs=[pl.BlockSpec((1, high, half), lambda z, c: (z, 0, 0))] * parts
            + [pl.BlockSpec((parts, 1, high, half), lambda z, c: (0, z, 0, 0))],
        ),
        out_shape=[jax.ShapeDtypeStruct((nz, high, half), BF16)] * parts
        + [jax.ShapeDtypeStruct((parts, nz, high, half), BF16)],
        **params(),
    )(core, *tokens.arrays)


def grad_pre_chunk(tokens, mine, other, nz, row, core, scale):
    part, model = mine[0].shape
    width = tokens.width
    count = len(tokens.arrays)
    long = tokens.arrays[0].shape[1]

    def body(c_ref, *refs):
        ins = refs[:count]
        out_ref, w_ref = refs[count + 2 * nz :]
        for h in range(nz):

            @pl.when((pl.program_id(0) ^ c_ref[1]) == h)
            def _(h=h):
                for at, ref in ((c_ref[0], refs[count + h]), (1 - c_ref[0], refs[count + nz + h])):
                    w_ref[pl.ds(pl.multiple_of(at * part, 16), part), :] = ref[...]

        w = w_ref[row : row + width, :]
        for n in range(tokens.count):
            grad_act = dot(w, tokens.cot(ins, n)[...], ((1,), (0,))) * scale
            out_ref[0, :, n * long : (n + 1) * long] = (
                grad_act * gelu_slope(tokens.hidden(ins, n))
            ).astype(BF16)

    w_specs = [once((part, model), lambda z, c: (0, 0))] * nz
    return pl.pallas_call(
        body,
        grid_spec=pltpu.PrefetchScalarGridSpec(
            num_scalar_prefetch=1,
            grid=(nz,),
            in_specs=tokens.specs + w_specs * 2,
            out_specs=pl.BlockSpec((1, width, tokens.count * long), lambda z, c: (z, 0, 0)),
            scratch_shapes=[pltpu.VMEM((CORES * part, model), BF16)],
        ),
        out_shape=jax.ShapeDtypeStruct((nz, width, tokens.count * long), BF16),
        **params(),
    )(core, *tokens.arrays, *mine, *other)


def grad_in_chunk(grads, inputs, core, scale, cut, block, width):
    nz, _, long = grads.shape
    model, tokens = inputs[0].shape
    count = len(inputs)
    half = nz // CORES
    high = model // cut

    def body(c_ref, g_ref, *refs):
        in_refs, outs = refs[:count], refs[count:]
        left = jnp.concatenate([i[...] for i in in_refs], axis=1)
        total = (dot(left, g_ref[0], ((1,), (1,))) * scale).astype(BF16)
        step = pl.program_id(0)
        for n in range(half):

            @pl.when(step == n)
            def _(n=n):
                for h in range(cut):
                    outs[n * cut + h][...] = total[h * high : (h + 1) * high]

        @pl.when(step >= half)
        def _():
            outs[-1][0] = total

    return pl.pallas_call(
        body,
        grid_spec=pltpu.PrefetchScalarGridSpec(
            num_scalar_prefetch=1,
            grid=(nz,),
            in_specs=[
                pl.BlockSpec(
                    (1, width, long),
                    lambda z, c: ((c[0] + 1 + z // half) % CORES * half + z % half, block, 0),
                )
            ]
            + [once((model, tokens), lambda z, c: (0, 0))] * count,
            out_specs=[pl.BlockSpec((high, width), lambda z, c: (0, 0))] * (half * cut)
            + [pl.BlockSpec((1, model, width), lambda z, c: (jnp.maximum(z - half, 0), 0, 0))],
        ),
        out_shape=[jax.ShapeDtypeStruct((high, width), BF16)] * (half * cut)
        + [jax.ShapeDtypeStruct((half, model, width), BF16)],
        **params(),
    )(core, grads, *inputs)


def transposed(value):
    rows, cols = value.shape
    wide = 2 * LANES

    def body(in_ref, out_ref):
        out_ref[...] = in_ref[...].T

    return pl.pallas_call(
        body,
        grid=(cols // wide,),
        in_specs=[pl.BlockSpec((rows, wide), lambda n: (0, n))],
        out_specs=pl.BlockSpec((wide, rows), lambda n: (n, 0)),
        out_shape=jax.ShapeDtypeStruct((cols, rows), value.dtype),
        **params(),
    )(value)


def half_rows(weight, core):
    rows, cols = weight.shape
    high = rows // CORES // 2

    def body(c_ref, in_ref, out_ref):
        out_ref[...] = in_ref[...].astype(BF16)

    return pl.pallas_call(
        body,
        grid_spec=pltpu.PrefetchScalarGridSpec(
            num_scalar_prefetch=1,
            grid=(2,),
            in_specs=[pl.BlockSpec((high, cols), lambda n, c: (c[0] * 2 + n, 0))],
            out_specs=pl.BlockSpec((high, cols), lambda n, c: (n, 0)),
        ),
        out_shape=jax.ShapeDtypeStruct((2 * high, cols), BF16),
        **params(WIDE),
    )(core, weight)


def stack(pieces, places, inner=False):
    count = len(pieces)
    shape = pieces[0].shape
    out = (shape[0], count, *shape[1:]) if inner else (count, *shape)

    def body(at_ref, *refs):
        for n in range(count):
            if inner:
                for p in range(shape[0]):
                    refs[count][p, at_ref[n]] = refs[n][p]
            else:
                refs[count][at_ref[n]] = refs[n][...]

    return pl.pallas_call(
        body,
        grid_spec=pltpu.PrefetchScalarGridSpec(
            num_scalar_prefetch=1,
            grid=(),
            in_specs=[pl.BlockSpec(shape, lambda at: (0,) * len(shape))] * count,
            out_specs=pl.BlockSpec(out, lambda at: (0,) * len(out)),
        ),
        out_shape=jax.ShapeDtypeStruct(out, pieces[0].dtype),
        **params(SMALL),
    )(places, *pieces)


def add_tiles(tiles):
    def body(*refs):
        refs[-1][...] = sum(ref[...] for ref in refs[:-1])

    return pl.pallas_call(
        body, out_shape=jax.ShapeDtypeStruct(tiles[0].shape, F32), **params(SMALL)
    )(*tiles)


def reduce_step(place, keep, crosses, from_y, from_z, shift, stage, ny, split):
    lead, nz, mid, _, high, wide = keep.shape
    bit = len(from_z)

    def zed(n, at):
        if stage == "y":
            return n
        if stage == "end":
            return at[2]
        low = at[2] % (1 << bit)
        mine = (at[2] // (1 << bit)) % 2
        return n * (2 << bit) + (1 - mine) * (1 << bit) + low

    count = {"y": nz, "z": nz >> (bit + 1), "end": 1}[stage]
    six = (lead, 1, mid, 1, high, wide)
    five = (lead, 1, mid, high, wide)
    specs = [pl.BlockSpec(six, lambda n, at: (0, zed(n, at), 0, (at[1] + shift) % ny, 0, 0))]
    each = len(crosses) // lead
    long = nz // each
    for h in range(len(crosses)):
        specs.append(
            pl.BlockSpec(
                six[1:],
                lambda n, at, h=h % each: (
                    jnp.clip(zed(n, at) - h * long, 0, long - 1),
                    0,
                    (at[1] + shift) % ny,
                    0,
                    0,
                ),
            )
        )
    specs += [pl.BlockSpec(five, lambda n, at: (0, zed(n, at), 0, 0, 0))] * len(from_y)
    specs += [
        pl.BlockSpec(five, lambda n, at, j=j: (0, zed(n, at) // (2 << j), 0, 0, 0)) for j in range(bit)
    ]

    def body(at_ref, *refs):
        ins = refs[: len(specs)]
        outs = refs[len(specs) :]
        for p in range(lead):
            for m in range(mid):
                total = ins[1 + p * each][0, m, 0]
                for h in range(1, each):
                    total = jnp.where(
                        zed(pl.program_id(0), at_ref) >= h * long, ins[1 + p * each + h][0, m, 0], total
                    )
                total = total.astype(F32) + ins[0][p, 0, m, 0].astype(F32)
                for ref in ins[1 + len(crosses) :]:
                    total = total + ref[p, 0, m].astype(F32)
                total = total.astype(BF16)
                if not split:
                    outs[0][p, 0, m] = total
                    continue
                for s in range(mid):

                    @pl.when((at_ref[0] + s) % mid == m)
                    def _(s=s, total=total):
                        outs[s][p] = total

    if split:
        out_specs = [pl.BlockSpec((lead, high, wide), lambda n, at: (0, 0, 0))] * mid
        out_shape = [jax.ShapeDtypeStruct((lead, high, wide), BF16)] * mid
    else:
        out_specs = [pl.BlockSpec(five, lambda n, at: (0, n, 0, 0, 0))]
        out_shape = [jax.ShapeDtypeStruct((lead, count, mid, high, wide), BF16)]
    out = pl.pallas_call(
        body,
        grid_spec=pltpu.PrefetchScalarGridSpec(
            num_scalar_prefetch=1, grid=(count,), in_specs=specs, out_specs=out_specs
        ),
        out_shape=out_shape,
        **params(SMALL),
    )(place, keep, *crosses, *from_y, *from_z)
    return out if split else out[0]


def moments_kernel(core, weight, first, second, mine, other, grid, state_spec, grad_specs, owner, axis, tiles):
    block = state_spec.block_shape
    count = len(mine)
    long = 16 * (1 + len(tiles))

    def body(c_ref, w_ref, m_ref, v_ref, *refs):
        mine_refs, other_refs = refs[:count], refs[count : 2 * count]
        tile_refs = refs[2 * count : 2 * count + len(tiles)]
        new_m_ref, new_v_ref, u_ref, sum_ref = refs[2 * count + len(tiles) :]
        totals = [jnp.zeros((8, LANES), F32)] * 2
        start = 0
        ours = owner(pl.program_id(0)) == c_ref[0]
        for mine_ref, other_ref in zip(mine_refs, other_refs):
            size = mine_ref.size // block[1 - axis]
            shape = (size, block[1]) if axis == 0 else (block[0], size)
            at = (slice(start, start + size), slice(None))
            at = at if axis == 0 else at[::-1]
            grad = jnp.where(ours, mine_ref[...].reshape(shape), other_ref[...].reshape(shape)).astype(F32)
            weight = w_ref[at]
            new_m, new_v, update = moments(weight, m_ref[at], v_ref[at], grad)
            new_m_ref[at] = new_m
            new_v_ref[at] = new_v
            u_ref[at] = update
            for n, value in enumerate((weight, update)):
                square = value * value
                for col in range(0, shape[1], LANES):
                    totals[n] = totals[n] + square[:, col : col + LANES].reshape(-1, 8, LANES).sum(0)
            start += size

        @pl.when(pl.program_id(0) == 0)
        def _():
            sum_ref[:16] = jnp.zeros((16, LANES), F32)
            for n, tile_ref in enumerate(tile_refs):
                sum_ref[16 * (n + 1) : 16 * (n + 2)] = tile_ref[...]

        sum_ref[:8] += totals[0]
        sum_ref[8:16] += totals[1]

    state = jax.ShapeDtypeStruct(weight.shape, F32)
    return pl.pallas_call(
        body,
        grid_spec=pltpu.PrefetchScalarGridSpec(
            num_scalar_prefetch=1,
            grid=grid,
            in_specs=[state_spec] * 3
            + grad_specs * 2
            + [pl.BlockSpec((16, LANES), lambda n, c: (0, 0))] * len(tiles),
            out_specs=[state_spec] * 3 + [pl.BlockSpec((long, LANES), lambda n, c: (0, 0))],
        ),
        out_shape=[state] * 3 + [jax.ShapeDtypeStruct((long, LANES), F32)],
        **params(STATE),
    )(core, weight, first, second, *mine, *other, *tiles)


def step_weights(weight, update, tiles, at):
    rows, cols = weight.shape
    high = rows // 5
    count = len(tiles)

    def body(w_ref, u_ref, *refs):
        sums = sum(ref[at : at + 16] for ref in refs[:count])
        ratio = jnp.sqrt(jnp.sum(sums[:8], keepdims=True)) / jnp.sqrt(jnp.sum(sums[8:], keepdims=True))
        refs[count][...] = w_ref[...] - 0.4 * ratio * u_ref[...]

    spec = pl.BlockSpec((high, cols), lambda n: (n, 0))
    tile = pl.BlockSpec(tiles[0].shape, lambda n: (0, 0))
    return pl.pallas_call(
        body,
        grid=(rows // high,),
        in_specs=[spec] * 2 + [tile] * count,
        out_specs=spec,
        out_shape=jax.ShapeDtypeStruct(weight.shape, F32),
        **params(STATE),
    )(weight, update, *tiles)


class Order:
    def __init__(self):
        self.last = None

    def after(self, *values):
        if self.last is None:
            return values
        return lax.optimization_barrier((*values, self.last))[:-1]

    def did(self, value):
        self.last = value


def plan(nz, nx, ny):
    def along_x(value, step):
        pairs = [
            (z * nx + x, z * nx + (x + step) % nx) for z in range(nz) for x in range(nx)
        ]
        return lax.ppermute(value, "gx", pairs)

    def along_z(value, flip):
        pairs = [(z * nx + x, (z ^ flip) * nx + x) for z in range(nz) for x in range(nx)]
        return lax.ppermute(value, "gx", pairs)

    def along_y(value, step):
        pairs = [
            (y * CORES + c, (y + step) % ny * CORES + c) for y in range(ny) for c in range(CORES)
        ]
        return lax.ppermute(value, "gy", pairs)

    def across(value):
        pairs = [(k, k ^ 1) for k in range(ny * CORES)]
        return lax.ppermute(value, "gy", pairs)

    class Reduce:
        def __init__(self, order, at, sends, keep, shape):
            self.order, self.at, self.place = order, at, jnp.stack(at).astype(jnp.int32)
            self.keep = keep.reshape(shape)
            each = len(sends) // shape[0]
            self.crosses = [
                across(send).reshape(shape[1] // each, *shape[2:]) for send in sends
            ]
            self.from_y = []
            self.from_z = []

        def step(self, shift, stage, split=False):
            got = self.order.after(self.keep, *self.crosses, *self.from_y, *self.from_z)
            lead = 1 + len(self.crosses)
            count = lead + len(self.from_y)
            out = reduce_step(
                self.place, got[0], got[1:lead], got[lead:count], got[count:], shift, stage, ny, split
            )
            self.order.did(out[0] if split else out)
            return out

        def send_y(self):
            from_y = []
            for s in range(1, ny):
                from_y.append(along_y(self.step(s, "y"), s))
            self.from_y = from_y

        def send_z(self):
            bit = len(self.from_z)
            self.from_z.append(along_z(self.step(0, "z"), 1 << bit))

        def finish(self):
            out = self.step(0, "end", True)
            self.held = [out[0]] + [along_x(out[s], s) for s in range(1, len(out))]
            if len(out) == 1:
                self.share_y(out[0])

        def share_y(self, value):
            self.held = [value] + [along_y(value, s) for s in range(1, ny)]

        def stacked(self, place, size, inner=False):
            places = jnp.stack([(place - s) % size for s in range(size)]).astype(jnp.int32)
            value = stack(self.order.after(*self.held), places, inner)
            self.order.did(value)
            return value

        def stack_x(self):
            self.share_y(self.stacked(self.at[0], nx))

        def stack_y(self, inner=False):
            value = self.stacked(self.at[1], ny, inner)
            self.held = [value, across(value)]

    def local(inputs, hidden_pre, cotangent, w_in, m_in, v_in, w_out, m_out, v_out):
        model = inputs.shape[1]
        hidden_width = hidden_pre.shape[1]
        shard = hidden_width // (nz * nx)
        rows = model // (nz * nx)
        cuts = widths(shard)
        chunks = range(len(cuts))
        last = len(cuts) - 1
        starts = [sum(cuts[:k]) for k in chunks]
        scale_in = 1.0 / math.sqrt(model)
        scale_out = 1.0 / math.sqrt(hidden_width)
        place = lax.axis_index("gx")
        side = lax.axis_index("gy")
        z, x = place // nx, place % nx
        y, c = side // CORES, side % CORES
        core = jnp.reshape(c, (1,)).astype(jnp.int32)
        at_core = jnp.stack([c, z]).astype(jnp.int32)
        order = Order()

        packs, hiddens = [], []
        for t in range(1, nx):
            sent = pack(*order.after(hidden_pre, cotangent), (x + t) % nx, nz, nx, cuts)
            order.did(sent)
            packs.append(along_x(sent, t))

        part = half_rows(*order.after(w_out), core)
        order.did(part)
        flipped = transposed(*order.after(inputs))
        order.did(flipped)
        columns = [flipped] + [along_x(flipped, t) for t in range(1, nx)]
        own = pack(*order.after(hidden_pre, cotangent), x, nz, nx, cuts)
        order.did(own)
        for t in range(nx):
            value = pack_later(*order.after(hidden_pre), (x + t) % nx, nz, nx, cuts)
            if value:
                order.did(value[0])
            hiddens.append([along_x(h, t) for h in value] if t else value)
        found = {0: part, nz // 2: along_z(part, nz // 2)}
        bit = nz // 4
        while bit:
            for key in list(found):
                value = found[key]
                if key:
                    (value,) = order.after(value)
                found[key ^ bit] = along_z(value, bit)
            bit //= 2
        found = [found[key] for key in range(nz)]
        crossed = [across(value) for value in [*order.after(*found[: nz // 2]), *found[nz // 2 :]]]
        packs = [own] + packs

        parts = [2] + [2] * last
        outs = [None for _ in chunks]
        pieces_in = [(0, 0, cuts[0])]
        if last:
            pieces_in.append((1, 0, cuts[1]))
        ins = [None for _ in pieces_in]
        pres = [None for _ in chunks]

        def tokens(k, *more):
            later = [] if k == 0 else [value[k - 1] for value in hiddens]
            got = order.after(*packs, *later, *more)
            count = nx + len(later)
            blocks = Tokens(got[:nx], got[nx:count] if later else None, model, nz, cuts[k])
            return blocks, got[count:]

        def start_out(k):
            blocks, _ = tokens(k, *([*crossed[: nz // 2], found[nz // 2]] if k == 0 else []))
            *sends, keep = grad_out_chunk(blocks, core, nz, scale_out, parts[k])
            order.did(keep)
            shape = (parts[k], nz, 1, ny, cuts[k] // parts[k] // ny, model // CORES)
            outs[k] = Reduce(order, (x, y, z), sends, keep, shape)

        def start_pre(k):
            blocks, got = tokens(k, *found, *crossed)
            pres[k] = grad_pre_chunk(blocks, got[:nz], got[nz:], nz, starts[k], at_core, scale_out)
            order.did(pres[k])

        def start_in(k):
            chunk, block, width = pieces_in[k]
            got = order.after(pres[chunk], *columns)
            *sends, keep = grad_in_chunk(
                got[0], got[1:], core, scale_in, (1 if chunk else 1), block, width
            )
            order.did(keep)
            shape = (nz // CORES, nz, nx, ny, rows // ny, width)
            ins[k] = Reduce(order, (x, y, z), sends, keep, shape)

        def sums(tile):
            tiles = order.after(tile, *[along_z(tile, flip) for flip in range(1, nz)])
            tile = add_tiles(tiles)
            order.did(tile)
            return [tile] + [along_x(tile, t) for t in range(1, nx)]

        def new_weights(weight, update, tiles, at):
            got = order.after(weight, update, *tiles)
            value = step_weights(got[0], got[1], got[2:], at)
            order.did(value)
            return value

        def moments_out(tile):
            half = model // CORES
            got = order.after(
                w_out,
                m_out,
                v_out,
                tile,
                *[outs[k].held[0] for k in chunks],
                *[outs[k].held[1] for k in chunks],
            )
            new = moments_kernel(
                core,
                *got[:3],
                got[4 : 5 + last],
                got[5 + last :],
                (model // LANES,),
                pl.BlockSpec((shard, LANES), lambda n, c: (0, n)),
                [
                    pl.BlockSpec((p, ny, w // p // ny, LANES), lambda n, c: (0, 0, 0, n % (half // LANES)))
                    for w, p in zip(cuts, parts)
                ],
                lambda n: n // (half // LANES),
                0,
                [got[3]],
            )
            order.did(new[3])
            return new

        start_out(0)
        outs[0].send_y()
        start_pre(0)
        start_in(0)
        outs[0].send_z()
        ins[0].send_y()
        if last:
            start_pre(1)
            start_in(1)
            outs[0].send_z()
            start_out(1)
            ins[1].send_y()
            outs[1].send_y()
            ins[0].send_z()
            ins[1].send_z()
            ins[0].send_z()
            outs[1].send_z()
            ins[1].send_z()
            outs[0].finish()
            ins[0].finish()
            outs[1].send_z()
            ins[1].finish()
            ins[0].stack_x()
            ins[1].stack_x()
            outs[0].stack_y(True)
            ins[0].stack_y()
            outs[1].finish()
            ins[1].stack_y()
        else:
            outs[0].send_z()
            ins[0].send_z()
            outs[0].finish()
            ins[0].send_z()
            ins[0].finish()
            ins[0].stack_x()
            ins[0].stack_y()

        held = [value.held for value in ins]
        got = order.after(w_in, m_in, v_in, *[pair[0] for pair in held], *[pair[1] for pair in held])
        mine, other = got[3 : 3 + len(ins)], got[3 + len(ins) :]
        if shard % LANES:
            joined = [
                jnp.stack([jnp.where(c == 0, a, b), jnp.where(c == 0, b, a)]) for a, b in zip(mine, other)
            ]
            grad = jnp.concatenate(joined, axis=-1).transpose(1, 4, 0, 3, 2, 5)
            grad = grad.reshape(rows, hidden_width).astype(F32)
            first_in, second_in, update_in = moments(*got[:3], grad)
            tile = jnp.concatenate(
                [
                    jnp.sum((value * value).reshape(-1, 8, LANES), axis=0)
                    for value in (w_in, update_in)
                ]
            )
        else:
            zs = nz // CORES
            first_in, second_in, update_in, tile = moments_kernel(
                core,
                *got[:3],
                mine,
                other,
                (nz * nx,),
                pl.BlockSpec((rows, shard), lambda n, c: (0, n)),
                [
                    pl.BlockSpec(
                        (ny, 1, 1, rows // ny, w), lambda n, c: (0, n % nx, n // nx % zs, 0, 0)
                    )
                    for _, _, w in pieces_in
                ],
                lambda n: n // nx // zs,
                1,
                [],
            )
        order.did(tile)

        outs[last].stack_y(True)
        first_out, second_out, update_out, tile = moments_out(tile)
        tiles = sums(tile)
        new_w_in = new_weights(w_in, update_in, tiles, 16)
        new_w_out = new_weights(w_out, update_out, tiles, 0)
        return (new_w_in, first_in, second_in, new_w_out, first_out, second_out)

    return local


def solution(mesh):
    gx, gy = mesh.shape["gx"], mesh.shape["gy"]
    nz = CHIPS_Z
    state = P("gx", None)
    tokens = P(("gx", "gy"), None)
    return jax.shard_map(
        plan(nz, gx // nz, gy // CORES),
        mesh=mesh,
        in_specs=(tokens,) * 3 + (state,) * 6,
        out_specs=(state,) * 6,
        check_vma=False,
    )
```

```python
import functools
import math

import jax
import jax.numpy as jnp
from jax import lax
from jax.experimental import pallas as pl
from jax.experimental.pallas import tpu as pltpu
from jax.sharding import PartitionSpec as P

BF16 = jnp.bfloat16
F32 = jnp.float32
CORES = 2
CHIPS_Z = 4
LANES = 128
PARTS = 2
VMEM = 20 * 1024 * 1024
WIDE = 56 * 1024 * 1024
SMALL = 4 * 1024 * 1024


def moments(weight, first, second, grad):
    new_first = 0.9 * first + 0.1 * grad
    new_second = 0.95 * second + 0.05 * grad * grad
    update = new_first / (jnp.sqrt(new_second) + 1e-06) + 0.05 * weight
    return (new_first, new_second, update)


def squares(value):
    return jnp.sum(value * value)


def gelu(value):
    return 0.5 * value * (1.0 + lax.erf(value * (1.0 / math.sqrt(2.0))))


def gelu_slope(value):
    cdf = 0.5 * (1.0 + lax.erf(value * (1.0 / math.sqrt(2.0))))
    return cdf + value * (jnp.exp(-0.5 * value * value) * (1.0 / math.sqrt(2.0 * math.pi)))


def widths(shard):
    if shard % LANES:
        return (shard,)
    first = shard // LANES * 3 // 5 * LANES
    return (first, shard - first)


def dot(left, right, dims):
    return lax.dot_general(left, right, (dims, ((), ())), preferred_element_type=F32)


def params(grant=VMEM):
    return dict(
        compiler_params=pltpu.CompilerParams(vmem_limit_bytes=grant),
        cost_estimate=pl.CostEstimate(flops=1, bytes_accessed=1, transcendentals=0),
    )


def pack(hidden, cotangent, at, nz, nx, cuts):
    tokens, hidden_width = hidden.shape
    model = cotangent.shape[1]
    shard = hidden_width // (nz * nx)
    first = cuts[0]
    if shard % LANES:
        parts = [
            lax.dynamic_slice_in_dim(hidden, (z * nx + at) * shard, shard, 1).T for z in range(nz)
        ]
        return jnp.concatenate([cotangent.T, *parts])

    def body(at_ref, h_ref, cot_ref, out_ref):
        z = pl.program_id(0)

        @pl.when(z == 0)
        def _():
            out_ref[:model] = cot_ref[...].T

        out_ref[pl.ds(pl.multiple_of(model + z * first, LANES), first)] = h_ref[:, :first].T

    total = model + nz * first
    return pl.pallas_call(
        body,
        grid_spec=pltpu.PrefetchScalarGridSpec(
            num_scalar_prefetch=1,
            grid=(nz,),
            in_specs=[
                pl.BlockSpec((tokens, shard), lambda z, a: (0, z * nx + a[0])),
                pl.BlockSpec((tokens, model), lambda z, a: (0, 0)),
            ],
            out_specs=pl.BlockSpec((total, tokens), lambda z, a: (0, 0)),
        ),
        out_shape=jax.ShapeDtypeStruct((total, tokens), BF16),
        **params(WIDE),
    )(jnp.reshape(at, (1,)).astype(jnp.int32), hidden, cotangent)


def pack_later(hidden, at, nz, nx, cuts):
    tokens, hidden_width = hidden.shape
    shard = hidden_width // (nz * nx)
    if len(cuts) == 1:
        return []

    def body(at_ref, h_ref, *out_refs):
        start = cuts[0]
        for width, out_ref in zip(cuts[1:], out_refs):
            out_ref[0] = h_ref[:, start : start + width].T
            start += width

    return pl.pallas_call(
        body,
        grid_spec=pltpu.PrefetchScalarGridSpec(
            num_scalar_prefetch=1,
            grid=(nz,),
            in_specs=[pl.BlockSpec((tokens, shard), lambda z, a: (0, z * nx + a[0]))],
            out_specs=[pl.BlockSpec((1, w, tokens), lambda z, a: (z, 0, 0)) for w in cuts[1:]],
        ),
        out_shape=[jax.ShapeDtypeStruct((nz, w, tokens), BF16) for w in cuts[1:]],
        **params(WIDE),
    )(jnp.reshape(at, (1,)).astype(jnp.int32), hidden)


class Tokens:
    def __init__(self, packs, hiddens, model, nz, width):
        tokens = packs[0].shape[1]
        self.model, self.width, self.count = model, width, len(packs)
        if hiddens is None:
            self.arrays = list(packs)
            self.specs = [pl.BlockSpec(packs[0].shape, lambda z, c: (0, 0))] * len(packs)
        else:
            self.arrays = [*packs, *hiddens]
            self.specs = [pl.BlockSpec((model, tokens), lambda z, c: (0, 0))] * len(packs)
            self.specs += [pl.BlockSpec((1, width, tokens), lambda z, c: (z, 0, 0))] * len(packs)

    def cot(self, refs, n):
        return refs[n].at[: self.model]

    def hidden(self, refs, n):
        if len(refs) == self.count:
            row = self.model + pl.program_id(0) * self.width
            return refs[n][pl.ds(pl.multiple_of(row, 16), self.width)].astype(F32)
        return refs[self.count + n][0].astype(F32)


def grad_out_chunk(tokens, core, nz, scale, parts):
    width, model = tokens.width, tokens.model
    half = model // CORES
    high = width // parts
    count = len(tokens.arrays)

    def body(c_ref, *refs):
        ins, outs = refs[:count], refs[count:]
        acts = jnp.concatenate(
            [gelu(tokens.hidden(ins, n)).astype(BF16) for n in range(tokens.count)], axis=1
        )
        for which in range(2):
            cols = pl.ds(pl.multiple_of((c_ref[0] + 1 + which) % CORES * half, 16), half)
            right = jnp.concatenate([tokens.cot(ins, n)[cols, :] for n in range(tokens.count)], axis=1)
            total = (dot(acts, right, ((1,), (1,))) * scale).astype(BF16)
            for p in range(parts):
                value = total[p * high : (p + 1) * high]
                if which:
                    outs[parts][p, 0] = value
                else:
                    outs[p][0] = value

    return pl.pallas_call(
        body,
        grid_spec=pltpu.PrefetchScalarGridSpec(
            num_scalar_prefetch=1,
            grid=(nz,),
            in_specs=tokens.specs,
            out_specs=[pl.BlockSpec((1, high, half), lambda z, c: (z, 0, 0))] * parts
            + [pl.BlockSpec((parts, 1, high, half), lambda z, c: (0, z, 0, 0))],
        ),
        out_shape=[jax.ShapeDtypeStruct((nz, high, half), BF16)] * parts
        + [jax.ShapeDtypeStruct((parts, nz, high, half), BF16)],
        **params(),
    )(core, *tokens.arrays)


def grad_pre_chunk(tokens, mine, other, nz, row, core, scale):
    part, model = mine[0].shape
    width = tokens.width
    count = len(tokens.arrays)
    long = tokens.arrays[0].shape[1]

    def body(c_ref, *refs):
        ins = refs[:count]
        out_ref, w_ref = refs[count + 2 * nz :]
        for h in range(nz):

            @pl.when((pl.program_id(0) ^ c_ref[1]) == h)
            def _(h=h):
                for at, ref in ((c_ref[0], refs[count + h]), (1 - c_ref[0], refs[count + nz + h])):
                    w_ref[pl.ds(pl.multiple_of(at * part, 16), part), :] = ref[...]

        w = w_ref[row : row + width, :]
        for n in range(tokens.count):
            grad_act = dot(w, tokens.cot(ins, n)[...], ((1,), (0,))) * scale
            out_ref[0, :, n * long : (n + 1) * long] = (
                grad_act * gelu_slope(tokens.hidden(ins, n))
            ).astype(BF16)

    w_specs = [pl.BlockSpec((part, model), lambda z, c: (0, 0))] * nz
    return pl.pallas_call(
        body,
        grid_spec=pltpu.PrefetchScalarGridSpec(
            num_scalar_prefetch=1,
            grid=(nz,),
            in_specs=tokens.specs + w_specs * 2,
            out_specs=pl.BlockSpec((1, width, tokens.count * long), lambda z, c: (z, 0, 0)),
            scratch_shapes=[pltpu.VMEM((CORES * part, model), BF16)],
        ),
        out_shape=jax.ShapeDtypeStruct((nz, width, tokens.count * long), BF16),
        **params(),
    )(core, *tokens.arrays, *mine, *other)


def grad_in_chunk(grads, inputs, core, scale, cut, block, width):
    nz, _, long = grads.shape
    model, tokens = inputs[0].shape
    count = len(inputs)
    half = nz // CORES
    high = model // cut

    def body(c_ref, g_ref, *refs):
        in_refs, outs = refs[:count], refs[count:]
        left = jnp.concatenate([i[...] for i in in_refs], axis=1)
        total = (dot(left, g_ref[0], ((1,), (1,))) * scale).astype(BF16)
        step = pl.program_id(0)
        for n in range(half):

            @pl.when(step == n)
            def _(n=n):
                for h in range(cut):
                    outs[n * cut + h][...] = total[h * high : (h + 1) * high]

        @pl.when(step >= half)
        def _():
            outs[-1][0] = total

    return pl.pallas_call(
        body,
        grid_spec=pltpu.PrefetchScalarGridSpec(
            num_scalar_prefetch=1,
            grid=(nz,),
            in_specs=[
                pl.BlockSpec(
                    (1, width, long),
                    lambda z, c: ((c[0] + 1 + z // half) % CORES * half + z % half, block, 0),
                )
            ]
            + [pl.BlockSpec((model, tokens), lambda z, c: (0, 0))] * count,
            out_specs=[pl.BlockSpec((high, width), lambda z, c: (0, 0))] * (half * cut)
            + [pl.BlockSpec((1, model, width), lambda z, c: (jnp.maximum(z - half, 0), 0, 0))],
        ),
        out_shape=[jax.ShapeDtypeStruct((high, width), BF16)] * (half * cut)
        + [jax.ShapeDtypeStruct((half, model, width), BF16)],
        **params(),
    )(core, grads, *inputs)


def transposed(value):
    rows, cols = value.shape
    wide = 2 * LANES

    def body(in_ref, out_ref):
        out_ref[...] = in_ref[...].T

    return pl.pallas_call(
        body,
        grid=(cols // wide,),
        in_specs=[pl.BlockSpec((rows, wide), lambda n: (0, n))],
        out_specs=pl.BlockSpec((wide, rows), lambda n: (n, 0)),
        out_shape=jax.ShapeDtypeStruct((cols, rows), value.dtype),
        **params(),
    )(value)


def half_rows(weight, core):
    rows, cols = weight.shape
    high = rows // CORES // 2

    def body(c_ref, in_ref, out_ref):
        out_ref[...] = in_ref[...].astype(BF16)

    return pl.pallas_call(
        body,
        grid_spec=pltpu.PrefetchScalarGridSpec(
            num_scalar_prefetch=1,
            grid=(2,),
            in_specs=[pl.BlockSpec((high, cols), lambda n, c: (c[0] * 2 + n, 0))],
            out_specs=pl.BlockSpec((high, cols), lambda n, c: (n, 0)),
        ),
        out_shape=jax.ShapeDtypeStruct((2 * high, cols), BF16),
        **params(WIDE),
    )(core, weight)


def stack(pieces, places, inner=False):
    count = len(pieces)
    shape = pieces[0].shape
    out = (shape[0], count, *shape[1:]) if inner else (count, *shape)

    def body(at_ref, *refs):
        for n in range(count):
            if inner:
                for p in range(shape[0]):
                    refs[count][p, at_ref[n]] = refs[n][p]
            else:
                refs[count][at_ref[n]] = refs[n][...]

    return pl.pallas_call(
        body,
        grid_spec=pltpu.PrefetchScalarGridSpec(
            num_scalar_prefetch=1,
            grid=(),
            in_specs=[pl.BlockSpec(shape, lambda at: (0,) * len(shape))] * count,
            out_specs=pl.BlockSpec(out, lambda at: (0,) * len(out)),
        ),
        out_shape=jax.ShapeDtypeStruct(out, pieces[0].dtype),
        **params(SMALL),
    )(places, *pieces)


def add_tiles(tiles):
    def body(*refs):
        refs[-1][...] = sum(ref[...] for ref in refs[:-1])

    return pl.pallas_call(
        body, out_shape=jax.ShapeDtypeStruct(tiles[0].shape, F32), **params(SMALL)
    )(*tiles)


def reduce_step(place, keep, crosses, from_y, from_z, shift, stage, ny, split):
    lead, nz, mid, _, high, wide = keep.shape
    bit = len(from_z)

    def zed(n, at):
        if stage == "y":
            return n
        if stage == "end":
            return at[2]
        low = at[2] % (1 << bit)
        mine = (at[2] // (1 << bit)) % 2
        return n * (2 << bit) + (1 - mine) * (1 << bit) + low

    count = {"y": nz, "z": nz >> (bit + 1), "end": 1}[stage]
    six = (lead, 1, mid, 1, high, wide)
    five = (lead, 1, mid, high, wide)
    specs = [pl.BlockSpec(six, lambda n, at: (0, zed(n, at), 0, (at[1] + shift) % ny, 0, 0))]
    each = len(crosses) // lead
    long = nz // each
    for h in range(len(crosses)):
        specs.append(
            pl.BlockSpec(
                six[1:],
                lambda n, at, h=h % each: (
                    jnp.clip(zed(n, at) - h * long, 0, long - 1),
                    0,
                    (at[1] + shift) % ny,
                    0,
                    0,
                ),
            )
        )
    specs += [pl.BlockSpec(five, lambda n, at: (0, zed(n, at), 0, 0, 0))] * len(from_y)
    specs += [
        pl.BlockSpec(five, lambda n, at, j=j: (0, zed(n, at) // (2 << j), 0, 0, 0)) for j in range(bit)
    ]

    def body(at_ref, *refs):
        ins = refs[: len(specs)]
        outs = refs[len(specs) :]
        for p in range(lead):
            for m in range(mid):
                total = ins[1 + p * each][0, m, 0]
                for h in range(1, each):
                    total = jnp.where(
                        zed(pl.program_id(0), at_ref) >= h * long, ins[1 + p * each + h][0, m, 0], total
                    )
                total = total.astype(F32) + ins[0][p, 0, m, 0].astype(F32)
                for ref in ins[1 + len(crosses) :]:
                    total = total + ref[p, 0, m].astype(F32)
                total = total.astype(BF16)
                if not split:
                    outs[0][p, 0, m] = total
                    continue
                for s in range(mid):

                    @pl.when((at_ref[0] + s) % mid == m)
                    def _(s=s, total=total):
                        outs[s][p] = total

    if split:
        out_specs = [pl.BlockSpec((lead, high, wide), lambda n, at: (0, 0, 0))] * mid
        out_shape = [jax.ShapeDtypeStruct((lead, high, wide), BF16)] * mid
    else:
        out_specs = [pl.BlockSpec(five, lambda n, at: (0, n, 0, 0, 0))]
        out_shape = [jax.ShapeDtypeStruct((lead, count, mid, high, wide), BF16)]
    out = pl.pallas_call(
        body,
        grid_spec=pltpu.PrefetchScalarGridSpec(
            num_scalar_prefetch=1, grid=(count,), in_specs=specs, out_specs=out_specs
        ),
        out_shape=out_shape,
        **params(SMALL),
    )(place, keep, *crosses, *from_y, *from_z)
    return out if split else out[0]


def moments_kernel(core, weight, first, second, mine, other, grid, state_spec, grad_specs, owner, axis, tiles):
    block = state_spec.block_shape
    count = len(mine)
    long = 16 * (1 + len(tiles))

    def body(c_ref, w_ref, m_ref, v_ref, *refs):
        mine_refs, other_refs = refs[:count], refs[count : 2 * count]
        tile_refs = refs[2 * count : 2 * count + len(tiles)]
        new_m_ref, new_v_ref, u_ref, sum_ref = refs[2 * count + len(tiles) :]
        totals = [jnp.zeros((8, LANES), F32)] * 2
        start = 0
        ours = owner(pl.program_id(0)) == c_ref[0]
        for mine_ref, other_ref in zip(mine_refs, other_refs):
            size = mine_ref.size // block[1 - axis]
            shape = (size, block[1]) if axis == 0 else (block[0], size)
            at = (slice(start, start + size), slice(None))
            at = at if axis == 0 else at[::-1]
            grad = jnp.where(ours, mine_ref[...].reshape(shape), other_ref[...].reshape(shape)).astype(F32)
            weight = w_ref[at]
            new_m, new_v, update = moments(weight, m_ref[at], v_ref[at], grad)
            new_m_ref[at] = new_m
            new_v_ref[at] = new_v
            u_ref[at] = update
            for n, value in enumerate((weight, update)):
                square = value * value
                for col in range(0, shape[1], LANES):
                    totals[n] = totals[n] + square[:, col : col + LANES].reshape(-1, 8, LANES).sum(0)
            start += size

        @pl.when(pl.program_id(0) == 0)
        def _():
            sum_ref[:16] = jnp.zeros((16, LANES), F32)
            for n, tile_ref in enumerate(tile_refs):
                sum_ref[16 * (n + 1) : 16 * (n + 2)] = tile_ref[...]

        sum_ref[:8] += totals[0]
        sum_ref[8:16] += totals[1]

    state = jax.ShapeDtypeStruct(weight.shape, F32)
    return pl.pallas_call(
        body,
        grid_spec=pltpu.PrefetchScalarGridSpec(
            num_scalar_prefetch=1,
            grid=grid,
            in_specs=[state_spec] * 3
            + grad_specs * 2
            + [pl.BlockSpec((16, LANES), lambda n, c: (0, 0))] * len(tiles),
            out_specs=[state_spec] * 3 + [pl.BlockSpec((long, LANES), lambda n, c: (0, 0))],
        ),
        out_shape=[state] * 3 + [jax.ShapeDtypeStruct((long, LANES), F32)],
        **params(),
    )(core, weight, first, second, *mine, *other, *tiles)


def step_weights(weight, update, tiles, at):
    rows, cols = weight.shape
    high = rows // 5
    count = len(tiles)

    def body(w_ref, u_ref, *refs):
        sums = sum(ref[at : at + 16] for ref in refs[:count])
        ratio = jnp.sqrt(jnp.sum(sums[:8], keepdims=True)) / jnp.sqrt(jnp.sum(sums[8:], keepdims=True))
        refs[count][...] = w_ref[...] - 0.4 * ratio * u_ref[...]

    spec = pl.BlockSpec((high, cols), lambda n: (n, 0))
    tile = pl.BlockSpec(tiles[0].shape, lambda n: (0, 0))
    return pl.pallas_call(
        body,
        grid=(rows // high,),
        in_specs=[spec] * 2 + [tile] * count,
        out_specs=spec,
        out_shape=jax.ShapeDtypeStruct(weight.shape, F32),
        **params(),
    )(weight, update, *tiles)


class Order:
    def __init__(self):
        self.last = None

    def after(self, *values):
        if self.last is None:
            return values
        return lax.optimization_barrier((*values, self.last))[:-1]

    def did(self, value):
        self.last = value


def plan(nz, nx, ny):
    def along_x(value, step):
        pairs = [
            (z * nx + x, z * nx + (x + step) % nx) for z in range(nz) for x in range(nx)
        ]
        return lax.ppermute(value, "gx", pairs)

    def along_z(value, flip):
        pairs = [(z * nx + x, (z ^ flip) * nx + x) for z in range(nz) for x in range(nx)]
        return lax.ppermute(value, "gx", pairs)

    def along_y(value, step):
        pairs = [
            (y * CORES + c, (y + step) % ny * CORES + c) for y in range(ny) for c in range(CORES)
        ]
        return lax.ppermute(value, "gy", pairs)

    def across(value):
        pairs = [(k, k ^ 1) for k in range(ny * CORES)]
        return lax.ppermute(value, "gy", pairs)

    class Reduce:
        def __init__(self, order, at, sends, keep, shape):
            self.order, self.at, self.place = order, at, jnp.stack(at).astype(jnp.int32)
            self.keep = keep.reshape(shape)
            each = len(sends) // shape[0]
            self.crosses = [
                across(send).reshape(shape[1] // each, *shape[2:]) for send in sends
            ]
            self.from_y = []
            self.from_z = []

        def step(self, shift, stage, split=False):
            got = self.order.after(self.keep, *self.crosses, *self.from_y, *self.from_z)
            lead = 1 + len(self.crosses)
            count = lead + len(self.from_y)
            out = reduce_step(
                self.place, got[0], got[1:lead], got[lead:count], got[count:], shift, stage, ny, split
            )
            self.order.did(out[0] if split else out)
            return out

        def send_y(self):
            from_y = []
            for s in range(1, ny):
                from_y.append(along_y(self.step(s, "y"), s))
            self.from_y = from_y

        def send_z(self):
            bit = len(self.from_z)
            self.from_z.append(along_z(self.step(0, "z"), 1 << bit))

        def finish(self):
            out = self.step(0, "end", True)
            self.held = [out[0]] + [along_x(out[s], s) for s in range(1, len(out))]
            if len(out) == 1:
                self.share_y(out[0])

        def share_y(self, value):
            self.held = [value] + [along_y(value, s) for s in range(1, ny)]

        def stacked(self, place, size, inner=False):
            places = jnp.stack([(place - s) % size for s in range(size)]).astype(jnp.int32)
            value = stack(self.order.after(*self.held), places, inner)
            self.order.did(value)
            return value

        def stack_x(self):
            self.share_y(self.stacked(self.at[0], nx))

        def stack_y(self, inner=False):
            value = self.stacked(self.at[1], ny, inner)
            self.held = [value, across(value)]

    def local(inputs, hidden_pre, cotangent, w_in, m_in, v_in, w_out, m_out, v_out):
        model = inputs.shape[1]
        hidden_width = hidden_pre.shape[1]
        shard = hidden_width // (nz * nx)
        rows = model // (nz * nx)
        cuts = widths(shard)
        chunks = range(len(cuts))
        last = len(cuts) - 1
        starts = [sum(cuts[:k]) for k in chunks]
        scale_in = 1.0 / math.sqrt(model)
        scale_out = 1.0 / math.sqrt(hidden_width)
        place = lax.axis_index("gx")
        side = lax.axis_index("gy")
        z, x = place // nx, place % nx
        y, c = side // CORES, side % CORES
        core = jnp.reshape(c, (1,)).astype(jnp.int32)
        at_core = jnp.stack([c, z]).astype(jnp.int32)
        order = Order()

        packs, hiddens = [], []
        for t in range(1, nx):
            sent = pack(*order.after(hidden_pre, cotangent), (x + t) % nx, nz, nx, cuts)
            order.did(sent)
            packs.append(along_x(sent, t))

        part = half_rows(*order.after(w_out), core)
        order.did(part)
        flipped = transposed(*order.after(inputs))
        order.did(flipped)
        columns = [flipped] + [along_x(flipped, t) for t in range(1, nx)]
        own = pack(*order.after(hidden_pre, cotangent), x, nz, nx, cuts)
        order.did(own)
        for t in range(nx):
            value = pack_later(*order.after(hidden_pre), (x + t) % nx, nz, nx, cuts)
            if value:
                order.did(value[0])
            hiddens.append([along_x(h, t) for h in value] if t else value)
        found = {0: part, nz // 2: along_z(part, nz // 2)}
        bit = nz // 4
        while bit:
            for key in list(found):
                value = found[key]
                if key:
                    (value,) = order.after(value)
                found[key ^ bit] = along_z(value, bit)
            bit //= 2
        found = [found[key] for key in range(nz)]
        crossed = [across(value) for value in [*order.after(*found[: nz // 2]), *found[nz // 2 :]]]
        packs = [own] + packs

        parts = [2] + [2] * last
        outs = [None for _ in chunks]
        pieces_in = [(0, 0, cuts[0])]
        if last:
            pieces_in.append((1, 0, cuts[1]))
        ins = [None for _ in pieces_in]
        pres = [None for _ in chunks]

        def tokens(k, *more):
            later = [] if k == 0 else [value[k - 1] for value in hiddens]
            got = order.after(*packs, *later, *more)
            count = nx + len(later)
            blocks = Tokens(got[:nx], got[nx:count] if later else None, model, nz, cuts[k])
            return blocks, got[count:]

        def start_out(k):
            blocks, _ = tokens(k, *([*crossed[: nz // 2], found[nz // 2]] if k == 0 else []))
            *sends, keep = grad_out_chunk(blocks, core, nz, scale_out, parts[k])
            order.did(keep)
            shape = (parts[k], nz, 1, ny, cuts[k] // parts[k] // ny, model // CORES)
            outs[k] = Reduce(order, (x, y, z), sends, keep, shape)

        def start_pre(k):
            blocks, got = tokens(k, *found, *crossed)
            pres[k] = grad_pre_chunk(blocks, got[:nz], got[nz:], nz, starts[k], at_core, scale_out)
            order.did(pres[k])

        def start_in(k):
            chunk, block, width = pieces_in[k]
            got = order.after(pres[chunk], *columns)
            *sends, keep = grad_in_chunk(
                got[0], got[1:], core, scale_in, (1 if chunk else 1), block, width
            )
            order.did(keep)
            shape = (nz // CORES, nz, nx, ny, rows // ny, width)
            ins[k] = Reduce(order, (x, y, z), sends, keep, shape)

        def sums(tile):
            tiles = order.after(tile, *[along_z(tile, flip) for flip in range(1, nz)])
            tile = add_tiles(tiles)
            order.did(tile)
            return [tile] + [along_x(tile, t) for t in range(1, nx)]

        def new_weights(weight, update, tiles, at):
            got = order.after(weight, update, *tiles)
            value = step_weights(got[0], got[1], got[2:], at)
            order.did(value)
            return value

        def moments_out(tile):
            half = model // CORES
            got = order.after(
                w_out,
                m_out,
                v_out,
                tile,
                *[outs[k].held[0] for k in chunks],
                *[outs[k].held[1] for k in chunks],
            )
            new = moments_kernel(
                core,
                *got[:3],
                got[4 : 5 + last],
                got[5 + last :],
                (CORES,),
                pl.BlockSpec((shard, half), lambda n, c: (0, n)),
                [
                    pl.BlockSpec((p, ny, w // p // ny, half), lambda n, c: (0, 0, 0, 0))
                    for w, p in zip(cuts, parts)
                ],
                lambda n: n,
                0,
                [got[3]],
            )
            order.did(new[3])
            return new

        start_out(0)
        outs[0].send_y()
        start_pre(0)
        start_in(0)
        outs[0].send_z()
        ins[0].send_y()
        if last:
            start_pre(1)
            start_in(1)
            outs[0].send_z()
            start_out(1)
            ins[1].send_y()
            outs[1].send_y()
            ins[0].send_z()
            ins[1].send_z()
            ins[0].send_z()
            outs[1].send_z()
            ins[1].send_z()
            ins[0].finish()
            outs[1].send_z()
            ins[1].finish()
            ins[0].stack_x()
            ins[1].stack_x()
            outs[0].finish()
            ins[0].stack_y()
            outs[1].finish()
            outs[0].stack_y(True)
            ins[1].stack_y()
        else:
            outs[0].send_z()
            ins[0].send_z()
            outs[0].finish()
            ins[0].send_z()
            ins[0].finish()
            ins[0].stack_x()
            ins[0].stack_y()

        held = [value.held for value in ins]
        got = order.after(w_in, m_in, v_in, *[pair[0] for pair in held], *[pair[1] for pair in held])
        mine, other = got[3 : 3 + len(ins)], got[3 + len(ins) :]
        if shard % LANES:
            joined = [
                jnp.stack([jnp.where(c == 0, a, b), jnp.where(c == 0, b, a)]) for a, b in zip(mine, other)
            ]
            grad = jnp.concatenate(joined, axis=-1).transpose(1, 4, 0, 3, 2, 5)
            grad = grad.reshape(rows, hidden_width).astype(F32)
            first_in, second_in, update_in = moments(*got[:3], grad)
            tile = jnp.concatenate(
                [
                    jnp.sum((value * value).reshape(-1, 8, LANES), axis=0)
                    for value in (w_in, update_in)
                ]
            )
        else:
            zs = nz // CORES
            first_in, second_in, update_in, tile = moments_kernel(
                core,
                *got[:3],
                mine,
                other,
                (nz * nx,),
                pl.BlockSpec((rows, shard), lambda n, c: (0, n)),
                [
                    pl.BlockSpec(
                        (ny, 1, 1, rows // ny, w), lambda n, c: (0, n % nx, n // nx % zs, 0, 0)
                    )
                    for _, _, w in pieces_in
                ],
                lambda n: n // nx // zs,
                1,
                [],
            )
        order.did(tile)

        outs[last].stack_y(True)
        first_out, second_out, update_out, tile = moments_out(tile)
        tiles = sums(tile)
        new_w_in = new_weights(w_in, update_in, tiles, 16)
        new_w_out = new_weights(w_out, update_out, tiles, 0)
        return (new_w_in, first_in, second_in, new_w_out, first_out, second_out)

    return local


def solution(mesh):
    gx, gy = mesh.shape["gx"], mesh.shape["gy"]
    nz = CHIPS_Z
    state = P("gx", None)
    tokens = P(("gx", "gy"), None)
    return jax.shard_map(
        plan(nz, gx // nz, gy // CORES),
        mesh=mesh,
        in_specs=(tokens,) * 3 + (state,) * 6,
        out_specs=(state,) * 6,
        check_vma=False,
    )
```

```python
import functools
import math

import jax
import jax.numpy as jnp
from jax import lax
from jax.experimental import pallas as pl
from jax.experimental.pallas import tpu as pltpu
from jax.sharding import PartitionSpec as P

BF16 = jnp.bfloat16
F32 = jnp.float32
CORES = 2
CHIPS_Z = 4
LANES = 128
PARTS = 2
VMEM = 20 * 1024 * 1024
WIDE = 56 * 1024 * 1024
SMALL = 4 * 1024 * 1024


def moments(weight, first, second, grad):
    new_first = 0.9 * first + 0.1 * grad
    new_second = 0.95 * second + 0.05 * grad * grad
    update = new_first / (jnp.sqrt(new_second) + 1e-06) + 0.05 * weight
    return (new_first, new_second, update)


def squares(value):
    return jnp.sum(value * value)


def gelu(value):
    return 0.5 * value * (1.0 + lax.erf(value * (1.0 / math.sqrt(2.0))))


def gelu_slope(value):
    cdf = 0.5 * (1.0 + lax.erf(value * (1.0 / math.sqrt(2.0))))
    return cdf + value * (jnp.exp(-0.5 * value * value) * (1.0 / math.sqrt(2.0 * math.pi)))


def widths(shard):
    if shard % LANES:
        return (shard,)
    first = shard // LANES * 3 // 5 * LANES
    return (first, shard - first)


def dot(left, right, dims):
    return lax.dot_general(left, right, (dims, ((), ())), preferred_element_type=F32)


def params(grant=VMEM):
    return dict(
        compiler_params=pltpu.CompilerParams(vmem_limit_bytes=grant),
        cost_estimate=pl.CostEstimate(flops=1, bytes_accessed=1, transcendentals=0),
    )


def pack(hidden, cotangent, at, nz, nx, cuts):
    tokens, hidden_width = hidden.shape
    model = cotangent.shape[1]
    shard = hidden_width // (nz * nx)
    first = cuts[0]
    if shard % LANES:
        parts = [
            lax.dynamic_slice_in_dim(hidden, (z * nx + at) * shard, shard, 1).T for z in range(nz)
        ]
        return jnp.concatenate([cotangent.T, *parts])

    def body(at_ref, h_ref, cot_ref, out_ref):
        z = pl.program_id(0)

        @pl.when(z == 0)
        def _():
            out_ref[:model] = cot_ref[...].T

        out_ref[pl.ds(pl.multiple_of(model + z * first, LANES), first)] = h_ref[:, :first].T

    total = model + nz * first
    return pl.pallas_call(
        body,
        grid_spec=pltpu.PrefetchScalarGridSpec(
            num_scalar_prefetch=1,
            grid=(nz,),
            in_specs=[
                pl.BlockSpec((tokens, shard), lambda z, a: (0, z * nx + a[0])),
                pl.BlockSpec((tokens, model), lambda z, a: (0, 0)),
            ],
            out_specs=pl.BlockSpec((total, tokens), lambda z, a: (0, 0)),
        ),
        out_shape=jax.ShapeDtypeStruct((total, tokens), BF16),
        **params(WIDE),
    )(jnp.reshape(at, (1,)).astype(jnp.int32), hidden, cotangent)


def pack_later(hidden, at, nz, nx, cuts):
    tokens, hidden_width = hidden.shape
    shard = hidden_width // (nz * nx)
    if len(cuts) == 1:
        return []

    def body(at_ref, h_ref, *out_refs):
        start = cuts[0]
        for width, out_ref in zip(cuts[1:], out_refs):
            out_ref[0] = h_ref[:, start : start + width].T
            start += width

    return pl.pallas_call(
        body,
        grid_spec=pltpu.PrefetchScalarGridSpec(
            num_scalar_prefetch=1,
            grid=(nz,),
            in_specs=[pl.BlockSpec((tokens, shard), lambda z, a: (0, z * nx + a[0]))],
            out_specs=[pl.BlockSpec((1, w, tokens), lambda z, a: (z, 0, 0)) for w in cuts[1:]],
        ),
        out_shape=[jax.ShapeDtypeStruct((nz, w, tokens), BF16) for w in cuts[1:]],
        **params(WIDE),
    )(jnp.reshape(at, (1,)).astype(jnp.int32), hidden)


class Tokens:
    def __init__(self, packs, hiddens, model, nz, width):
        tokens = packs[0].shape[1]
        self.model, self.width, self.count = model, width, len(packs)
        if hiddens is None:
            self.arrays = list(packs)
            self.specs = [pl.BlockSpec(packs[0].shape, lambda z, c: (0, 0))] * len(packs)
        else:
            self.arrays = [*packs, *hiddens]
            self.specs = [pl.BlockSpec((model, tokens), lambda z, c: (0, 0))] * len(packs)
            self.specs += [pl.BlockSpec((1, width, tokens), lambda z, c: (z, 0, 0))] * len(packs)

    def cot(self, refs, n):
        return refs[n].at[: self.model]

    def hidden(self, refs, n):
        if len(refs) == self.count:
            row = self.model + pl.program_id(0) * self.width
            return refs[n][pl.ds(pl.multiple_of(row, 16), self.width)].astype(F32)
        return refs[self.count + n][0].astype(F32)


def grad_out_chunk(tokens, core, nz, scale, parts):
    width, model = tokens.width, tokens.model
    half = model // CORES
    high = width // parts
    count = len(tokens.arrays)

    def body(c_ref, *refs):
        ins, outs = refs[:count], refs[count:]
        acts = jnp.concatenate(
            [gelu(tokens.hidden(ins, n)).astype(BF16) for n in range(tokens.count)], axis=1
        )
        for which in range(2):
            cols = pl.ds(pl.multiple_of((c_ref[0] + 1 + which) % CORES * half, 16), half)
            right = jnp.concatenate([tokens.cot(ins, n)[cols, :] for n in range(tokens.count)], axis=1)
            total = (dot(acts, right, ((1,), (1,))) * scale).astype(BF16)
            for p in range(parts):
                value = total[p * high : (p + 1) * high]
                if which:
                    outs[parts][p, 0] = value
                else:
                    outs[p][0] = value

    return pl.pallas_call(
        body,
        grid_spec=pltpu.PrefetchScalarGridSpec(
            num_scalar_prefetch=1,
            grid=(nz,),
            in_specs=tokens.specs,
            out_specs=[pl.BlockSpec((1, high, half), lambda z, c: (z, 0, 0))] * parts
            + [pl.BlockSpec((parts, 1, high, half), lambda z, c: (0, z, 0, 0))],
        ),
        out_shape=[jax.ShapeDtypeStruct((nz, high, half), BF16)] * parts
        + [jax.ShapeDtypeStruct((parts, nz, high, half), BF16)],
        **params(),
    )(core, *tokens.arrays)


def grad_pre_chunk(tokens, mine, other, nz, row, core, scale):
    part, model = mine[0].shape
    width = tokens.width
    count = len(tokens.arrays)
    long = tokens.arrays[0].shape[1]

    def body(c_ref, *refs):
        ins = refs[:count]
        out_ref, w_ref = refs[count + 2 * nz :]
        for h in range(nz):

            @pl.when((pl.program_id(0) ^ c_ref[1]) == h)
            def _(h=h):
                for at, ref in ((c_ref[0], refs[count + h]), (1 - c_ref[0], refs[count + nz + h])):
                    w_ref[pl.ds(pl.multiple_of(at * part, 16), part), :] = ref[...]

        w = w_ref[row : row + width, :]
        for n in range(tokens.count):
            grad_act = dot(w, tokens.cot(ins, n)[...], ((1,), (0,))) * scale
            out_ref[0, :, n * long : (n + 1) * long] = (
                grad_act * gelu_slope(tokens.hidden(ins, n))
            ).astype(BF16)

    w_specs = [pl.BlockSpec((part, model), lambda z, c: (0, 0))] * nz
    return pl.pallas_call(
        body,
        grid_spec=pltpu.PrefetchScalarGridSpec(
            num_scalar_prefetch=1,
            grid=(nz,),
            in_specs=tokens.specs + w_specs * 2,
            out_specs=pl.BlockSpec((1, width, tokens.count * long), lambda z, c: (z, 0, 0)),
            scratch_shapes=[pltpu.VMEM((CORES * part, model), BF16)],
        ),
        out_shape=jax.ShapeDtypeStruct((nz, width, tokens.count * long), BF16),
        **params(),
    )(core, *tokens.arrays, *mine, *other)


def grad_in_chunk(grads, inputs, core, scale, cut, block, width):
    nz, _, long = grads.shape
    model, tokens = inputs[0].shape
    count = len(inputs)
    half = nz // CORES
    high = model // cut

    def body(c_ref, g_ref, *refs):
        in_refs, outs = refs[:count], refs[count:]
        left = jnp.concatenate([i[...] for i in in_refs], axis=1)
        total = (dot(left, g_ref[0], ((1,), (1,))) * scale).astype(BF16)
        step = pl.program_id(0)
        for n in range(half):

            @pl.when(step == n)
            def _(n=n):
                for h in range(cut):
                    outs[n * cut + h][...] = total[h * high : (h + 1) * high]

        @pl.when(step >= half)
        def _():
            outs[-1][0] = total

    return pl.pallas_call(
        body,
        grid_spec=pltpu.PrefetchScalarGridSpec(
            num_scalar_prefetch=1,
            grid=(nz,),
            in_specs=[
                pl.BlockSpec(
                    (1, width, long),
                    lambda z, c: ((c[0] + 1 + z // half) % CORES * half + z % half, block, 0),
                )
            ]
            + [pl.BlockSpec((model, tokens), lambda z, c: (0, 0))] * count,
            out_specs=[pl.BlockSpec((high, width), lambda z, c: (0, 0))] * (half * cut)
            + [pl.BlockSpec((1, model, width), lambda z, c: (jnp.maximum(z - half, 0), 0, 0))],
        ),
        out_shape=[jax.ShapeDtypeStruct((high, width), BF16)] * (half * cut)
        + [jax.ShapeDtypeStruct((half, model, width), BF16)],
        **params(),
    )(core, grads, *inputs)


def transposed(value):
    rows, cols = value.shape
    wide = 2 * LANES

    def body(in_ref, out_ref):
        out_ref[...] = in_ref[...].T

    return pl.pallas_call(
        body,
        grid=(cols // wide,),
        in_specs=[pl.BlockSpec((rows, wide), lambda n: (0, n))],
        out_specs=pl.BlockSpec((wide, rows), lambda n: (n, 0)),
        out_shape=jax.ShapeDtypeStruct((cols, rows), value.dtype),
        **params(),
    )(value)


def half_rows(weight, core):
    rows, cols = weight.shape
    high = rows // CORES // 2

    def body(c_ref, in_ref, out_ref):
        out_ref[...] = in_ref[...].astype(BF16)

    return pl.pallas_call(
        body,
        grid_spec=pltpu.PrefetchScalarGridSpec(
            num_scalar_prefetch=1,
            grid=(2,),
            in_specs=[pl.BlockSpec((high, cols), lambda n, c: (c[0] * 2 + n, 0))],
            out_specs=pl.BlockSpec((high, cols), lambda n, c: (n, 0)),
        ),
        out_shape=jax.ShapeDtypeStruct((2 * high, cols), BF16),
        **params(WIDE),
    )(core, weight)


def stack(pieces, places, inner=False):
    count = len(pieces)
    shape = pieces[0].shape
    out = (shape[0], count, *shape[1:]) if inner else (count, *shape)

    def body(at_ref, *refs):
        for n in range(count):
            if inner:
                for p in range(shape[0]):
                    refs[count][p, at_ref[n]] = refs[n][p]
            else:
                refs[count][at_ref[n]] = refs[n][...]

    return pl.pallas_call(
        body,
        grid_spec=pltpu.PrefetchScalarGridSpec(
            num_scalar_prefetch=1,
            grid=(),
            in_specs=[pl.BlockSpec(shape, lambda at: (0,) * len(shape))] * count,
            out_specs=pl.BlockSpec(out, lambda at: (0,) * len(out)),
        ),
        out_shape=jax.ShapeDtypeStruct(out, pieces[0].dtype),
        **params(SMALL),
    )(places, *pieces)


def add_tiles(tiles):
    def body(*refs):
        refs[-1][...] = sum(ref[...] for ref in refs[:-1])

    return pl.pallas_call(
        body, out_shape=jax.ShapeDtypeStruct(tiles[0].shape, F32), **params(SMALL)
    )(*tiles)


def reduce_step(place, keep, crosses, from_y, from_z, shift, stage, ny, split):
    lead, nz, mid, _, high, wide = keep.shape
    bit = len(from_z)

    def zed(n, at):
        if stage == "y":
            return n
        if stage == "end":
            return at[2]
        low = at[2] % (1 << bit)
        mine = (at[2] // (1 << bit)) % 2
        return n * (2 << bit) + (1 - mine) * (1 << bit) + low

    count = {"y": nz, "z": nz >> (bit + 1), "end": 1}[stage]
    six = (lead, 1, mid, 1, high, wide)
    five = (lead, 1, mid, high, wide)
    specs = [pl.BlockSpec(six, lambda n, at: (0, zed(n, at), 0, (at[1] + shift) % ny, 0, 0))]
    each = len(crosses) // lead
    long = nz // each
    for h in range(len(crosses)):
        specs.append(
            pl.BlockSpec(
                six[1:],
                lambda n, at, h=h % each: (
                    jnp.clip(zed(n, at) - h * long, 0, long - 1),
                    0,
                    (at[1] + shift) % ny,
                    0,
                    0,
                ),
            )
        )
    specs += [pl.BlockSpec(five, lambda n, at: (0, zed(n, at), 0, 0, 0))] * len(from_y)
    specs += [
        pl.BlockSpec(five, lambda n, at, j=j: (0, zed(n, at) // (2 << j), 0, 0, 0)) for j in range(bit)
    ]

    def body(at_ref, *refs):
        ins = refs[: len(specs)]
        outs = refs[len(specs) :]
        for p in range(lead):
            for m in range(mid):
                total = ins[1 + p * each][0, m, 0]
                for h in range(1, each):
                    total = jnp.where(
                        zed(pl.program_id(0), at_ref) >= h * long, ins[1 + p * each + h][0, m, 0], total
                    )
                total = total.astype(F32) + ins[0][p, 0, m, 0].astype(F32)
                for ref in ins[1 + len(crosses) :]:
                    total = total + ref[p, 0, m].astype(F32)
                total = total.astype(BF16)
                if not split:
                    outs[0][p, 0, m] = total
                    continue
                for s in range(mid):

                    @pl.when((at_ref[0] + s) % mid == m)
                    def _(s=s, total=total):
                        outs[s][p] = total

    if split:
        out_specs = [pl.BlockSpec((lead, high, wide), lambda n, at: (0, 0, 0))] * mid
        out_shape = [jax.ShapeDtypeStruct((lead, high, wide), BF16)] * mid
    else:
        out_specs = [pl.BlockSpec(five, lambda n, at: (0, n, 0, 0, 0))]
        out_shape = [jax.ShapeDtypeStruct((lead, count, mid, high, wide), BF16)]
    out = pl.pallas_call(
        body,
        grid_spec=pltpu.PrefetchScalarGridSpec(
            num_scalar_prefetch=1, grid=(count,), in_specs=specs, out_specs=out_specs
        ),
        out_shape=out_shape,
        **params(SMALL),
    )(place, keep, *crosses, *from_y, *from_z)
    return out if split else out[0]


def moments_kernel(core, weight, first, second, mine, other, grid, state_spec, grad_specs, owner, axis, tiles):
    block = state_spec.block_shape
    count = len(mine)
    long = 16 * (1 + len(tiles))

    def body(c_ref, w_ref, m_ref, v_ref, *refs):
        mine_refs, other_refs = refs[:count], refs[count : 2 * count]
        tile_refs = refs[2 * count : 2 * count + len(tiles)]
        new_m_ref, new_v_ref, u_ref, sum_ref = refs[2 * count + len(tiles) :]
        totals = [jnp.zeros((8, LANES), F32)] * 2
        start = 0
        ours = owner(pl.program_id(0)) == c_ref[0]
        for mine_ref, other_ref in zip(mine_refs, other_refs):
            size = mine_ref.size // block[1 - axis]
            shape = (size, block[1]) if axis == 0 else (block[0], size)
            at = (slice(start, start + size), slice(None))
            at = at if axis == 0 else at[::-1]
            grad = jnp.where(ours, mine_ref[...].reshape(shape), other_ref[...].reshape(shape)).astype(F32)
            weight = w_ref[at]
            new_m, new_v, update = moments(weight, m_ref[at], v_ref[at], grad)
            new_m_ref[at] = new_m
            new_v_ref[at] = new_v
            u_ref[at] = update
            for n, value in enumerate((weight, update)):
                square = value * value
                for col in range(0, shape[1], LANES):
                    totals[n] = totals[n] + square[:, col : col + LANES].reshape(-1, 8, LANES).sum(0)
            start += size

        @pl.when(pl.program_id(0) == 0)
        def _():
            sum_ref[:16] = jnp.zeros((16, LANES), F32)
            for n, tile_ref in enumerate(tile_refs):
                sum_ref[16 * (n + 1) : 16 * (n + 2)] = tile_ref[...]

        sum_ref[:8] += totals[0]
        sum_ref[8:16] += totals[1]

    state = jax.ShapeDtypeStruct(weight.shape, F32)
    return pl.pallas_call(
        body,
        grid_spec=pltpu.PrefetchScalarGridSpec(
            num_scalar_prefetch=1,
            grid=grid,
            in_specs=[state_spec] * 3
            + grad_specs * 2
            + [pl.BlockSpec((16, LANES), lambda n, c: (0, 0))] * len(tiles),
            out_specs=[state_spec] * 3 + [pl.BlockSpec((long, LANES), lambda n, c: (0, 0))],
        ),
        out_shape=[state] * 3 + [jax.ShapeDtypeStruct((long, LANES), F32)],
        **params(),
    )(core, weight, first, second, *mine, *other, *tiles)


def step_weights(weight, update, tiles, at):
    rows, cols = weight.shape
    high = rows // 5
    count = len(tiles)

    def body(w_ref, u_ref, *refs):
        sums = sum(ref[at : at + 16] for ref in refs[:count])
        ratio = jnp.sqrt(jnp.sum(sums[:8], keepdims=True)) / jnp.sqrt(jnp.sum(sums[8:], keepdims=True))
        refs[count][...] = w_ref[...] - 0.4 * ratio * u_ref[...]

    spec = pl.BlockSpec((high, cols), lambda n: (n, 0))
    tile = pl.BlockSpec(tiles[0].shape, lambda n: (0, 0))
    return pl.pallas_call(
        body,
        grid=(rows // high,),
        in_specs=[spec] * 2 + [tile] * count,
        out_specs=spec,
        out_shape=jax.ShapeDtypeStruct(weight.shape, F32),
        **params(),
    )(weight, update, *tiles)


class Order:
    def __init__(self):
        self.last = None

    def after(self, *values):
        if self.last is None:
            return values
        return lax.optimization_barrier((*values, self.last))[:-1]

    def did(self, value):
        self.last = value


def plan(nz, nx, ny):
    def along_x(value, step):
        pairs = [
            (z * nx + x, z * nx + (x + step) % nx) for z in range(nz) for x in range(nx)
        ]
        return lax.ppermute(value, "gx", pairs)

    def along_z(value, flip):
        pairs = [(z * nx + x, (z ^ flip) * nx + x) for z in range(nz) for x in range(nx)]
        return lax.ppermute(value, "gx", pairs)

    def along_y(value, step):
        pairs = [
            (y * CORES + c, (y + step) % ny * CORES + c) for y in range(ny) for c in range(CORES)
        ]
        return lax.ppermute(value, "gy", pairs)

    def across(value):
        pairs = [(k, k ^ 1) for k in range(ny * CORES)]
        return lax.ppermute(value, "gy", pairs)

    class Reduce:
        def __init__(self, order, at, sends, keep, shape):
            self.order, self.at, self.place = order, at, jnp.stack(at).astype(jnp.int32)
            self.keep = keep.reshape(shape)
            each = len(sends) // shape[0]
            self.crosses = [
                across(send).reshape(shape[1] // each, *shape[2:]) for send in sends
            ]
            self.from_y = []
            self.from_z = []

        def step(self, shift, stage, split=False):
            got = self.order.after(self.keep, *self.crosses, *self.from_y, *self.from_z)
            lead = 1 + len(self.crosses)
            count = lead + len(self.from_y)
            out = reduce_step(
                self.place, got[0], got[1:lead], got[lead:count], got[count:], shift, stage, ny, split
            )
            self.order.did(out[0] if split else out)
            return out

        def send_y(self):
            from_y = []
            for s in range(1, ny):
                from_y.append(along_y(self.step(s, "y"), s))
            self.from_y = from_y

        def send_z(self):
            bit = len(self.from_z)
            self.from_z.append(along_z(self.step(0, "z"), 1 << bit))

        def finish(self):
            out = self.step(0, "end", True)
            self.held = [out[0]] + [along_x(out[s], s) for s in range(1, len(out))]
            if len(out) == 1:
                self.share_y(out[0])

        def share_y(self, value):
            self.held = [value] + [along_y(value, s) for s in range(1, ny)]

        def stacked(self, place, size, inner=False):
            places = jnp.stack([(place - s) % size for s in range(size)]).astype(jnp.int32)
            value = stack(self.order.after(*self.held), places, inner)
            self.order.did(value)
            return value

        def stack_x(self):
            self.share_y(self.stacked(self.at[0], nx))

        def stack_y(self, inner=False):
            value = self.stacked(self.at[1], ny, inner)
            self.held = [value, across(value)]

    def local(inputs, hidden_pre, cotangent, w_in, m_in, v_in, w_out, m_out, v_out):
        model = inputs.shape[1]
        hidden_width = hidden_pre.shape[1]
        shard = hidden_width // (nz * nx)
        rows = model // (nz * nx)
        cuts = widths(shard)
        chunks = range(len(cuts))
        last = len(cuts) - 1
        starts = [sum(cuts[:k]) for k in chunks]
        scale_in = 1.0 / math.sqrt(model)
        scale_out = 1.0 / math.sqrt(hidden_width)
        place = lax.axis_index("gx")
        side = lax.axis_index("gy")
        z, x = place // nx, place % nx
        y, c = side // CORES, side % CORES
        core = jnp.reshape(c, (1,)).astype(jnp.int32)
        at_core = jnp.stack([c, z]).astype(jnp.int32)
        order = Order()

        packs, hiddens = [], []
        for t in range(1, nx):
            sent = pack(*order.after(hidden_pre, cotangent), (x + t) % nx, nz, nx, cuts)
            order.did(sent)
            packs.append(along_x(sent, t))

        part = half_rows(*order.after(w_out), core)
        order.did(part)
        flipped = transposed(*order.after(inputs))
        order.did(flipped)
        columns = [flipped] + [along_x(flipped, t) for t in range(1, nx)]
        own = pack(*order.after(hidden_pre, cotangent), x, nz, nx, cuts)
        order.did(own)
        for t in range(nx):
            value = pack_later(*order.after(hidden_pre), (x + t) % nx, nz, nx, cuts)
            if value:
                order.did(value[0])
            hiddens.append([along_x(h, t) for h in value] if t else value)
        found = {0: part, nz // 2: along_z(part, nz // 2)}
        bit = nz // 4
        while bit:
            for key in list(found):
                value = found[key]
                if key:
                    (value,) = order.after(value)
                found[key ^ bit] = along_z(value, bit)
            bit //= 2
        found = [found[key] for key in range(nz)]
        crossed = [across(value) for value in [*order.after(*found[: nz // 2]), *found[nz // 2 :]]]
        packs = [own] + packs

        parts = [2] + [2] * last
        outs = [None for _ in chunks]
        pieces_in = [(0, 0, cuts[0])]
        if last:
            pieces_in.append((1, 0, cuts[1]))
        ins = [None for _ in pieces_in]
        pres = [None for _ in chunks]

        def tokens(k, *more):
            later = [] if k == 0 else [value[k - 1] for value in hiddens]
            got = order.after(*packs, *later, *more)
            count = nx + len(later)
            blocks = Tokens(got[:nx], got[nx:count] if later else None, model, nz, cuts[k])
            return blocks, got[count:]

        def start_out(k):
            blocks, _ = tokens(k, *([*crossed[: nz // 2], found[nz // 2]] if k == 0 else []))
            *sends, keep = grad_out_chunk(blocks, core, nz, scale_out, parts[k])
            order.did(keep)
            shape = (parts[k], nz, 1, ny, cuts[k] // parts[k] // ny, model // CORES)
            outs[k] = Reduce(order, (x, y, z), sends, keep, shape)

        def start_pre(k):
            blocks, got = tokens(k, *found, *crossed)
            pres[k] = grad_pre_chunk(blocks, got[:nz], got[nz:], nz, starts[k], at_core, scale_out)
            order.did(pres[k])

        def start_in(k):
            chunk, block, width = pieces_in[k]
            got = order.after(pres[chunk], *columns)
            *sends, keep = grad_in_chunk(
                got[0], got[1:], core, scale_in, (1 if chunk else 1), block, width
            )
            order.did(keep)
            shape = (nz // CORES, nz, nx, ny, rows // ny, width)
            ins[k] = Reduce(order, (x, y, z), sends, keep, shape)

        def sums(tile):
            tiles = order.after(tile, *[along_z(tile, flip) for flip in range(1, nz)])
            tile = add_tiles(tiles)
            order.did(tile)
            return [tile] + [along_x(tile, t) for t in range(1, nx)]

        def new_weights(weight, update, tiles, at):
            got = order.after(weight, update, *tiles)
            value = step_weights(got[0], got[1], got[2:], at)
            order.did(value)
            return value

        def moments_out(tile):
            half = model // CORES
            got = order.after(
                w_out,
                m_out,
                v_out,
                tile,
                *[outs[k].held[0] for k in chunks],
                *[outs[k].held[1] for k in chunks],
            )
            new = moments_kernel(
                core,
                *got[:3],
                got[4 : 5 + last],
                got[5 + last :],
                (CORES,),
                pl.BlockSpec((shard, half), lambda n, c: (0, n)),
                [
                    pl.BlockSpec((p, ny, w // p // ny, half), lambda n, c: (0, 0, 0, 0))
                    for w, p in zip(cuts, parts)
                ],
                lambda n: n,
                0,
                [got[3]],
            )
            order.did(new[3])
            return new

        start_out(0)
        outs[0].send_y()
        start_pre(0)
        start_in(0)
        outs[0].send_z()
        ins[0].send_y()
        if last:
            start_pre(1)
            start_in(1)
            outs[0].send_z()
            start_out(1)
            ins[1].send_y()
            outs[1].send_y()
            ins[0].send_z()
            ins[1].send_z()
            outs[0].finish()
            ins[0].send_z()
            outs[1].send_z()
            ins[1].send_z()
            ins[0].finish()
            outs[1].send_z()
            ins[1].finish()
            ins[0].stack_x()
            ins[1].stack_x()
            outs[0].stack_y(True)
            ins[0].stack_y()
            outs[1].finish()
            ins[1].stack_y()
        else:
            outs[0].send_z()
            ins[0].send_z()
            outs[0].finish()
            ins[0].send_z()
            ins[0].finish()
            ins[0].stack_x()
            ins[0].stack_y()

        held = [value.held for value in ins]
        got = order.after(w_in, m_in, v_in, *[pair[0] for pair in held], *[pair[1] for pair in held])
        mine, other = got[3 : 3 + len(ins)], got[3 + len(ins) :]
        if shard % LANES:
            joined = [
                jnp.stack([jnp.where(c == 0, a, b), jnp.where(c == 0, b, a)]) for a, b in zip(mine, other)
            ]
            grad = jnp.concatenate(joined, axis=-1).transpose(1, 4, 0, 3, 2, 5)
            grad = grad.reshape(rows, hidden_width).astype(F32)
            first_in, second_in, update_in = moments(*got[:3], grad)
            tile = jnp.concatenate(
                [
                    jnp.sum((value * value).reshape(-1, 8, LANES), axis=0)
                    for value in (w_in, update_in)
                ]
            )
        else:
            zs = nz // CORES
            first_in, second_in, update_in, tile = moments_kernel(
                core,
                *got[:3],
                mine,
                other,
                (nz * nx,),
                pl.BlockSpec((rows, shard), lambda n, c: (0, n)),
                [
                    pl.BlockSpec(
                        (ny, 1, 1, rows // ny, w), lambda n, c: (0, n % nx, n // nx % zs, 0, 0)
                    )
                    for _, _, w in pieces_in
                ],
                lambda n: n // nx // zs,
                1,
                [],
            )
        order.did(tile)

        outs[last].stack_y(True)
        first_out, second_out, update_out, tile = moments_out(tile)
        tiles = sums(tile)
        new_w_in = new_weights(w_in, update_in, tiles, 16)
        new_w_out = new_weights(w_out, update_out, tiles, 0)
        return (new_w_in, first_in, second_in, new_w_out, first_out, second_out)

    return local


def solution(mesh):
    gx, gy = mesh.shape["gx"], mesh.shape["gy"]
    nz = CHIPS_Z
    state = P("gx", None)
    tokens = P(("gx", "gy"), None)
    return jax.shard_map(
        plan(nz, gx // nz, gy // CORES),
        mesh=mesh,
        in_specs=(tokens,) * 3 + (state,) * 6,
        out_specs=(state,) * 6,
        check_vma=False,
    )
```
